512 devices in a mesh: wide: 32 (over z_hi, x, core), mid: 4 (over y), narrow: 4 (over z_lo).
Axes of the slice: x: 4, y: 4, z: 16 (z_hi: 4, z_lo: 4; z = z_hi * 4 + z_lo), core: 2. Of those that a mesh axis runs over, the one named last changes fastest.
Arguments:
- mold_temp: float32 [512, 64, 512], P('wide', 'mid', 'narrow'), may hold values from -1 to 0.5
- capacity: float32 [512, 64, 512], P('wide', 'mid', 'narrow'), may hold values from 0.25 to 4
- melt_temp: float32 [64, 65536], P(None, ('wide', 'mid', 'narrow')), may hold values from 0.5 to 2.5
- log_pressure: float32 [64, 65536], P(None, ('wide', 'mid', 'narrow')), may hold values from 0 to 1.5
- target_volume: float32 [64, 65536], P(None, ('wide', 'mid', 'narrow')), may hold values from 0.7 to 1.4
- inflow: float32 [64, 65536], P(None, ('wide', 'mid', 'narrow')), may hold values from -3 to 3
- self_blocks: bfloat16 [64, 64, 65536], P(None, None, ('wide', 'mid', 'narrow'))
- link_blocks: bfloat16 [2, 64, 64, 65536], P(None, None, None, ('wide', 'mid', 'narrow')), may hold values from -0.119628906 to 0.119628906
- link_columns: int32 [2, 65536], P(None, ('wide', 'mid', 'narrow')), may hold values from 0 to 127
- wall_owner: int32 [65536], P(('wide', 'mid', 'narrow')), may hold values from 0 to 31, as said below
- wall_slot: int32 [65536], P(('wide', 'mid', 'narrow')), may hold values from 0 to 31
- transfer_coef: float32 [64, 65536], P(None, ('wide', 'mid', 'narrow')), may hold values from 0.2 to 1
Outputs:
- mold_out: float32 [512, 64, 512], P('wide', 'mid', 'narrow')
- pressure: float32 [64, 65536], P(None, ('wide', 'mid', 'narrow'))
- shrinkage: float32 [64, 65536], P(None, ('wide', 'mid', 'narrow'))
The draws below stay inside these ranges and needn't reach their ends.
Inputs may be any that keep to these rules, and one draw needn't show every extreme that they name: `wall_owner`: in each device's 128 blocks no owner is named more than 16 times and one owner exactly 16 times; that owner is the same on all devices with the same mid and narrow indices. `link_columns`: indices among the 128 blocks of the same device.
All inputs are finite; a program needn't handle non-finite values.
Results may differ from the reference program's by a relative error of at most 0.01.
Values sent between devices are 32-bit elements; how exact they have to be, the bound alone decides.
A program may use at most 64 MiB of HBM per device.

```python
import math
import jax
import jax.numpy as jnp
from jax import lax

CX = 16
CY = 16
CZ = 128
BLOCK = 64
NBD = 128
NOFF = 2
ITERS = 2
SWEEPS = 4
INNER = 2
GROUPS = 32
NX = 512
NY = 64
NZ = 512
FACES = 32
NBLK = 65536
CAP = 16
N_MID = 4
N_NARROW = 4


def draw_self_blocks(key, part):
    key = jax.random.fold_in(key, 1)
    first, second = jax.random.split(key, 2)
    spread = 0.15
    low = 3.0
    high = 5.0
    linked = jax.random.uniform(first, (BLOCK, BLOCK, NBLK), jnp.float32, -spread, spread)
    center = jax.random.uniform(second, (BLOCK, 1, NBLK), jnp.float32, low, high)
    places = jnp.arange(BLOCK, dtype=jnp.int32)
    identity = (places[:, None] == places[None, :]).astype(jnp.float32)[:, :, None]
    return (linked * (1.0 - identity) + center * identity).astype(jnp.bfloat16)


def draw_wall_owner(key, part):
    key = jax.random.fold_in(key, 2)
    first, second, third = jax.random.split(key, 3)
    devices_all = NBLK // NBD
    sharing = devices_all // GROUPS
    slot_count = GROUPS * CAP
    favourite = jax.random.randint(first, (sharing,), 0, GROUPS)
    target = jnp.tile(favourite, GROUPS)
    slot_index = jnp.arange(slot_count, dtype=jnp.int32)
    scores = jax.random.randint(second, (devices_all, slot_count), 0, 1 << 20) * slot_count + slot_index[None, :]
    forced = slot_index[None, :] // CAP == target[:, None]
    scores = jnp.where(forced, slot_index[None, :] - slot_count, scores)
    chosen = jnp.argsort(scores, axis=1, stable=True)[:, :NBD] // CAP
    shuffle = jax.random.randint(third, (devices_all, NBD), 0, 1 << 20) * NBD + jnp.arange(NBD, dtype=jnp.int32)[None, :]
    order = jnp.argsort(shuffle, axis=1, stable=True)
    return jnp.take_along_axis(chosen, order, axis=1).reshape(NBLK).astype(jnp.int32)


def set_ends(array, key, low, largest):
    shape = array.shape
    spot = [jax.random.randint(jax.random.fold_in(key, axis), (), 0, shape[axis]) for axis in range(len(shape))]
    array = array.at[tuple(spot)].set(low)
    longest = shape.index(max(shape))
    spot[longest] = (spot[longest] + 1) % shape[longest]
    return array.at[tuple(spot)].set(largest)


def block_scale(stream_key, dims, cuts, low, largest):
    level = 1.0
    for axis_at, parts in cuts:
        steps = jax.random.uniform(jax.random.fold_in(jax.random.fold_in(stream_key, 6), axis_at), (parts,), jnp.float32, low / len(cuts), largest / len(cuts))
        level = level * jnp.repeat(jnp.exp(steps), dims[axis_at] // parts).reshape((-1,) + (1,) * (len(dims) - 1 - axis_at))
    return level


def gaussian(stream_key, dims, scale, bound, cuts=(), held_as=jnp.bfloat16):
    loudness = block_scale(stream_key, dims, cuts, -0.22, 0.18) if cuts else 1.0
    values = jax.random.normal(stream_key, dims, jnp.float32) * scale * loudness
    return jnp.minimum(jnp.maximum(values, -bound), bound).astype(held_as)


def setup_inputs(seed: int = 0) -> dict:
    splits = jax.random.split(jax.random.key(seed), 13)
    return {
        "mold_temp": jnp.clip(-1.0 + 1.5 * jax.random.uniform(splits[0], (NX, NY, NZ), jnp.float32) ** block_scale(splits[0], (NX, NY, NZ), ((0, 32), (1, 4), (2, 4)), -0.2, 0.2), -1.0, 0.5),
        "capacity": jnp.clip(jnp.exp(math.log(4.0) - 2.7725887 * jax.random.uniform(splits[1], (NX, NY, NZ), jnp.float32) ** block_scale(splits[1], (NX, NY, NZ), ((0, 32), (1, 4), (2, 4)), -0.2, 0.2)), 0.25, 4.0),
        "melt_temp": jnp.clip(0.5 + 2.0 * jax.random.uniform(splits[2], (BLOCK, NBLK), jnp.float32) ** block_scale(splits[2], (BLOCK, NBLK), ((1, 512),), -0.2, 0.2), 0.5, 2.5),
        "log_pressure": jnp.clip(1.5 * jax.random.uniform(splits[3], (BLOCK, NBLK), jnp.float32) ** block_scale(splits[3], (BLOCK, NBLK), ((1, 512),), -0.2, 0.2), 0.0, 1.5),
        "target_volume": jnp.clip(0.7 + 0.7 * jax.random.uniform(splits[4], (BLOCK, NBLK), jnp.float32) ** block_scale(splits[4], (BLOCK, NBLK), ((1, 512),), -0.2, 0.2), 0.7, 1.4),
        "inflow": gaussian(splits[5], (BLOCK, NBLK), 0.5, 3.0, ((1, 512),), jnp.float32),
        "self_blocks": draw_self_blocks(jax.random.fold_in(splits[12], 71), 0),
        "link_blocks": jnp.clip(jax.random.uniform(splits[7], (NOFF, BLOCK, BLOCK, NBLK), jnp.float32, -0.119628906, 0.119628906) * block_scale(splits[7], (NOFF, BLOCK, BLOCK, NBLK), ((3, 512),), -0.4, 0.0), -0.119628906, 0.119628906).astype(jnp.bfloat16),
        "link_columns": set_ends(jax.random.randint(splits[8], (NOFF, NBLK), 0, NBD), jax.random.fold_in(splits[8], 1), 0, NBD - 1).astype(jnp.int32),
        "wall_owner": draw_wall_owner(jax.random.fold_in(splits[12], 71), 0),
        "wall_slot": set_ends(jax.random.randint(splits[10], (NBLK,), 0, FACES), jax.random.fold_in(splits[10], 1), 0, FACES - 1).astype(jnp.int32),
        "transfer_coef": jnp.clip(jnp.exp(math.log(1.0) - 1.609438 * jax.random.uniform(splits[11], (BLOCK, NBLK), jnp.float32) ** block_scale(splits[11], (BLOCK, NBLK), ((1, 512),), -0.2, 0.2)), 0.2, 1.0),
    }


CONDUCT = 1.0
COOLING = 0.5
TAIT_C = 0.3
EXPAND = 0.25
BULK_BASE = 0.5
BULK_SLOPE = 0.3


def neighbours(field):
    padded = jnp.pad(field, 1)
    beside = padded[2:, 1:-1, 1:-1] + padded[:-2, 1:-1, 1:-1]
    beside = beside + padded[1:-1, 2:, 1:-1] + padded[1:-1, :-2, 1:-1]
    beside = beside + padded[1:-1, 1:-1, 2:] + padded[1:-1, 1:-1, :-2]
    return beside


def sweeps(field, start_field, capacity, source):
    for sweep_index in range(SWEEPS):
        field = (capacity * start_field + source + CONDUCT * neighbours(field)) / (capacity + 6.0 * CONDUCT)
    return field


def to_faces(field):
    layer = field[::CX]
    layer = layer.reshape(GROUPS, N_MID, CY, N_NARROW, CZ).transpose(0, 1, 3, 2, 4)
    return layer.reshape(GROUPS, N_MID, N_NARROW, FACES, BLOCK)


def from_faces(face_values):
    layer = face_values.reshape(GROUPS, N_MID, N_NARROW, CY, CZ).transpose(0, 1, 3, 2, 4)
    layer = layer.reshape(GROUPS, NY, NZ)
    return jnp.zeros((NX, NY, NZ), jnp.float32).at[::CX].set(layer)


def block_product(self_blocks, link_blocks, link_columns, values):
    devices_all = NBLK // NBD

    def one_device(device):
        start = (device * NBD).astype(jnp.int32)
        own = lax.dynamic_slice_in_dim(self_blocks, start, NBD, 2).astype(jnp.float32)
        links = lax.dynamic_slice_in_dim(link_blocks, start, NBD, 3).astype(jnp.float32)
        columns = lax.dynamic_slice_in_dim(link_columns, start, NBD, 1)
        local = lax.dynamic_slice_in_dim(values, start, NBD, 1).astype(jnp.float32)
        nearby = local[:, columns]
        first = jnp.einsum("ijb,jb->ib", own, local, precision=lax.Precision.HIGHEST)
        second = jnp.einsum("nijb,jnb->ib", links, nearby, precision=lax.Precision.HIGHEST)
        return first + second

    result = lax.map(one_device, jnp.arange(devices_all, dtype=jnp.int32))
    return jnp.transpose(result, (1, 0, 2)).reshape(BLOCK, NBLK)


def newton(state, melt, target_volume, inflow, self_blocks, link_blocks, link_columns, self_diag):
    bulk_modulus = BULK_BASE * jnp.exp(-BULK_SLOPE * melt)
    growth = jnp.exp(state)
    pressure = bulk_modulus * (growth - 1.0)
    base_volume = jnp.exp(EXPAND * melt)
    volume = base_volume * (1.0 - TAIT_C * state)
    rounded = pressure.astype(jnp.bfloat16)
    residual = block_product(self_blocks, link_blocks, link_columns, rounded) + (target_volume - volume) - inflow
    press_slope = bulk_modulus * growth
    diagonal = self_diag * press_slope + TAIT_C * base_volume
    update = -residual / diagonal
    for repeat in range(INNER):
        weighted = (press_slope * update).astype(jnp.bfloat16)
        linked = block_product(self_blocks, link_blocks, link_columns, weighted) - self_diag * weighted.astype(jnp.float32)
        update = (-residual - linked) / diagonal
    return state + update


def reference(mold_temp, capacity, melt_temp, log_pressure, target_volume, inflow, self_blocks, link_blocks, link_columns, wall_owner, wall_slot, transfer_coef):
    block_device = jnp.arange(NBLK, dtype=jnp.int32) // NBD
    mid_index = (block_device // N_NARROW) % N_MID
    narrow_index = block_device % N_NARROW
    self_diag = jnp.diagonal(self_blocks, axis1=0, axis2=1).T.astype(jnp.float32)
    field = mold_temp
    melt = melt_temp
    state = log_pressure
    for iteration in range(ITERS):
        wall = to_faces(field)[wall_owner, mid_index, narrow_index, wall_slot].T
        flux = transfer_coef * (melt - wall)
        melt = melt - COOLING * flux
        empty = jnp.zeros((GROUPS, N_MID, N_NARROW, FACES, BLOCK), jnp.float32)
        face_source = empty.at[wall_owner, mid_index, narrow_index, wall_slot].add(flux.T)
        field = sweeps(field, mold_temp, capacity, from_faces(face_source))
        state = newton(state, melt, target_volume, inflow, self_blocks, link_blocks, link_columns, self_diag)
    pressure = BULK_BASE * jnp.exp(-BULK_SLOPE * melt) * (jnp.exp(state) - 1.0)
    shrinkage = 1.0 - jnp.exp(EXPAND * melt) * (1.0 - TAIT_C * state)
    return field, pressure, shrinkage
```

```python
import functools

import jax
import jax.numpy as jnp
from jax import lax
from jax.experimental import pallas as pl
from jax.experimental.pallas import tpu as pltpu
from jax.sharding import PartitionSpec as P

BLOCK = 64
ITERS = 2
SWEEPS = 4
INNER = 2
WIDTH = 4
FAR_FIRST = (2, 1, 3)

CONDUCT = 1.0
COOLING = 0.5
TAIT_C = 0.3
EXPAND = 0.25
BULK_BASE = 0.5
BULK_SLOPE = 0.3

MESH = pl.DeviceIdType.MESH
F32 = jnp.float32
BF16 = jnp.bfloat16


def flip(v, k):
    if k == 0:
        return v
    if k == 1:
        return v + 1 - 2 * (v % 2)
    if k == 2:
        return (v + 2) % 4
    return 3 - v


def split_terms(x):
    hi = x.astype(BF16)
    lo = (x - hi.astype(F32)).astype(BF16)
    return hi, lo


def kernel(
    mold, cap, melt_in, logp, target_in, inflow_in, coef_in, columns_in, owner_in, slot_in, self_in, link_in,
    out_field, out_press, out_shrink,
    selfb, linkb, tab, spread, rs1, psum, rs2, near, rows_in, pack, pack_in, ext, inv, base, plain,
    srcb, src_in, lower, lower_in,
    hot, hot_t, col_hot, diag, kv, resid, jdiag, slope, upd, state, melt, target, inflow, coef,
    columns, owner, slot,
    load_sem, zsend_sem, zrecv_sem, gsend_sem, grecv_sem, csend_sem, crecv_sem, ysend_sem, yrecv_sem,
    xsend_sem, xrecv_sem, lsend_sem, lrecv_sem, wsend_sem, wrecv_sem, msend_sem, mrecv_sem, nsend_sem, nrecv_sem,
):
    cx, cy, cz = mold.shape
    planes, width = near.shape[1], WIDTH
    w = lax.axis_index("wide")
    m = lax.axis_index("mid")
    n = lax.axis_index("narrow")
    n_w, n_m, n_n = lax.axis_size("wide"), lax.axis_size("mid"), lax.axis_size("narrow")
    zh, x, c = w // 8, (w // 2) % 4, w % 2

    def z_peer(k):
        return (flip(zh, k) * 8 + x * 2 + c, m, n)

    def xc_peer(j):
        return (zh * 8 + flip(x, j // 2) * 2 + flip(c, j % 2), m, n)

    def beside(dw, dm, dn):
        return ((w + n_w + dw) % n_w, (m + n_m + dm) % n_m, (n + n_n + dn) % n_n)

    barrier = pltpu.get_barrier_semaphore()
    peers = [z_peer(k) for k in range(1, 4)] + [xc_peer(j) for j in range(1, 8)]
    peers += [beside(-1, 0, 0), beside(1, 0, 0)]
    peers += [beside(0, dm, dn) for dm in (-1, 0, 1) for dn in (-1, 0, 1) if (dm, dn) != (0, 0)]
    for peer in peers:
        pl.semaphore_signal(barrier, inc=1, device_id=peer, device_id_type=MESH)

    loads = [
        pltpu.make_async_copy(src, dst, load_sem.at[i])
        for i, (src, dst) in enumerate((
            (mold, near.at[0, pl.ds(width, cx)]), (cap, near.at[2, pl.ds(width, cx)]),
            (owner_in, owner), (slot_in, slot), (melt_in, melt), (coef_in, coef), (columns_in, columns),
            (self_in, selfb), (link_in, linkb), (logp, state), (target_in, target), (inflow_in, inflow),
        ))
    ]
    for load in loads:
        load.start()

    def remote(src, dst, sems, peer):
        return pltpu.make_async_remote_copy(
            src_ref=src, dst_ref=dst, send_sem=sems[0], recv_sem=sems[1],
            device_id=peer, device_id_type=MESH,
        )

    def w_sems(a, q):
        return (wsend_sem.at[a, q], wrecv_sem.at[a, q])

    def send_low(a):
        remote(
            near.at[a, pl.ds(width, width)], near.at[a, pl.ds(width + cx, width)], w_sems(a, 0), beside(-1, 0, 0)
        ).start()

    def send_high(a):
        remote(near.at[a, pl.ds(cx, width)], near.at[a, pl.ds(0, width)], w_sems(a, 1), beside(1, 0, 0)).start()

    def wide_to_mid(a):
        got = near.at[a, pl.ds(width + cx, width)]
        remote(got, got, w_sems(a, 0), beside(-1, 0, 0)).wait_recv()
        got = near.at[a, pl.ds(0, width)]
        remote(got, got, w_sems(a, 1), beside(1, 0, 0)).wait_recv()
        sems = (msend_sem.at[a], mrecv_sem.at[a])
        remote(near.at[a, :, pl.ds(0, 8)], rows_in.at[a, 0], sems, beside(0, -1, 0)).start()
        remote(near.at[a, :, pl.ds(8, 8)], rows_in.at[a, 1], sems, beside(0, 1, 0)).start()

    lane = lax.broadcasted_iota(jnp.int32, (24, cz), 1)
    row8 = lax.broadcasted_iota(jnp.int32, (8, cz), 0)
    lane8 = lax.broadcasted_iota(jnp.int32, (8, cz), 1)

    def mid_to_narrow(a, dst):
        got = rows_in.at[a]
        remote(got, got, (msend_sem.at[a], mrecv_sem.at[a]), beside(0, 1, 0)).wait_recv()
        packed = [jnp.zeros((24, cz), F32), jnp.zeros((24, cz), F32)]
        for p in range(planes):
            ghost = jnp.where(row8 < width, rows_in[a, 0, p], rows_in[a, 1, p])
            whole = jnp.concatenate([near[a, p], ghost], axis=0)
            dst[p, :, 0:cz] = whole
            g, q = p // 16, p % 16
            packed[g] = jnp.where(lane // 8 == q, pltpu.roll(whole, width + 8 * q, 1), packed[g])
        for g in range(2):
            pack[a, g] = packed[g]
        sems = (nsend_sem.at[a], nrecv_sem.at[a])
        remote(pack.at[a], pack_in.at[a, 0], sems, beside(0, 0, -1)).start()
        remote(pack.at[a], pack_in.at[a, 1], sems, beside(0, 0, 1)).start()

    def narrow_done(a, dst):
        got = pack_in.at[a]
        remote(got, got, (nsend_sem.at[a], nrecv_sem.at[a]), beside(0, 0, 1)).wait_recv()
        for g in range(2):
            comb = jnp.where(lane % 8 >= width, pack_in[a, 0, g], pack_in[a, 1, g])
            for p in range(16 * g, min(planes, 16 * g + 16)):
                dst[p, :, cz:2 * cz] = pltpu.roll(comb, cz - (8 * (p % 16) + width), 1)

    row_at = lax.broadcasted_iota(jnp.int32, (24, 2 * cz), 0)
    row_at = jnp.where(row_at < cy + width, row_at, row_at - 24) + m * cy
    lane_at = lax.broadcasted_iota(jnp.int32, (24, 2 * cz), 1)
    lane_real = (lane_at < cz + width) | (lane_at >= 2 * cz - width)
    lane_at = jnp.where(lane_at < cz + width, lane_at, lane_at - 2 * cz) + n * cz
    inside = lane_real & (row_at >= 0) & (row_at < n_m * cy) & (lane_at >= 0) & (lane_at < n_n * cz)
    inside = jnp.where(inside, 1.0, 0.0)

    def prepare():
        for p in range(planes):
            here = inside
            if p < width:
                here = jnp.where(w > 0, inside, 0.0)
            elif p >= width + cx:
                here = jnp.where(w < n_w - 1, inside, 0.0)
            capacity, start = inv[p], ext[0, p]
            base[p] = capacity * start
            inv[p] = here / (capacity + 6.0 * CONDUCT)
            ext[0, p] = jnp.where(here > 0.0, start, 0.0)

    def around(plane):
        rows = pltpu.roll(plane, 1, 0) + pltpu.roll(plane, 23, 0)
        return rows + (pltpu.roll(plane, 1, 1) + pltpu.roll(plane, 2 * cz - 1, 1))

    def plain_sweeps():
        for k in range(SWEEPS):
            now, later = k % 2, (k + 1) % 2
            edge = k + 1
            for p in range(edge, planes - edge):
                total = (ext[now, p - 1] + ext[now, p + 1]) + around(ext[now, p]) + base[p]
                new = total * inv[p]
                if k == SWEEPS - 1:
                    plain[p - width] = new[:cy, :cz]
                else:
                    ext[later, p] = new

    def apply(v16):
        v = v16.astype(F32)
        linked = jnp.dot(v16, col_hot[...], preferred_element_type=F32)
        near0, near1 = linked[:, :128], linked[:, 128:]

        def rows(t, carry):
            sums = []
            for u in range(8):
                i = t * 8 + u
                prod = selfb[i].astype(F32) * v + linkb[0, i].astype(F32) * near0 + linkb[1, i].astype(F32) * near1
                sums.append(jnp.sum(prod, axis=0, keepdims=True))
            kv[pl.ds(pl.multiple_of(t * 8, 8), 8), :] = jnp.concatenate(sums, axis=0)
            return carry

        lax.fori_loop(0, BLOCK // 8, rows, 0)
        return kv[...]

    def newton_start():
        mt, st = melt[...], state[...]
        bulk = BULK_BASE * jnp.exp(-BULK_SLOPE * mt)
        growth = jnp.exp(st)
        press = bulk * (growth - 1.0)
        base_volume = jnp.exp(EXPAND * mt)
        volume = base_volume * (1.0 - TAIT_C * st)
        sl = bulk * growth
        slope[...] = sl
        jd = diag[...] * sl + TAIT_C * base_volume
        jdiag[...] = jd
        res = apply(press.astype(BF16)) + (target[...] - volume) - inflow[...]
        resid[...] = res
        upd[...] = -res / jd

    def newton_step():
        weighted = (slope[...] * upd[...]).astype(BF16)
        linked = apply(weighted) - diag[...] * weighted.astype(F32)
        upd[...] = (-resid[...] - linked) / jdiag[...]

    def gather_start(it):
        for k in FAR_FIRST:
            remote(tab.at[it, 0, 0], tab.at[it, k, 0], z_sems(it, k), z_peer(k)).start()
        gather_on(it, 0)

    def z_sems(it, k):
        return (zsend_sem.at[it, k], zrecv_sem.at[it, k])

    def gather_sems(it, k):
        return (gsend_sem.at[it, k], grecv_sem.at[it, k])

    def scatter_sems(it, k):
        return (csend_sem.at[it, k], crecv_sem.at[it, k])

    def sum_sems(it, k):
        return (ysend_sem.at[it, k], yrecv_sem.at[it, k])

    def gather_on(it, k):
        for j in range(1, 8):
            remote(tab.at[it, k, 0], tab.at[it, k, j], gather_sems(it, k), xc_peer(j)).start()

    def z_arrived(it, k):
        got = tab.at[it, k, 0]
        remote(got, got, z_sems(it, k), z_peer(k)).wait_recv()
        gather_on(it, k)

    for it in range(ITERS):
        src_in[it] = jnp.zeros((10, 8, cz), F32)
    loads[0].wait()
    tab[0, 0, 0] = near[0, width]
    pl.semaphore_wait(barrier, len(peers))
    gather_start(0)
    send_low(0)
    send_high(0)
    loads[1].wait()
    send_low(2)
    send_high(2)

    for it in range(ITERS):
        if it == 0:
            loads[2].wait()
            loads[3].wait()
            rel = jnp.bitwise_xor(owner[...], w)
            place = rel * 16 + slot[...] // 2
            half = slot[...] % 2
            faces = lax.broadcasted_iota(jnp.int32, (512, 128), 0)
            hot32 = jnp.where(faces == place, 1.0, 0.0)
            hot[...] = hot32.astype(BF16)
            hot_t[...] = hot32.T.astype(BF16)
        z_arrived(it, 1)
        z_arrived(it, 3)
        z_arrived(it, 2)
        if it == 0:
            for load in loads[4:]:
                load.wait()
            froms = lax.broadcasted_iota(jnp.int32, (128, 128), 0)
            for k in range(2):
                col_hot[:, k * 128:(k + 1) * 128] = jnp.where(froms == columns[k:k + 1, :], 1.0, 0.0).astype(BF16)
            wide_to_mid(0)
            wide_to_mid(2)

            def pick(t, carry):
                sums = []
                for u in range(8):
                    i = t * 8 + u
                    mask = lax.broadcasted_iota(jnp.int32, (BLOCK, 128), 0) == i
                    sums.append(jnp.sum(jnp.where(mask, selfb[i].astype(F32), 0.0), axis=0, keepdims=True))
                diag[pl.ds(pl.multiple_of(t * 8, 8), 8), :] = jnp.concatenate(sums, axis=0)
                return carry

            lax.fori_loop(0, BLOCK // 8, pick, 0)
        else:
            got = lower_in.at[it - 1]
            remote(got, got, (lsend_sem.at[it - 1], lrecv_sem.at[it - 1]), beside(1, 0, 0)).wait_recv()
            for p in range(3):
                near[1, width + cx - 3 + p] = plain[cx - 3 + p] + lower_in[it - 1, p]
            send_high(1)
            for p in range(width, cx - width):
                near[1, width + p] = plain[p]
        found = jnp.zeros((128, 256), F32)
        for k in (0, 1, 3, 2):
            got = tab.at[it, k, pl.ds(1, 7)]
            remote(got, got, gather_sems(it, k), xc_peer(1)).wait_recv()
            hi, lo = split_terms(tab[it, k].reshape(128, 128))
            found = found + jnp.dot(
                hot_t[:, k * 128:(k + 1) * 128], jnp.concatenate([hi, lo], axis=1), preferred_element_type=F32
            )
        found = (found[:, :128] + found[:, 128:]).T
        wall = jnp.where(half == 1, found[BLOCK:], found[:BLOCK])
        flux = coef[...] * (melt[...] - wall)
        melt[...] = melt[...] - COOLING * flux
        placed = jnp.concatenate([jnp.where(half == 0, flux, 0.0), jnp.where(half == 1, flux, 0.0)], axis=0)
        hi, lo = split_terms(placed)
        terms = jnp.concatenate([hi, lo], axis=0)
        for k in FAR_FIRST + (0,):
            summed = lax.dot_general(
                hot[k * 128:(k + 1) * 128, :], terms, (((1,), (1,)), ((), ())), preferred_element_type=F32
            )
            spread[it, k] = (summed[:, :128] + summed[:, 128:]).reshape(8, 16, 128)
            for j in range(1, 8):
                remote(spread.at[it, k, j], rs1.at[it, k, j], scatter_sems(it, k), xc_peer(j)).start()
        if it > 0:
            wide_to_mid(1)
        newton_start()
        for k in FAR_FIRST + (0,):
            got = rs1.at[it, k, pl.ds(1, 7)]
            remote(got, got, scatter_sems(it, k), xc_peer(1)).wait_recv()
            total = spread[it, k, 0]
            for j in range(1, 8):
                total = total + rs1[it, k, j]
            psum[it, k] = total
            if k > 0:
                remote(psum.at[it, k], rs2.at[it, k], sum_sems(it, k), z_peer(k)).start()
        if it == 0:
            mid_to_narrow(0, ext.at[0])
            mid_to_narrow(2, inv)
            newton_step()
            narrow_done(0, ext.at[0])
            narrow_done(2, inv)
            prepare()
        else:
            mid_to_narrow(1, ext.at[0])
            newton_step()
            narrow_done(1, ext.at[0])
            for p in range(planes):
                ext[0, p] = jnp.where(inv[p] > 0.0, ext[0, p], 0.0)
        plain_sweeps()
        source = psum[it, 0]
        for k in (1, 3, 2):
            got = rs2.at[it, k]
            remote(got, got, sum_sems(it, k), z_peer(k)).wait_recv()
            source = source + rs2[it, k]
        srcb[it, 0] = source[:8]
        srcb[it, 1] = source[8:]
        def send_edges(side, parts):
            for src, place_at, count, dm, dn in parts:
                remote(
                    srcb.at[it, pl.ds(src, count)], src_in.at[it, pl.ds(place_at, count)],
                    (xsend_sem.at[it, side], xrecv_sem.at[it, side]), beside(0, dm, dn),
                ).start()

        send_edges(0, ((0, 0, 1, -1, 0), (1, 1, 1, 1, 0)))

        @pl.when(n > 0)
        def _():
            send_edges(1, ((0, 2, 2, 0, -1), (0, 4, 1, -1, -1), (1, 5, 1, 1, -1)))

        @pl.when(n < n_n - 1)
        def _():
            send_edges(2, ((0, 6, 2, 0, 1), (0, 8, 1, -1, 1), (1, 9, 1, 1, 1)))

        newton_step()
        state[...] = state[...] + upd[...]
        if it == ITERS - 1:
            mt, st = melt[...], state[...]
            out_press[...] = BULK_BASE * jnp.exp(-BULK_SLOPE * mt) * (jnp.exp(st) - 1.0)
            out_shrink[...] = 1.0 - jnp.exp(EXPAND * mt) * (1.0 - TAIT_C * st)
        def edges(side, first, count):
            got = src_in.at[it, pl.ds(first, count)]
            return remote(got, got, (xsend_sem.at[it, side], xrecv_sem.at[it, side]), beside(0, 1, 0))

        edges(0, 0, 2).wait_recv()

        @pl.when(n < n_n - 1)
        def _():
            edges(1, 2, 4).wait_recv()

        @pl.when(n > 0)
        def _():
            edges(2, 6, 4).wait_recv()

        def corner(up, down):
            return jnp.where(row8 < width, src_in[it, up], src_in[it, down])

        def lanes(after, before):
            return jnp.where(lane8 < width, after, before)

        main = jnp.concatenate([source, corner(0, 1)], axis=0)
        sides = jnp.concatenate(
            [lanes(src_in[it, 2], src_in[it, 6]), lanes(src_in[it, 3], src_in[it, 7]), lanes(corner(4, 5), corner(8, 9))],
            axis=0,
        )
        wide_source = jnp.concatenate([main, sides], axis=1)
        nothing = jnp.zeros((24, 2 * cz), F32)
        level = [{0: wide_source * inv[width]}]

        def grown(k, p):
            have = level[k - 1]
            total = nothing
            if p == 0:
                total = wide_source
            for q in (p - 1, p + 1):
                if q in have:
                    total = total + have[q]
            if p in have:
                total = total + around(have[p])
            return total * inv[width + p]

        level.append({p: grown(1, p) for p in (0, -1, 1)})
        level.append({p: grown(2, p) for p in (0, -1, 1)})
        wall_plane = plain[0] + grown(3, 0)[:cy, :cz]
        if it < ITERS - 1:
            tab[it + 1, 0, 0] = wall_plane
            gather_start(it + 1)
        level[2].update({p: grown(2, p) for p in (-2, 2)})
        for p in (-3, -2, -1):
            lower[it, p + 3] = grown(3, p)[:cy, :cz]
        remote(lower.at[it], lower_in.at[it], (lsend_sem.at[it], lrecv_sem.at[it]), beside(-1, 0, 0)).start()
        first = [wall_plane] + [plain[p] + grown(3, p)[:cy, :cz] for p in (1, 2, 3)]
        if it < ITERS - 1:
            for p in range(4):
                near[1, width + p] = first[p]
            send_low(1)
            near[1, cx] = plain[cx - 4]
        else:
            for p in range(4):
                out_field[p] = first[p]
            for p in range(4, cx - 3):
                out_field[p] = plain[p]
            got = lower_in.at[it]
            remote(got, got, (lsend_sem.at[it], lrecv_sem.at[it]), beside(1, 0, 0)).wait_recv()
            for p in range(3):
                out_field[cx - 3 + p] = plain[cx - 3 + p] + lower_in[it, p]

    for it in range(ITERS):
        for k in range(4):
            if k > 0:
                remote(tab.at[it, k, 0], tab.at[it, k, 0], z_sems(it, k), z_peer(k)).wait_send()
                remote(psum.at[it, k], psum.at[it, k], sum_sems(it, k), z_peer(k)).wait_send()
            region = tab.at[it, k, pl.ds(1, 7)]
            remote(region, region, gather_sems(it, k), z_peer(1)).wait_send()
            region = spread.at[it, k, pl.ds(1, 7)]
            remote(region, region, scatter_sems(it, k), z_peer(1)).wait_send()
        for side, first, count, sent in ((0, 0, 2, None), (1, 2, 4, n > 0), (2, 6, 4, n < n_n - 1)):
            region = src_in.at[it, pl.ds(first, count)]
            edge = remote(region, region, (xsend_sem.at[it, side], xrecv_sem.at[it, side]), z_peer(1))
            if sent is None:
                edge.wait_send()
            else:
                pl.when(sent)(edge.wait_send)
        remote(lower.at[it], lower.at[it], (lsend_sem.at[it], lrecv_sem.at[it]), z_peer(1)).wait_send()
    for a in range(3):
        for q in range(2):
            region = near.at[a, pl.ds(0, width)]
            remote(region, region, w_sems(a, q), z_peer(1)).wait_send()
        region = rows_in.at[a]
        remote(region, region, (msend_sem.at[a], mrecv_sem.at[a]), z_peer(1)).wait_send()
        region = pack_in.at[a]
        remote(region, region, (nsend_sem.at[a], nrecv_sem.at[a]), z_peer(1)).wait_send()


def per_device(
    mold_temp, capacity, melt_temp, log_pressure, target_volume, inflow, self_blocks, link_blocks,
    link_columns, wall_owner, wall_slot, transfer_coef,
):
    cx, cy, cz = mold_temp.shape
    cells, blocks = melt_temp.shape
    planes = cx + 2 * WIDTH
    vmem = pl.BlockSpec(memory_space=pltpu.VMEM)
    hbm = pl.BlockSpec(memory_space=pltpu.HBM)

    def scratch(*shape):
        return pltpu.VMEM(shape, F32)

    cav = scratch(cells, blocks)
    return pl.pallas_call(
        kernel,
        out_shape=(
            jax.ShapeDtypeStruct(mold_temp.shape, F32),
            jax.ShapeDtypeStruct(melt_temp.shape, F32),
            jax.ShapeDtypeStruct(melt_temp.shape, F32),
        ),
        in_specs=[hbm] * 12,
        out_specs=(vmem, vmem, vmem),
        scratch_shapes=[
            pltpu.VMEM(self_blocks.shape, BF16),
            pltpu.VMEM(link_blocks.shape, BF16),
            scratch(ITERS, 4, 8, 16, 128),
            scratch(ITERS, 4, 8, 16, 128),
            scratch(ITERS, 4, 8, 16, 128),
            scratch(ITERS, 4, 16, 128),
            scratch(ITERS, 4, 16, 128),
            scratch(3, planes, cy, cz),
            scratch(3, 2, planes, 8, cz),
            scratch(3, 2, 24, cz),
            scratch(3, 2, 2, 24, cz),
            scratch(2, planes, 24, 2 * cz),
            scratch(planes, 24, 2 * cz),
            scratch(planes, 24, 2 * cz),
            scratch(cx, cy, cz),
            scratch(ITERS, 2, 8, cz),
            scratch(ITERS, 10, 8, cz),
            scratch(ITERS, 3, cy, cz),
            scratch(ITERS, 3, cy, cz),
            pltpu.VMEM((512, 128), BF16),
            pltpu.VMEM((128, 512), BF16),
            pltpu.VMEM((128, 256), BF16),
            cav, cav, cav, cav, cav, cav, cav, cav, cav, cav, cav,
            pltpu.VMEM((2, blocks), jnp.int32),
            pltpu.VMEM((1, blocks), jnp.int32),
            pltpu.VMEM((1, blocks), jnp.int32),
            pltpu.SemaphoreType.DMA((12,)),
            *[pltpu.SemaphoreType.DMA((ITERS, 4))] * 8,
            *[pltpu.SemaphoreType.DMA((ITERS, 3))] * 2,
            *[pltpu.SemaphoreType.DMA((ITERS,))] * 2,
            pltpu.SemaphoreType.DMA((3, 2)),
            pltpu.SemaphoreType.DMA((3, 2)),
            pltpu.SemaphoreType.DMA((3,)),
            pltpu.SemaphoreType.DMA((3,)),
            pltpu.SemaphoreType.DMA((3,)),
            pltpu.SemaphoreType.DMA((3,)),
        ],
        compiler_params=pltpu.CompilerParams(
            collective_id=0, has_side_effects=True, vmem_limit_bytes=56 * 1024 * 1024
        ),
    )(
        mold_temp, capacity, melt_temp, log_pressure, target_volume, inflow, transfer_coef,
        link_columns, wall_owner.reshape(1, blocks), wall_slot.reshape(1, blocks), self_blocks, link_blocks,
    )


def solution(mesh):
    cavity = P(None, ("wide", "mid", "narrow"))
    brick = P("wide", "mid", "narrow")
    flat = P(("wide", "mid", "narrow"))
    return jax.shard_map(
        per_device,
        mesh=mesh,
        in_specs=(
            brick, brick, cavity, cavity, cavity, cavity,
            P(None, None, ("wide", "mid", "narrow")),
            P(None, None, None, ("wide", "mid", "narrow")),
            cavity, flat, flat, cavity,
        ),
        out_specs=(brick, cavity, cavity),
        check_vma=False,
    )
```

```python
import functools

import jax
import jax.numpy as jnp
from jax import lax
from jax.experimental import pallas as pl
from jax.experimental.pallas import tpu as pltpu
from jax.sharding import PartitionSpec as P

BLOCK = 64
ITERS = 2
SWEEPS = 4
INNER = 2
WIDTH = 4
FAR_FIRST = (2, 1, 3)

CONDUCT = 1.0
COOLING = 0.5
TAIT_C = 0.3
EXPAND = 0.25
BULK_BASE = 0.5
BULK_SLOPE = 0.3

MESH = pl.DeviceIdType.MESH
F32 = jnp.float32
BF16 = jnp.bfloat16


def flip(v, k):
    if k == 0:
        return v
    if k == 1:
        return v + 1 - 2 * (v % 2)
    if k == 2:
        return (v + 2) % 4
    return 3 - v


def split_terms(x):
    hi = x.astype(BF16)
    lo = (x - hi.astype(F32)).astype(BF16)
    return hi, lo


def kernel(
    mold, cap, melt_in, logp, target_in, inflow_in, coef_in, columns_in, owner_in, slot_in, self_in, link_in,
    out_field, out_press, out_shrink,
    selfb, linkb, tab, spread, rs1, psum, rs2, near,
    row_own, row_ghost, lane_own, lane_ghost, rows_own, rows_ghost, lanes_own, lanes_ghost, corner_own, corner_ghost,
    ext, inv, base, plain, srcb, src_in, lower, lower_in,
    hot, hot_t, col_hot, diag, kv, resid, jdiag, slope, upd, state, melt, target, inflow, coef,
    columns, owner, slot,
    load_sem, zsend_sem, zrecv_sem, gsend_sem, grecv_sem, csend_sem, crecv_sem, ysend_sem, yrecv_sem,
    xsend_sem, xrecv_sem, lsend_sem, lrecv_sem, hsend_sem, hrecv_sem,
):
    cx, cy, cz = mold.shape
    planes = near.shape[1]
    w = lax.axis_index("wide")
    m = lax.axis_index("mid")
    n = lax.axis_index("narrow")
    n_w, n_m, n_n = lax.axis_size("wide"), lax.axis_size("mid"), lax.axis_size("narrow")
    zh, x, c = w // 8, (w // 2) % 4, w % 2

    def z_peer(k):
        return (flip(zh, k) * 8 + x * 2 + c, m, n)

    def xc_peer(j):
        return (zh * 8 + flip(x, j // 2) * 2 + flip(c, j % 2), m, n)

    def beside(dw, dm, dn):
        return ((w + n_w + dw) % n_w, (m + n_m + dm) % n_m, (n + n_n + dn) % n_n)

    barrier = pltpu.get_barrier_semaphore()
    peers = [z_peer(k) for k in range(1, 4)] + [xc_peer(j) for j in range(1, 8)]
    peers += [beside(-1, 0, 0), beside(1, 0, 0)]
    peers += [beside(0, dm, dn) for dm in (-1, 0, 1) for dn in (-1, 0, 1) if (dm, dn) != (0, 0)]
    for peer in peers:
        pl.semaphore_signal(barrier, inc=1, device_id=peer, device_id_type=MESH)

    loads = [
        pltpu.make_async_copy(src, dst, load_sem.at[i])
        for i, (src, dst) in enumerate((
            (owner_in, owner), (slot_in, slot), (coef_in, coef), (melt_in, melt),
            (mold, near.at[0, pl.ds(WIDTH, cx)]), (cap, near.at[1, pl.ds(WIDTH, cx)]), (columns_in, columns),
            (self_in, selfb), (link_in, linkb), (logp, state), (target_in, target), (inflow_in, inflow),
        ))
    ]
    for load in loads:
        load.start()

    def remote(src, dst, sems, peer):
        return pltpu.make_async_remote_copy(
            src_ref=src, dst_ref=dst, send_sem=sems[0], recv_sem=sems[1],
            device_id=peer, device_id_type=MESH,
        )

    def wait_recv(region, sems):
        remote(region, region, sems, beside(0, 1, 0)).wait_recv()

    def z_sems(it, k):
        return (zsend_sem.at[it, k], zrecv_sem.at[it, k])

    def gather_sems(it, k):
        return (gsend_sem.at[it, k], grecv_sem.at[it, k])

    def gather_on(it, k):
        for j in range(1, 8):
            remote(tab.at[it, k, 0], tab.at[it, k, j], gather_sems(it, k), xc_peer(j)).start()

    def gather_start(it):
        for k in FAR_FIRST:
            remote(tab.at[it, 0, 0], tab.at[it, k, 0], z_sems(it, k), z_peer(k)).start()

    def z_arrived(it, k):
        wait_recv(tab.at[it, k, 0], z_sems(it, k))
        gather_on(it, k)

    def cool(it):
        found = jnp.zeros((128, 256), F32)
        for k in (0, 1, 3, 2):
            wait_recv(tab.at[it, k, pl.ds(1, 7)], gather_sems(it, k))
            hi, lo = split_terms(tab[it, k].reshape(128, 128))
            found = found + jnp.dot(
                hot_t[:, k * 128:(k + 1) * 128], jnp.concatenate([hi, lo], axis=1), preferred_element_type=F32
            )
        found = (found[:, :128] + found[:, 128:]).T
        wall = jnp.where(half == 1, found[BLOCK:], found[:BLOCK])
        melt[...] = melt[...] - COOLING * (coef[...] * (melt[...] - wall))

    def scatter_sems(a, k):
        return (csend_sem.at[a, k], crecv_sem.at[a, k])

    def sum_sems(a, k):
        return (ysend_sem.at[a, k], yrecv_sem.at[a, k])

    def scatter_terms(values):
        parts = []
        for value in values:
            placed = jnp.concatenate([jnp.where(half == 0, value, 0.0), jnp.where(half == 1, value, 0.0)], axis=0)
            parts.extend(split_terms(placed))
        return jnp.concatenate(parts, axis=0)

    def scatter_start(a, terms):
        for k in FAR_FIRST + (0,):
            summed = lax.dot_general(
                hot[k * 128:(k + 1) * 128, :], terms, (((1,), (1,)), ((), ())), preferred_element_type=F32
            )
            for q in range(2):
                one = summed[:, 256 * q:256 * q + 128] + summed[:, 256 * q + 128:256 * q + 256]
                spread[a, k, :, q] = one.reshape(8, 16, 128)
            for j in range(1, 8):
                remote(spread.at[a, k, j], rs1.at[a, k, j], scatter_sems(a, k), xc_peer(j)).start()

    def scatter_on(a, k):
        wait_recv(rs1.at[a, k, pl.ds(1, 7)], scatter_sems(a, k))
        for q in range(2):
            total = spread[a, k, 0, q]
            for j in range(1, 8):
                total = total + rs1[a, k, j, q]
            psum[a, k, q] = total
        if k > 0:
            remote(psum.at[a, k], rs2.at[a, k], sum_sems(a, k), z_peer(k)).start()

    def scatter_done(a):
        for k in (1, 3, 2):
            wait_recv(rs2.at[a, k], sum_sems(a, k))
        return [((psum[a, 0, q] + rs2[a, 1, q]) + (rs2[a, 3, q] + rs2[a, 2, q])) for q in range(2)]

    lane = lax.broadcasted_iota(jnp.int32, (cy, cz), 1)
    lane24 = lax.broadcasted_iota(jnp.int32, (24, cz), 1)
    row8 = lax.broadcasted_iota(jnp.int32, (8, cz), 0)
    lane8 = lax.broadcasted_iota(jnp.int32, (8, cz), 1)
    own_planes = list(range(WIDTH, WIDTH + cx))
    ghost_planes = list(range(WIDTH)) + list(range(WIDTH + cx, planes))
    arrays = ((0, 1), (2,))

    def h_sems(g, step, kind):
        return (hsend_sem.at[g, step, kind], hrecv_sem.at[g, step, kind])

    def group(g):
        return pl.ds(arrays[g][0], len(arrays[g]))

    def send_low(g):
        remote(
            near.at[group(g), pl.ds(WIDTH, WIDTH)], near.at[group(g), pl.ds(WIDTH + cx, WIDTH)],
            h_sems(g, 0, 0), beside(-1, 0, 0),
        ).start()

    def send_high(g):
        remote(
            near.at[group(g), pl.ds(cx, WIDTH)], near.at[group(g), pl.ds(0, WIDTH)], h_sems(g, 0, 1), beside(1, 0, 0)
        ).start()

    def send_edges(g, step):
        which, row_out, lane_out, rows_in, lanes_in, corner_in = (
            (own_planes, row_own, lane_own, rows_own, lanes_own, corner_own),
            (ghost_planes, row_ghost, lane_ghost, rows_ghost, lanes_ghost, corner_ghost),
        )[step]
        for a in arrays[g]:
            packed = jnp.zeros((cy, cz), F32)
            for q, p in enumerate(which):
                packed = jnp.where(lane // 8 == q, pltpu.roll(near[a, p], WIDTH + 8 * q, 1), packed)
            lane_out[a, 0] = packed[:8]
            lane_out[a, 1] = packed[8:]
            for t in range(len(which) // 2):
                q = 4 * (t // 2) + t % 2
                one, two = near[a, which[q]], near[a, which[q + 2]]
                row_out[a, 0, t] = jnp.where(row8 < WIDTH, one[:8], pltpu.roll(two[:8], 4, 0))
                row_out[a, 1, t] = jnp.where(row8 < WIDTH, pltpu.roll(one[8:], 4, 0), two[8:])
        some = group(g)
        for side, dm in ((0, -1), (1, 1)):
            remote(row_out.at[some, side], rows_in.at[some, side], h_sems(g, step, 2), beside(0, dm, 0)).start()
        for side, dn in ((0, -1), (1, 1)):
            remote(lane_out.at[some], lanes_in.at[some, side], h_sems(g, step, 3), beside(0, 0, dn)).start()
            for tile, dm in ((0, -1), (1, 1)):
                remote(
                    lane_out.at[some, tile], corner_in.at[some, side, tile], h_sems(g, step, 4), beside(0, dm, dn)
                ).start()

    def take_edges(g, step, places):
        which, rows_in, lanes_in, corner_in = (
            (own_planes, rows_own, lanes_own, corner_own), (ghost_planes, rows_ghost, lanes_ghost, corner_ghost),
        )[step]
        some = group(g)
        for kind, region in ((2, rows_in), (3, lanes_in), (4, corner_in)):
            wait_recv(region.at[some], h_sems(g, step, kind))
        for a, dst in zip(arrays[g], places):
            sides = []
            for side in range(2):
                corner = jnp.where(row8 < WIDTH, corner_in[a, side, 0], corner_in[a, side, 1])
                sides.append(jnp.concatenate([lanes_in[a, side, 0], lanes_in[a, side, 1], corner], axis=0))
            comb = jnp.where(lane24 % 8 >= WIDTH, sides[0], sides[1])
            for t in range(len(which) // 2):
                q = 4 * (t // 2) + t % 2
                after, before = rows_in[a, 0, t], rows_in[a, 1, t]
                ghosts = (
                    (q, jnp.where(row8 < WIDTH, after, pltpu.roll(before, 4, 0))),
                    (q + 2, jnp.where(row8 < WIDTH, pltpu.roll(after, 4, 0), before)),
                )
                for at, ghost in ghosts:
                    p = which[at]
                    dst[p, 0:cy, 0:cz] = near[a, p]
                    dst[p, cy:24, 0:cz] = ghost
                    dst[p, :, cz:2 * cz] = pltpu.roll(comb, cz - (8 * at + WIDTH), 1)

    def wide_arrived(g):
        wait_recv(near.at[group(g), pl.ds(WIDTH + cx, WIDTH)], h_sems(g, 0, 0))
        wait_recv(near.at[group(g), pl.ds(0, WIDTH)], h_sems(g, 0, 1))
        send_edges(g, 1)

    def prepare():
        row_at = lax.broadcasted_iota(jnp.int32, (24, 2 * cz), 0)
        row_at = jnp.where(row_at < cy + WIDTH, row_at, row_at - 24) + m * cy
        lane_at = lax.broadcasted_iota(jnp.int32, (24, 2 * cz), 1)
        lane_real = (lane_at < cz + WIDTH) | (lane_at >= 2 * cz - WIDTH)
        lane_at = jnp.where(lane_at < cz + WIDTH, lane_at, lane_at - 2 * cz) + n * cz
        inside = lane_real & (row_at >= 0) & (row_at < n_m * cy) & (lane_at >= 0) & (lane_at < n_n * cz)
        inside = jnp.where(inside, 1.0, 0.0)
        for p in range(planes):
            here = inside
            if p < WIDTH:
                here = jnp.where(w > 0, inside, 0.0)
            elif p >= WIDTH + cx:
                here = jnp.where(w < n_w - 1, inside, 0.0)
            capacity, start = inv[p], ext[0, p]
            base[p] = capacity * start
            inv[p] = here / (capacity + 6.0 * CONDUCT)
            ext[0, p] = jnp.where(here > 0.0, start, 0.0)

    def around(plane):
        rows = pltpu.roll(plane, 1, 0) + pltpu.roll(plane, 23, 0)
        return rows + (pltpu.roll(plane, 1, 1) + pltpu.roll(plane, 2 * cz - 1, 1))

    def plain_sweeps():
        for k in range(SWEEPS):
            now, later = k % 2, (k + 1) % 2
            edge = k + 1
            for p in range(edge, planes - edge):
                total = (ext[now, p - 1] + ext[now, p + 1]) + around(ext[now, p]) + base[p]
                new = total * inv[p]
                if k == SWEEPS - 1:
                    plain[p - WIDTH] = new[:cy, :cz]
                else:
                    ext[later, p] = new

    def edge_sems(it, side):
        return (xsend_sem.at[it, side], xrecv_sem.at[it, side])

    def source_start(it, source):
        srcb[it, 0] = source[:8]
        srcb[it, 1] = source[8:]

        def send(side, parts):
            for src, place_at, count, dm, dn in parts:
                remote(
                    srcb.at[it, pl.ds(src, count)], src_in.at[it, pl.ds(place_at, count)],
                    edge_sems(it, side), beside(0, dm, dn),
                ).start()

        send(0, ((0, 0, 1, -1, 0), (1, 1, 1, 1, 0)))

        @pl.when(n > 0)
        def _():
            send(1, ((0, 2, 2, 0, -1), (0, 4, 1, -1, -1), (1, 5, 1, 1, -1)))

        @pl.when(n < n_n - 1)
        def _():
            send(2, ((0, 6, 2, 0, 1), (0, 8, 1, -1, 1), (1, 9, 1, 1, 1)))

    def source_done(it):
        wait_recv(src_in.at[it, pl.ds(0, 2)], edge_sems(it, 0))

        @pl.when(n < n_n - 1)
        def _():
            wait_recv(src_in.at[it, pl.ds(2, 4)], edge_sems(it, 1))

        @pl.when(n > 0)
        def _():
            wait_recv(src_in.at[it, pl.ds(6, 4)], edge_sems(it, 2))

        def corner(up, down):
            return jnp.where(row8 < WIDTH, src_in[it, up], src_in[it, down])

        def lanes(after, before):
            return jnp.where(lane8 < WIDTH, after, before)

        main = jnp.concatenate([srcb[it, 0], srcb[it, 1], corner(0, 1)], axis=0)
        sides = jnp.concatenate(
            [lanes(src_in[it, 2], src_in[it, 6]), lanes(src_in[it, 3], src_in[it, 7]), lanes(corner(4, 5), corner(8, 9))],
            axis=0,
        )
        return jnp.concatenate([main, sides], axis=1)

    def grown(wide_source, have, p):
        total = jnp.zeros((24, 2 * cz), F32)
        if p == 0:
            total = wide_source
        for q in (p - 1, p + 1):
            if q in have:
                total = total + have[q]
        if p in have:
            total = total + around(have[p])
        return total * inv[WIDTH + p]

    def first_sweeps(wide_source):
        one = {0: wide_source * inv[WIDTH]}
        two = {p: grown(wide_source, one, p) for p in (0, -1, 1)}
        three = {p: grown(wide_source, two, p) for p in (0, -1, 1)}
        wall = grown(wide_source, three, 0)[:cy, :cz]
        return two, three, wall

    def last_sweeps(it, wide_source, two, three):
        three.update({p: grown(wide_source, two, p) for p in (-2, 2)})
        for p in (-3, -2, -1):
            lower[it, p + 3] = grown(wide_source, three, p)[:cy, :cz]
        remote(lower.at[it], lower_in.at[it], (lsend_sem.at[it], lrecv_sem.at[it]), beside(-1, 0, 0)).start()
        return [grown(wide_source, three, p)[:cy, :cz] for p in (1, 2, 3)]

    def lower_arrived(it):
        wait_recv(lower_in.at[it], (lsend_sem.at[it], lrecv_sem.at[it]))

    def apply(v16):
        v = v16.astype(F32)
        linked = jnp.dot(v16, col_hot[...], preferred_element_type=F32)
        near0, near1 = linked[:, :128], linked[:, 128:]

        def rows(t, carry):
            sums = []
            for u in range(8):
                i = t * 8 + u
                prod = selfb[i].astype(F32) * v + linkb[0, i].astype(F32) * near0 + linkb[1, i].astype(F32) * near1
                sums.append(jnp.sum(prod, axis=0, keepdims=True))
            kv[pl.ds(pl.multiple_of(t * 8, 8), 8), :] = jnp.concatenate(sums, axis=0)
            return carry

        lax.fori_loop(0, BLOCK // 8, rows, 0)
        return kv[...]

    def newton_start():
        mt, st = melt[...], state[...]
        bulk = BULK_BASE * jnp.exp(-BULK_SLOPE * mt)
        growth = jnp.exp(st)
        press = bulk * (growth - 1.0)
        base_volume = jnp.exp(EXPAND * mt)
        volume = base_volume * (1.0 - TAIT_C * st)
        sl = bulk * growth
        slope[...] = sl
        jd = diag[...] * sl + TAIT_C * base_volume
        jdiag[...] = jd
        res = apply(press.astype(BF16)) + (target[...] - volume) - inflow[...]
        resid[...] = res
        upd[...] = -res / jd

    def newton_step():
        weighted = (slope[...] * upd[...]).astype(BF16)
        linked = apply(weighted) - diag[...] * weighted.astype(F32)
        upd[...] = (-resid[...] - linked) / jdiag[...]

    for load in loads[:4]:
        load.wait()
    rel = jnp.bitwise_xor(owner[...], w)
    place = rel * 16 + slot[...] // 2
    half = slot[...] % 2
    faces = lax.broadcasted_iota(jnp.int32, (512, 128), 0)
    hot32 = jnp.where(faces == place, 1.0, 0.0)
    hot[...] = hot32.astype(BF16)
    terms = scatter_terms((coef[...] * melt[...], coef[...]))
    for it in range(ITERS):
        src_in[it] = jnp.zeros((10, 8, cz), F32)
    loads[4].wait()
    tab[0, 0, 0] = near[0, WIDTH]
    pl.semaphore_wait(barrier, len(peers))

    scatter_start(0, terms)
    loads[5].wait()
    send_low(0)
    send_high(0)
    gather_start(0)
    send_edges(0, 0)
    gather_on(0, 0)
    hot_t[...] = hot32.T.astype(BF16)
    scatter_on(0, 2)
    scatter_on(0, 1)
    scatter_on(0, 3)
    for load in loads[6:]:
        load.wait()
    froms = lax.broadcasted_iota(jnp.int32, (128, 128), 0)
    for k in range(2):
        col_hot[:, k * 128:(k + 1) * 128] = jnp.where(froms == columns[k:k + 1, :], 1.0, 0.0).astype(BF16)
    z_arrived(0, 1)
    z_arrived(0, 3)
    wide_arrived(0)
    z_arrived(0, 2)
    scatter_on(0, 0)
    square = coef[...] * coef[...]
    scatter_start(1, scatter_terms((square * melt[...], square)))
    take_edges(0, 0, (ext.at[0], inv))

    sum_a, sum_b = scatter_done(0)
    first_wall = near[0, WIDTH]
    source_start(0, sum_a - sum_b * first_wall)
    take_edges(0, 1, (ext.at[0], inv))
    prepare()
    plain_sweeps()
    spread_source = source_done(0)
    two, three, wall_part = first_sweeps(spread_source)
    second_wall = plain[0] + wall_part
    tab[1, 0, 0] = second_wall
    gather_start(1)
    upper = last_sweeps(0, spread_source, two, three)
    near[2, WIDTH] = second_wall
    for p in range(1, 4):
        near[2, WIDTH + p] = plain[p] + upper[p - 1]
    send_low(1)
    gather_on(1, 0)
    for p in range(4, cx - 3):
        near[2, WIDTH + p] = plain[p]
    for k in FAR_FIRST + (0,):
        scatter_on(1, k)

    def pick(t, carry):
        sums = []
        for u in range(8):
            i = t * 8 + u
            mask = lax.broadcasted_iota(jnp.int32, (BLOCK, 128), 0) == i
            sums.append(jnp.sum(jnp.where(mask, selfb[i].astype(F32), 0.0), axis=0, keepdims=True))
        diag[pl.ds(pl.multiple_of(t * 8, 8), 8), :] = jnp.concatenate(sums, axis=0)
        return carry

    lax.fori_loop(0, BLOCK // 8, pick, 0)
    cool(0)
    newton_start()
    z_arrived(1, 1)
    z_arrived(1, 3)
    lower_arrived(0)
    for p in range(3):
        near[2, WIDTH + cx - 3 + p] = plain[cx - 3 + p] + lower_in[0, p]
    send_high(1)
    send_edges(1, 0)
    newton_step()
    z_arrived(1, 2)
    newton_step()
    state[...] = state[...] + upd[...]

    sum_c, sum_d = scatter_done(1)
    source_start(1, sum_a - COOLING * sum_c + COOLING * sum_d * first_wall - sum_b * second_wall)
    wide_arrived(1)
    take_edges(1, 0, (ext.at[0],))
    cool(1)
    newton_start()
    spread_source = source_done(1)
    two, three, wall_part = first_sweeps(spread_source)
    upper = last_sweeps(1, spread_source, two, three)
    newton_step()
    take_edges(1, 1, (ext.at[0],))
    for p in range(planes):
        ext[0, p] = jnp.where(inv[p] > 0.0, ext[0, p], 0.0)
    plain_sweeps()
    out_field[0] = plain[0] + wall_part
    for p in range(1, 4):
        out_field[p] = plain[p] + upper[p - 1]
    for p in range(4, cx - 3):
        out_field[p] = plain[p]
    newton_step()
    mt, st = melt[...], state[...] + upd[...]
    out_press[...] = BULK_BASE * jnp.exp(-BULK_SLOPE * mt) * (jnp.exp(st) - 1.0)
    out_shrink[...] = 1.0 - jnp.exp(EXPAND * mt) * (1.0 - TAIT_C * st)
    lower_arrived(1)
    for p in range(3):
        out_field[cx - 3 + p] = plain[cx - 3 + p] + lower_in[1, p]

    def wait_send(region, sems):
        remote(region, region, sems, beside(0, 1, 0)).wait_send()

    for it in range(ITERS):
        for k in range(4):
            if k > 0:
                wait_send(tab.at[it, k, 0], z_sems(it, k))
                wait_send(psum.at[it, k], sum_sems(it, k))
            wait_send(tab.at[it, k, pl.ds(1, 7)], gather_sems(it, k))
            wait_send(spread.at[it, k, pl.ds(1, 7)], scatter_sems(it, k))
        wait_send(src_in.at[it, pl.ds(0, 2)], edge_sems(it, 0))

        @pl.when(n > 0)
        def _():
            wait_send(src_in.at[it, pl.ds(2, 4)], edge_sems(it, 1))

        @pl.when(n < n_n - 1)
        def _():
            wait_send(src_in.at[it, pl.ds(6, 4)], edge_sems(it, 2))

        wait_send(lower.at[it], (lsend_sem.at[it], lrecv_sem.at[it]))
    for g in range(2):
        some = group(g)
        wait_send(near.at[some, pl.ds(0, WIDTH)], h_sems(g, 0, 0))
        wait_send(near.at[some, pl.ds(0, WIDTH)], h_sems(g, 0, 1))
        for step, regions in ((0, (rows_own, lanes_own, corner_own)), (1, (rows_ghost, lanes_ghost, corner_ghost))):
            for kind, region in enumerate(regions):
                wait_send(region.at[some], h_sems(g, step, 2 + kind))


def per_device(
    mold_temp, capacity, melt_temp, log_pressure, target_volume, inflow, self_blocks, link_blocks,
    link_columns, wall_owner, wall_slot, transfer_coef,
):
    cx, cy, cz = mold_temp.shape
    cells, blocks = melt_temp.shape
    planes = cx + 2 * WIDTH
    vmem = pl.BlockSpec(memory_space=pltpu.VMEM)
    hbm = pl.BlockSpec(memory_space=pltpu.HBM)

    def scratch(*shape):
        return pltpu.VMEM(shape, F32)

    cav = scratch(cells, blocks)
    return pl.pallas_call(
        kernel,
        out_shape=(
            pltpu.VMEM(mold_temp.shape, F32),
            pltpu.VMEM(melt_temp.shape, F32),
            pltpu.VMEM(melt_temp.shape, F32),
        ),
        in_specs=[hbm] * 12,
        out_specs=(vmem, vmem, vmem),
        scratch_shapes=[
            pltpu.VMEM(self_blocks.shape, BF16),
            pltpu.VMEM(link_blocks.shape, BF16),
            scratch(ITERS, 4, 8, 16, 128),
            scratch(2, 4, 8, 2, 16, 128),
            scratch(2, 4, 8, 2, 16, 128),
            scratch(2, 4, 2, 16, 128),
            scratch(2, 4, 2, 16, 128),
            scratch(3, planes, cy, cz),
            scratch(3, 2, 8, 8, cz),
            scratch(3, 2, 4, 8, cz),
            scratch(3, 2, 8, cz),
            scratch(3, 2, 8, cz),
            scratch(3, 2, 8, 8, cz),
            scratch(3, 2, 4, 8, cz),
            scratch(3, 2, 2, 8, cz),
            scratch(3, 2, 2, 8, cz),
            scratch(3, 2, 2, 8, cz),
            scratch(3, 2, 2, 8, cz),
            scratch(2, planes, 24, 2 * cz),
            scratch(planes, 24, 2 * cz),
            scratch(planes, 24, 2 * cz),
            scratch(cx, cy, cz),
            scratch(ITERS, 2, 8, cz),
            scratch(ITERS, 10, 8, cz),
            scratch(ITERS, 3, cy, cz),
            scratch(ITERS, 3, cy, cz),
            pltpu.VMEM((512, 128), BF16),
            pltpu.VMEM((128, 512), BF16),
            pltpu.VMEM((128, 256), BF16),
            cav, cav, cav, cav, cav, cav, cav, cav, cav, cav, cav,
            pltpu.VMEM((2, blocks), jnp.int32),
            pltpu.VMEM((1, blocks), jnp.int32),
            pltpu.VMEM((1, blocks), jnp.int32),
            pltpu.SemaphoreType.DMA((12,)),
            *[pltpu.SemaphoreType.DMA((ITERS, 4))] * 8,
            *[pltpu.SemaphoreType.DMA((ITERS, 3))] * 2,
            *[pltpu.SemaphoreType.DMA((ITERS,))] * 2,
            *[pltpu.SemaphoreType.DMA((2, 2, 5))] * 2,
        ],
        compiler_params=pltpu.CompilerParams(
            collective_id=0, has_side_effects=True, vmem_limit_bytes=56 * 1024 * 1024
        ),
    )(
        mold_temp, capacity, melt_temp, log_pressure, target_volume, inflow, transfer_coef,
        link_columns, wall_owner.reshape(1, blocks), wall_slot.reshape(1, blocks), self_blocks, link_blocks,
    )


def solution(mesh):
    cavity = P(None, ("wide", "mid", "narrow"))
    brick = P("wide", "mid", "narrow")
    flat = P(("wide", "mid", "narrow"))
    return jax.shard_map(
        per_device,
        mesh=mesh,
        in_specs=(
            brick, brick, cavity, cavity, cavity, cavity,
            P(None, None, ("wide", "mid", "narrow")),
            P(None, None, None, ("wide", "mid", "narrow")),
            cavity, flat, flat, cavity,
        ),
        out_specs=(brick, cavity, cavity),
        check_vma=False,
    )
```

```python
import functools

import jax
import jax.numpy as jnp
from jax import lax
from jax.experimental import pallas as pl
from jax.experimental.pallas import tpu as pltpu
from jax.sharding import PartitionSpec as P

BLOCK = 64
ITERS = 2
SWEEPS = 4
INNER = 2
WIDTH = 4
FAR_FIRST = (2, 1, 3)

CONDUCT = 1.0
COOLING = 0.5
TAIT_C = 0.3
EXPAND = 0.25
BULK_BASE = 0.5
BULK_SLOPE = 0.3

MESH = pl.DeviceIdType.MESH
F32 = jnp.float32
BF16 = jnp.bfloat16


def flip(v, k):
    if k == 0:
        return v
    if k == 1:
        return v + 1 - 2 * (v % 2)
    if k == 2:
        return (v + 2) % 4
    return 3 - v


def split_terms(x):
    hi = x.astype(BF16)
    lo = (x - hi.astype(F32)).astype(BF16)
    return hi, lo


def kernel(
    mold, cap, melt_in, logp, target_in, inflow_in, coef_in, columns_in, owner_in, slot_in, self_in, link_in,
    out_field, out_press, out_shrink,
    selfb, linkb, tab, spread, rs1, psum, rs2, near,
    row_own, row_ghost, lane_own, lane_ghost, rows_own, rows_ghost, lanes_own, lanes_ghost, corner_own, corner_ghost,
    ext, inv, base, plain, srcb, src_in, lower, lower_in,
    hot, hot_t, col_hot, diag, kv, resid, jdiag, slope, upd, state, melt, target, inflow, coef,
    columns, owner, slot,
    load_sem, zsend_sem, zrecv_sem, gsend_sem, grecv_sem, csend_sem, crecv_sem, ysend_sem, yrecv_sem,
    xsend_sem, xrecv_sem, lsend_sem, lrecv_sem, hsend_sem, hrecv_sem,
):
    cx, cy, cz = mold.shape
    planes = near.shape[1]
    w = lax.axis_index("wide")
    m = lax.axis_index("mid")
    n = lax.axis_index("narrow")
    n_w, n_m, n_n = lax.axis_size("wide"), lax.axis_size("mid"), lax.axis_size("narrow")
    zh, x, c = w // 8, (w // 2) % 4, w % 2

    def z_peer(k):
        return (flip(zh, k) * 8 + x * 2 + c, m, n)

    def xc_peer(j):
        return (zh * 8 + flip(x, j // 2) * 2 + flip(c, j % 2), m, n)

    def beside(dw, dm, dn):
        return ((w + n_w + dw) % n_w, (m + n_m + dm) % n_m, (n + n_n + dn) % n_n)

    barrier = pltpu.get_barrier_semaphore()
    peers = [z_peer(k) for k in range(1, 4)] + [xc_peer(j) for j in range(1, 8)]
    peers += [beside(-1, 0, 0), beside(1, 0, 0)]
    peers += [beside(0, dm, dn) for dm in (-1, 0, 1) for dn in (-1, 0, 1) if (dm, dn) != (0, 0)]
    for peer in peers:
        pl.semaphore_signal(barrier, inc=1, device_id=peer, device_id_type=MESH)

    loads = [
        pltpu.make_async_copy(src, dst, load_sem.at[i])
        for i, (src, dst) in enumerate((
            (owner_in, owner), (slot_in, slot), (coef_in, coef), (melt_in, melt),
            (mold, near.at[0, pl.ds(WIDTH, cx)]), (cap, near.at[1, pl.ds(WIDTH, cx)]), (columns_in, columns),
            (self_in, selfb), (link_in, linkb), (logp, state), (target_in, target), (inflow_in, inflow),
        ))
    ]
    for load in loads:
        load.start()

    def remote(src, dst, sems, peer):
        return pltpu.make_async_remote_copy(
            src_ref=src, dst_ref=dst, send_sem=sems[0], recv_sem=sems[1],
            device_id=peer, device_id_type=MESH,
        )

    def wait_recv(region, sems):
        remote(region, region, sems, beside(0, 1, 0)).wait_recv()

    def z_sems(it, k):
        return (zsend_sem.at[it, k], zrecv_sem.at[it, k])

    def gather_sems(it, k):
        return (gsend_sem.at[it, k], grecv_sem.at[it, k])

    def gather_on(it, k):
        for j in range(1, 8):
            remote(tab.at[it, k, 0], tab.at[it, k, j], gather_sems(it, k), xc_peer(j)).start()

    def gather_start(it):
        for k in FAR_FIRST:
            remote(tab.at[it, 0, 0], tab.at[it, k, 0], z_sems(it, k), z_peer(k)).start()

    def z_arrived(it, k):
        wait_recv(tab.at[it, k, 0], z_sems(it, k))
        gather_on(it, k)

    def cool(it):
        found = jnp.zeros((128, 256), F32)
        for k in (0, 1, 3, 2):
            wait_recv(tab.at[it, k, pl.ds(1, 7)], gather_sems(it, k))
            hi, lo = split_terms(tab[it, k].reshape(128, 128))
            found = found + jnp.dot(
                hot_t[:, k * 128:(k + 1) * 128], jnp.concatenate([hi, lo], axis=1), preferred_element_type=F32
            )
        found = (found[:, :128] + found[:, 128:]).T
        wall = jnp.where(half == 1, found[BLOCK:], found[:BLOCK])
        melt[...] = melt[...] - COOLING * (coef[...] * (melt[...] - wall))

    def scatter_sems(a, k):
        return (csend_sem.at[a, k], crecv_sem.at[a, k])

    def sum_sems(a, k):
        return (ysend_sem.at[a, k], yrecv_sem.at[a, k])

    def scatter_terms(values):
        parts = []
        for value in values:
            placed = jnp.concatenate([jnp.where(half == 0, value, 0.0), jnp.where(half == 1, value, 0.0)], axis=0)
            parts.extend(split_terms(placed))
        return jnp.concatenate(parts, axis=0)

    def scatter_fill(a, terms):
        for k in range(4):
            summed = lax.dot_general(
                hot[k * 128:(k + 1) * 128, :], terms, (((1,), (1,)), ((), ())), preferred_element_type=F32
            )
            for q in range(2):
                one = summed[:, 256 * q:256 * q + 128] + summed[:, 256 * q + 128:256 * q + 256]
                spread[a, k, :, q] = one.reshape(8, 16, 128)

    def scatter_start(a, k):
        for j in range(1, 8):
            remote(spread.at[a, k, j], rs1.at[a, k, j], scatter_sems(a, k), xc_peer(j)).start()

    def scatter_on(a, k):
        wait_recv(rs1.at[a, k, pl.ds(1, 7)], scatter_sems(a, k))
        for q in range(2):
            total = spread[a, k, 0, q]
            for j in range(1, 8):
                total = total + rs1[a, k, j, q]
            psum[a, k, q] = total
        if k > 0:
            remote(psum.at[a, k], rs2.at[a, k], sum_sems(a, k), z_peer(k)).start()

    def scatter_done(a):
        for k in (1, 3, 2):
            wait_recv(rs2.at[a, k], sum_sems(a, k))
        return [((psum[a, 0, q] + rs2[a, 1, q]) + (rs2[a, 3, q] + rs2[a, 2, q])) for q in range(2)]

    lane = lax.broadcasted_iota(jnp.int32, (cy, cz), 1)
    lane24 = lax.broadcasted_iota(jnp.int32, (24, cz), 1)
    row8 = lax.broadcasted_iota(jnp.int32, (8, cz), 0)
    lane8 = lax.broadcasted_iota(jnp.int32, (8, cz), 1)
    own_planes = list(range(WIDTH, WIDTH + cx))
    ghost_planes = list(range(WIDTH)) + list(range(WIDTH + cx, planes))
    arrays = ((0, 1), (2,))

    def h_sems(g, step, kind):
        return (hsend_sem.at[g, step, kind], hrecv_sem.at[g, step, kind])

    def group(g):
        return pl.ds(arrays[g][0], len(arrays[g]))

    def send_low(g):
        remote(
            near.at[group(g), pl.ds(WIDTH, WIDTH)], near.at[group(g), pl.ds(WIDTH + cx, WIDTH)],
            h_sems(g, 0, 0), beside(-1, 0, 0),
        ).start()

    def send_high(g):
        remote(
            near.at[group(g), pl.ds(cx, WIDTH)], near.at[group(g), pl.ds(0, WIDTH)], h_sems(g, 0, 1), beside(1, 0, 0)
        ).start()

    def pack_edges(g, step):
        which, row_out, lane_out = ((own_planes, row_own, lane_own), (ghost_planes, row_ghost, lane_ghost))[step]
        for a in arrays[g]:
            packed = jnp.zeros((cy, cz), F32)
            for q, p in enumerate(which):
                packed = jnp.where(lane // 8 == q, pltpu.roll(near[a, p], WIDTH + 8 * q, 1), packed)
            lane_out[a, 0] = packed[:8]
            lane_out[a, 1] = packed[8:]
            for t in range(len(which) // 2):
                q = 4 * (t // 2) + t % 2
                one, two = near[a, which[q]], near[a, which[q + 2]]
                row_out[a, 0, t] = jnp.where(row8 < WIDTH, one[:8], pltpu.roll(two[:8], 4, 0))
                row_out[a, 1, t] = jnp.where(row8 < WIDTH, pltpu.roll(one[8:], 4, 0), two[8:])

    def send_edges(g, step):
        row_out, lane_out, rows_in, lanes_in, corner_in = (
            (row_own, lane_own, rows_own, lanes_own, corner_own),
            (row_ghost, lane_ghost, rows_ghost, lanes_ghost, corner_ghost),
        )[step]
        some = group(g)
        for side, dm in ((0, -1), (1, 1)):
            remote(row_out.at[some, side], rows_in.at[some, side], h_sems(g, step, 2), beside(0, dm, 0)).start()
        for side, dn in ((0, -1), (1, 1)):
            remote(lane_out.at[some], lanes_in.at[some, side], h_sems(g, step, 3), beside(0, 0, dn)).start()
            for tile, dm in ((0, -1), (1, 1)):
                remote(
                    lane_out.at[some, tile], corner_in.at[some, side, tile], h_sems(g, step, 4), beside(0, dm, dn)
                ).start()

    def take_edges(g, step, places):
        which, rows_in, lanes_in, corner_in = (
            (own_planes, rows_own, lanes_own, corner_own), (ghost_planes, rows_ghost, lanes_ghost, corner_ghost),
        )[step]
        some = group(g)
        for kind, region in ((2, rows_in), (3, lanes_in), (4, corner_in)):
            wait_recv(region.at[some], h_sems(g, step, kind))
        for a, dst in zip(arrays[g], places):
            sides = []
            for side in range(2):
                corner = jnp.where(row8 < WIDTH, corner_in[a, side, 0], corner_in[a, side, 1])
                sides.append(jnp.concatenate([lanes_in[a, side, 0], lanes_in[a, side, 1], corner], axis=0))
            comb = jnp.where(lane24 % 8 >= WIDTH, sides[0], sides[1])
            for t in range(len(which) // 2):
                q = 4 * (t // 2) + t % 2
                after, before = rows_in[a, 0, t], rows_in[a, 1, t]
                ghosts = (
                    (q, jnp.where(row8 < WIDTH, after, pltpu.roll(before, 4, 0))),
                    (q + 2, jnp.where(row8 < WIDTH, pltpu.roll(after, 4, 0), before)),
                )
                for at, ghost in ghosts:
                    p = which[at]
                    dst[p, 0:cy, 0:cz] = near[a, p]
                    dst[p, cy:24, 0:cz] = ghost
                    dst[p, :, cz:2 * cz] = pltpu.roll(comb, cz - (8 * at + WIDTH), 1)

    def wide_arrived(g):
        wait_recv(near.at[group(g), pl.ds(WIDTH + cx, WIDTH)], h_sems(g, 0, 0))
        wait_recv(near.at[group(g), pl.ds(0, WIDTH)], h_sems(g, 0, 1))
        pack_edges(g, 1)
        send_edges(g, 1)

    def prepare():
        row_at = lax.broadcasted_iota(jnp.int32, (24, 2 * cz), 0)
        row_at = jnp.where(row_at < cy + WIDTH, row_at, row_at - 24) + m * cy
        lane_at = lax.broadcasted_iota(jnp.int32, (24, 2 * cz), 1)
        lane_real = (lane_at < cz + WIDTH) | (lane_at >= 2 * cz - WIDTH)
        lane_at = jnp.where(lane_at < cz + WIDTH, lane_at, lane_at - 2 * cz) + n * cz
        inside = lane_real & (row_at >= 0) & (row_at < n_m * cy) & (lane_at >= 0) & (lane_at < n_n * cz)
        inside = jnp.where(inside, 1.0, 0.0)
        for p in range(planes):
            here = inside
            if p < WIDTH:
                here = jnp.where(w > 0, inside, 0.0)
            elif p >= WIDTH + cx:
                here = jnp.where(w < n_w - 1, inside, 0.0)
            capacity, start = inv[p], ext[0, p]
            base[p] = capacity * start
            inv[p] = here / (capacity + 6.0 * CONDUCT)
            ext[0, p] = jnp.where(here > 0.0, start, 0.0)

    def around(plane):
        rows = pltpu.roll(plane, 1, 0) + pltpu.roll(plane, 23, 0)
        return rows + (pltpu.roll(plane, 1, 1) + pltpu.roll(plane, 2 * cz - 1, 1))

    def plain_sweeps():
        for k in range(SWEEPS):
            now, later = k % 2, (k + 1) % 2
            edge = k + 1
            for p in range(edge, planes - edge):
                total = (ext[now, p - 1] + ext[now, p + 1]) + around(ext[now, p]) + base[p]
                new = total * inv[p]
                if k == SWEEPS - 1:
                    plain[p - WIDTH] = new[:cy, :cz]
                else:
                    ext[later, p] = new

    def edge_sems(it, side):
        return (xsend_sem.at[it, side], xrecv_sem.at[it, side])

    def source_start(it, source):
        srcb[it, 0] = source[:8]
        srcb[it, 1] = source[8:]

        def send(side, parts):
            for src, place_at, count, dm, dn in parts:
                remote(
                    srcb.at[it, pl.ds(src, count)], src_in.at[it, pl.ds(place_at, count)],
                    edge_sems(it, side), beside(0, dm, dn),
                ).start()

        send(0, ((0, 0, 1, -1, 0), (1, 1, 1, 1, 0)))

        @pl.when(n > 0)
        def _():
            send(1, ((0, 2, 2, 0, -1), (0, 4, 1, -1, -1), (1, 5, 1, 1, -1)))

        @pl.when(n < n_n - 1)
        def _():
            send(2, ((0, 6, 2, 0, 1), (0, 8, 1, -1, 1), (1, 9, 1, 1, 1)))

    def source_done(it):
        wait_recv(src_in.at[it, pl.ds(0, 2)], edge_sems(it, 0))

        @pl.when(n < n_n - 1)
        def _():
            wait_recv(src_in.at[it, pl.ds(2, 4)], edge_sems(it, 1))

        @pl.when(n > 0)
        def _():
            wait_recv(src_in.at[it, pl.ds(6, 4)], edge_sems(it, 2))

        def corner(up, down):
            return jnp.where(row8 < WIDTH, src_in[it, up], src_in[it, down])

        def lanes(after, before):
            return jnp.where(lane8 < WIDTH, after, before)

        main = jnp.concatenate([srcb[it, 0], srcb[it, 1], corner(0, 1)], axis=0)
        sides = jnp.concatenate(
            [lanes(src_in[it, 2], src_in[it, 6]), lanes(src_in[it, 3], src_in[it, 7]), lanes(corner(4, 5), corner(8, 9))],
            axis=0,
        )
        return jnp.concatenate([main, sides], axis=1)

    def grown(wide_source, have, p):
        total = jnp.zeros((24, 2 * cz), F32)
        if p == 0:
            total = wide_source
        for q in (p - 1, p + 1):
            if q in have:
                total = total + have[q]
        if p in have:
            total = total + around(have[p])
        return total * inv[WIDTH + p]

    def first_sweeps(wide_source):
        one = {0: wide_source * inv[WIDTH]}
        two = {p: grown(wide_source, one, p) for p in (0, -1, 1)}
        three = {p: grown(wide_source, two, p) for p in (0, -1, 1)}
        wall = grown(wide_source, three, 0)[:cy, :cz]
        return two, three, wall

    def last_sweeps(it, wide_source, two, three):
        three.update({p: grown(wide_source, two, p) for p in (-2, 2)})
        for p in (-3, -2, -1):
            lower[it, p + 3] = grown(wide_source, three, p)[:cy, :cz]
        remote(lower.at[it], lower_in.at[it], (lsend_sem.at[it], lrecv_sem.at[it]), beside(-1, 0, 0)).start()
        return [grown(wide_source, three, p)[:cy, :cz] for p in (1, 2, 3)]

    def lower_arrived(it):
        wait_recv(lower_in.at[it], (lsend_sem.at[it], lrecv_sem.at[it]))

    def apply(v16):
        v = v16.astype(F32)
        linked = jnp.dot(v16, col_hot[...], preferred_element_type=F32)
        near0, near1 = linked[:, :128], linked[:, 128:]

        def rows(t, carry):
            sums = []
            for u in range(8):
                i = t * 8 + u
                prod = selfb[i].astype(F32) * v + linkb[0, i].astype(F32) * near0 + linkb[1, i].astype(F32) * near1
                sums.append(jnp.sum(prod, axis=0, keepdims=True))
            kv[pl.ds(pl.multiple_of(t * 8, 8), 8), :] = jnp.concatenate(sums, axis=0)
            return carry

        lax.fori_loop(0, BLOCK // 8, rows, 0)
        return kv[...]

    def newton_start():
        mt, st = melt[...], state[...]
        bulk = BULK_BASE * jnp.exp(-BULK_SLOPE * mt)
        growth = jnp.exp(st)
        press = bulk * (growth - 1.0)
        base_volume = jnp.exp(EXPAND * mt)
        volume = base_volume * (1.0 - TAIT_C * st)
        sl = bulk * growth
        slope[...] = sl
        jd = diag[...] * sl + TAIT_C * base_volume
        jdiag[...] = jd
        rounded = press.astype(BF16)
        res = apply(rounded) + diag[...] * rounded.astype(F32) + (target[...] - volume) - inflow[...]
        resid[...] = res
        upd[...] = -res / jd

    def newton_step():
        weighted = (slope[...] * upd[...]).astype(BF16)
        upd[...] = (-resid[...] - apply(weighted)) / jdiag[...]

    for load in loads[:4]:
        load.wait()
    rel = jnp.bitwise_xor(owner[...], w)
    place = rel * 16 + slot[...] // 2
    half = slot[...] % 2
    faces = lax.broadcasted_iota(jnp.int32, (512, 128), 0)
    hot32 = jnp.where(faces == place, 1.0, 0.0)
    hot[...] = hot32.astype(BF16)
    scatter_fill(0, scatter_terms((coef[...] * melt[...], coef[...])))
    for it in range(ITERS):
        src_in[it] = jnp.zeros((10, 8, cz), F32)
    loads[4].wait()
    loads[5].wait()
    tab[0, 0, 0] = near[0, WIDTH]
    pack_edges(0, 0)
    pl.semaphore_wait(barrier, len(peers))

    for k in FAR_FIRST:
        scatter_start(0, k)
    send_low(0)
    send_high(0)
    gather_start(0)
    send_edges(0, 0)
    scatter_start(0, 0)
    gather_on(0, 0)
    hot_t[...] = hot32.T.astype(BF16)
    for load in loads[6:]:
        load.wait()
    froms = lax.broadcasted_iota(jnp.int32, (128, 128), 0)
    for k in range(2):
        col_hot[:, k * 128:(k + 1) * 128] = jnp.where(froms == columns[k:k + 1, :], 1.0, 0.0).astype(BF16)

    def pick(t, carry):
        sums = []
        for u in range(8):
            i = t * 8 + u
            mask = lax.broadcasted_iota(jnp.int32, (BLOCK, 128), 0) == i
            block = selfb[i].astype(F32)
            sums.append(jnp.sum(jnp.where(mask, block, 0.0), axis=0, keepdims=True))
            selfb[i] = jnp.where(mask, 0.0, block).astype(BF16)
        diag[pl.ds(pl.multiple_of(t * 8, 8), 8), :] = jnp.concatenate(sums, axis=0)
        return carry

    lax.fori_loop(0, BLOCK // 8, pick, 0)
    for k in FAR_FIRST:
        scatter_on(0, k)
    square = coef[...] * coef[...]
    scatter_fill(1, scatter_terms((square * melt[...], square)))
    z_arrived(0, 1)
    z_arrived(0, 3)
    wide_arrived(0)
    for k in FAR_FIRST + (0,):
        scatter_start(1, k)
    take_edges(0, 0, (ext.at[0], inv))
    scatter_on(0, 0)

    sum_a, sum_b = scatter_done(0)
    first_wall = near[0, WIDTH]
    source_start(0, sum_a - sum_b * first_wall)
    z_arrived(0, 2)
    take_edges(0, 1, (ext.at[0], inv))
    prepare()
    plain_sweeps()
    spread_source = source_done(0)
    two, three, wall_part = first_sweeps(spread_source)
    second_wall = plain[0] + wall_part
    tab[1, 0, 0] = second_wall
    gather_start(1)
    gather_on(1, 0)
    upper = last_sweeps(0, spread_source, two, three)
    near[2, WIDTH] = second_wall
    for p in range(1, 4):
        near[2, WIDTH + p] = plain[p] + upper[p - 1]
    send_low(1)
    for k in FAR_FIRST + (0,):
        scatter_on(1, k)
    for p in range(4, cx - 3):
        near[2, WIDTH + p] = plain[p]

    cool(0)
    newton_start()
    z_arrived(1, 1)
    z_arrived(1, 3)
    lower_arrived(0)
    for p in range(3):
        near[2, WIDTH + cx - 3 + p] = plain[cx - 3 + p] + lower_in[0, p]
    send_high(1)
    pack_edges(1, 0)
    send_edges(1, 0)
    newton_step()
    sum_c, sum_d = scatter_done(1)
    source_start(1, sum_a - COOLING * sum_c + COOLING * sum_d * first_wall - sum_b * second_wall)
    z_arrived(1, 2)
    newton_step()
    state[...] = state[...] + upd[...]
    wide_arrived(1)
    take_edges(1, 0, (ext.at[0],))
    spread_source = source_done(1)
    two, three, wall_part = first_sweeps(spread_source)
    upper = last_sweeps(1, spread_source, two, three)

    cool(1)
    newton_start()
    take_edges(1, 1, (ext.at[0],))
    for p in range(planes):
        ext[0, p] = jnp.where(inv[p] > 0.0, ext[0, p], 0.0)
    plain_sweeps()
    out_field[0] = plain[0] + wall_part
    for p in range(1, 4):
        out_field[p] = plain[p] + upper[p - 1]
    for p in range(4, cx - 3):
        out_field[p] = plain[p]
    newton_step()
    lower_arrived(1)
    for p in range(3):
        out_field[cx - 3 + p] = plain[cx - 3 + p] + lower_in[1, p]
    newton_step()
    mt, st = melt[...], state[...] + upd[...]
    out_press[...] = BULK_BASE * jnp.exp(-BULK_SLOPE * mt) * (jnp.exp(st) - 1.0)
    out_shrink[...] = 1.0 - jnp.exp(EXPAND * mt) * (1.0 - TAIT_C * st)

    def wait_send(region, sems):
        remote(region, region, sems, beside(0, 1, 0)).wait_send()

    for it in range(ITERS):
        for k in range(4):
            if k > 0:
                wait_send(tab.at[it, k, 0], z_sems(it, k))
                wait_send(psum.at[it, k], sum_sems(it, k))
            wait_send(tab.at[it, k, pl.ds(1, 7)], gather_sems(it, k))
            wait_send(spread.at[it, k, pl.ds(1, 7)], scatter_sems(it, k))
        wait_send(src_in.at[it, pl.ds(0, 2)], edge_sems(it, 0))

        @pl.when(n > 0)
        def _():
            wait_send(src_in.at[it, pl.ds(2, 4)], edge_sems(it, 1))

        @pl.when(n < n_n - 1)
        def _():
            wait_send(src_in.at[it, pl.ds(6, 4)], edge_sems(it, 2))

        wait_send(lower.at[it], (lsend_sem.at[it], lrecv_sem.at[it]))
    for g in range(2):
        some = group(g)
        wait_send(near.at[some, pl.ds(0, WIDTH)], h_sems(g, 0, 0))
        wait_send(near.at[some, pl.ds(0, WIDTH)], h_sems(g, 0, 1))
        for step, regions in ((0, (rows_own, lanes_own, corner_own)), (1, (rows_ghost, lanes_ghost, corner_ghost))):
            for kind, region in enumerate(regions):
                wait_send(region.at[some], h_sems(g, step, 2 + kind))


def per_device(
    mold_temp, capacity, melt_temp, log_pressure, target_volume, inflow, self_blocks, link_blocks,
    link_columns, wall_owner, wall_slot, transfer_coef,
):
    cx, cy, cz = mold_temp.shape
    cells, blocks = melt_temp.shape
    planes = cx + 2 * WIDTH
    vmem = pl.BlockSpec(memory_space=pltpu.VMEM)
    hbm = pl.BlockSpec(memory_space=pltpu.HBM)

    def scratch(*shape):
        return pltpu.VMEM(shape, F32)

    cav = scratch(cells, blocks)
    return pl.pallas_call(
        kernel,
        out_shape=(
            pltpu.VMEM(mold_temp.shape, F32),
            pltpu.VMEM(melt_temp.shape, F32),
            pltpu.VMEM(melt_temp.shape, F32),
        ),
        in_specs=[hbm] * 12,
        out_specs=(vmem, vmem, vmem),
        scratch_shapes=[
            pltpu.VMEM(self_blocks.shape, BF16),
            pltpu.VMEM(link_blocks.shape, BF16),
            scratch(ITERS, 4, 8, 16, 128),
            scratch(2, 4, 8, 2, 16, 128),
            scratch(2, 4, 8, 2, 16, 128),
            scratch(2, 4, 2, 16, 128),
            scratch(2, 4, 2, 16, 128),
            scratch(3, planes, cy, cz),
            scratch(3, 2, 8, 8, cz),
            scratch(3, 2, 4, 8, cz),
            scratch(3, 2, 8, cz),
            scratch(3, 2, 8, cz),
            scratch(3, 2, 8, 8, cz),
            scratch(3, 2, 4, 8, cz),
            scratch(3, 2, 2, 8, cz),
            scratch(3, 2, 2, 8, cz),
            scratch(3, 2, 2, 8, cz),
            scratch(3, 2, 2, 8, cz),
            scratch(2, planes, 24, 2 * cz),
            scratch(planes, 24, 2 * cz),
            scratch(planes, 24, 2 * cz),
            scratch(cx, cy, cz),
            scratch(ITERS, 2, 8, cz),
            scratch(ITERS, 10, 8, cz),
            scratch(ITERS, 3, cy, cz),
            scratch(ITERS, 3, cy, cz),
            pltpu.VMEM((512, 128), BF16),
            pltpu.VMEM((128, 512), BF16),
            pltpu.VMEM((128, 256), BF16),
            cav, cav, cav, cav, cav, cav, cav, cav, cav, cav, cav,
            pltpu.VMEM((2, blocks), jnp.int32),
            pltpu.VMEM((1, blocks), jnp.int32),
            pltpu.VMEM((1, blocks), jnp.int32),
            pltpu.SemaphoreType.DMA((12,)),
            *[pltpu.SemaphoreType.DMA((ITERS, 4))] * 8,
            *[pltpu.SemaphoreType.DMA((ITERS, 3))] * 2,
            *[pltpu.SemaphoreType.DMA((ITERS,))] * 2,
            *[pltpu.SemaphoreType.DMA((2, 2, 5))] * 2,
        ],
        compiler_params=pltpu.CompilerParams(
            collective_id=0, has_side_effects=True, vmem_limit_bytes=56 * 1024 * 1024
        ),
    )(
        mold_temp, capacity, melt_temp, log_pressure, target_volume, inflow, transfer_coef,
        link_columns, wall_owner.reshape(1, blocks), wall_slot.reshape(1, blocks), self_blocks, link_blocks,
    )


def solution(mesh):
    cavity = P(None, ("wide", "mid", "narrow"))
    brick = P("wide", "mid", "narrow")
    flat = P(("wide", "mid", "narrow"))
    return jax.shard_map(
        per_device,
        mesh=mesh,
        in_specs=(
            brick, brick, cavity, cavity, cavity, cavity,
            P(None, None, ("wide", "mid", "narrow")),
            P(None, None, None, ("wide", "mid", "narrow")),
            cavity, flat, flat, cavity,
        ),
        out_specs=(brick, cavity, cavity),
        check_vma=False,
    )
```

```python
import functools

import jax
import jax.numpy as jnp
from jax import lax
from jax.experimental import pallas as pl
from jax.experimental.pallas import tpu as pltpu
from jax.sharding import PartitionSpec as P

BLOCK = 64
ITERS = 2
SWEEPS = 4
INNER = 2
WIDTH = 4
DISTANCE = (0, 1, 3, 2)

CONDUCT = 1.0
COOLING = 0.5
TAIT_C = 0.3
EXPAND = 0.25
BULK_BASE = 0.5
BULK_SLOPE = 0.3

MESH = pl.DeviceIdType.MESH
F32 = jnp.float32
BF16 = jnp.bfloat16


def flip(v, k):
    if k == 0:
        return v
    if k == 1:
        return v + 1 - 2 * (v % 2)
    if k == 2:
        return (v + 2) % 4
    return 3 - v


def split_terms(x):
    hi = x.astype(BF16)
    lo = (x - hi.astype(F32)).astype(BF16)
    return hi, lo


def kernel(
    mold, cap, melt_in, logp, target_in, inflow_in, coef_in, columns_in, owner_in, slot_in, self_in, link_in,
    out_field, out_press, out_shrink,
    selfb, linkb, tab, spread, rs1, psum, rs2, near,
    row_own, row_ghost, lane_own, lane_ghost, rows_own, rows_ghost, lanes_own, lanes_ghost, corner_own, corner_ghost,
    ext, inv, base, plain, srcb, src_in, lower, lower_in,
    hot, hot_t, col_hot, diag, kv, resid, jdiag, slope, upd, state, melt, target, inflow, coef,
    columns, owner, slot,
    load_sem, zsend_sem, zrecv_sem, gsend_sem, grecv_sem, csend_sem, crecv_sem, ysend_sem, yrecv_sem,
    xsend_sem, xrecv_sem, lsend_sem, lrecv_sem, hsend_sem, hrecv_sem,
):
    cx, cy, cz = mold.shape
    planes = near.shape[1]
    w = lax.axis_index("wide")
    m = lax.axis_index("mid")
    n = lax.axis_index("narrow")
    n_w, n_m, n_n = lax.axis_size("wide"), lax.axis_size("mid"), lax.axis_size("narrow")
    zh, x, c = w // 8, (w // 2) % 4, w % 2

    def z_peer(k):
        return (flip(zh, k) * 8 + x * 2 + c, m, n)

    def xc_peer(j):
        return (zh * 8 + flip(x, j // 2) * 2 + flip(c, j % 2), m, n)

    def beside(dw, dm, dn):
        return ((w + n_w + dw) % n_w, (m + n_m + dm) % n_m, (n + n_n + dn) % n_n)

    barrier = pltpu.get_barrier_semaphore()
    peers = [z_peer(k) for k in range(1, 4)] + [xc_peer(j) for j in range(1, 8)]
    peers += [beside(-1, 0, 0), beside(1, 0, 0)]
    peers += [beside(0, dm, dn) for dm in (-1, 0, 1) for dn in (-1, 0, 1) if (dm, dn) != (0, 0)]
    for peer in peers:
        pl.semaphore_signal(barrier, inc=1, device_id=peer, device_id_type=MESH)

    loads = [
        pltpu.make_async_copy(src, dst, load_sem.at[i])
        for i, (src, dst) in enumerate((
            (owner_in, owner), (slot_in, slot), (coef_in, coef), (melt_in, melt),
            (mold, near.at[0, pl.ds(WIDTH, cx)]), (cap, near.at[1, pl.ds(WIDTH, cx)]), (columns_in, columns),
            (self_in, selfb), (link_in, linkb), (logp, state), (target_in, target), (inflow_in, inflow),
        ))
    ]
    for load in loads:
        load.start()

    def remote(src, dst, sems, peer):
        return pltpu.make_async_remote_copy(
            src_ref=src, dst_ref=dst, send_sem=sems[0], recv_sem=sems[1],
            device_id=peer, device_id_type=MESH,
        )

    def wait_recv(region, sems):
        remote(region, region, sems, beside(0, 1, 0)).wait_recv()

    def z_sems(it, k):
        return (zsend_sem.at[it, k], zrecv_sem.at[it, k])

    def gather_sems(it, part):
        return (gsend_sem.at[it, part], grecv_sem.at[it, part])

    gather_parts = ((0, 3), (3, 1))
    scatter_parts = ((3, 1), (1, 2), (0, 1))

    def gather_start(it):
        for k in (3, 1, 2):
            remote(tab.at[it, 0, 0], tab.at[it, 0, k], z_sems(it, k), z_peer(DISTANCE[k])).start()

    def gather_on(it, part):
        first, count = gather_parts[part]
        for k in range(max(first, 1), first + count):
            wait_recv(tab.at[it, 0, k], z_sems(it, k))
        for j in range(1, 8):
            remote(
                tab.at[it, 0, pl.ds(first, count)], tab.at[it, j, pl.ds(first, count)], gather_sems(it, part), xc_peer(j)
            ).start()

    def cool(it):
        for part, (first, count) in enumerate(gather_parts):
            wait_recv(tab.at[it, pl.ds(1, 7), pl.ds(first, count)], gather_sems(it, part))
        hi, lo = split_terms(tab[it].reshape(512, 128))
        found = jnp.dot(hot_t[...], jnp.concatenate([hi, lo], axis=1), preferred_element_type=F32)
        found = (found[:, :128] + found[:, 128:]).T
        wall = jnp.where(half == 1, found[BLOCK:], found[:BLOCK])
        melt[...] = melt[...] - COOLING * (coef[...] * (melt[...] - wall))

    def scatter_sems(a, part):
        return (csend_sem.at[a, part], crecv_sem.at[a, part])

    def sum_sems(a, k):
        return (ysend_sem.at[a, k], yrecv_sem.at[a, k])

    def scatter_terms(values):
        parts = []
        for value in values:
            placed = jnp.concatenate([jnp.where(half == 0, value, 0.0), jnp.where(half == 1, value, 0.0)], axis=0)
            parts.extend(split_terms(placed))
        return jnp.concatenate(parts, axis=0)

    def scatter_fill(a, terms):
        for j in range(0, 8, 2):
            summed = lax.dot_general(
                hot[j * 64:(j + 2) * 64, :], terms, (((1,), (1,)), ((), ())), preferred_element_type=F32
            )
            for q in range(2):
                one = summed[:, 256 * q:256 * q + 128] + summed[:, 256 * q + 128:256 * q + 256]
                spread[a, j:j + 2, :, q] = one.reshape(2, 4, 16, 128)

    def scatter_start(a, part):
        first, count = scatter_parts[part]
        for j in range(1, 8):
            remote(
                spread.at[a, j, pl.ds(first, count)], rs1.at[a, j, pl.ds(first, count)], scatter_sems(a, part), xc_peer(j)
            ).start()

    def scatter_on(a, part):
        first, count = scatter_parts[part]
        wait_recv(rs1.at[a, pl.ds(1, 7), pl.ds(first, count)], scatter_sems(a, part))
        for k in range(first, first + count):
            for q in range(2):
                total = spread[a, 0, k, q]
                for j in range(1, 8):
                    total = total + rs1[a, j, k, q]
                psum[a, k, q] = total
            if k > 0:
                remote(psum.at[a, k], rs2.at[a, k], sum_sems(a, k), z_peer(DISTANCE[k])).start()

    def scatter_done(a):
        for k in (1, 2, 3):
            wait_recv(rs2.at[a, k], sum_sems(a, k))
        return [((psum[a, 0, q] + rs2[a, 1, q]) + (rs2[a, 2, q] + rs2[a, 3, q])) for q in range(2)]

    lane = lax.broadcasted_iota(jnp.int32, (cy, cz), 1)
    lane24 = lax.broadcasted_iota(jnp.int32, (24, cz), 1)
    row8 = lax.broadcasted_iota(jnp.int32, (8, cz), 0)
    lane8 = lax.broadcasted_iota(jnp.int32, (8, cz), 1)
    own_planes = list(range(WIDTH, WIDTH + cx))
    ghost_planes = list(range(WIDTH)) + list(range(WIDTH + cx, planes))
    arrays = ((0, 1), (2,))

    def h_sems(g, step, kind):
        return (hsend_sem.at[g, step, kind], hrecv_sem.at[g, step, kind])

    def group(g):
        return pl.ds(arrays[g][0], len(arrays[g]))

    def send_low(g):
        remote(
            near.at[group(g), pl.ds(WIDTH, WIDTH)], near.at[group(g), pl.ds(WIDTH + cx, WIDTH)],
            h_sems(g, 0, 0), beside(-1, 0, 0),
        ).start()

    def send_high(g):
        remote(
            near.at[group(g), pl.ds(cx, WIDTH)], near.at[group(g), pl.ds(0, WIDTH)], h_sems(g, 0, 1), beside(1, 0, 0)
        ).start()

    def pack_edges(g, step):
        which, row_out, lane_out = ((own_planes, row_own, lane_own), (ghost_planes, row_ghost, lane_ghost))[step]
        for a in arrays[g]:
            packed = jnp.zeros((cy, cz), F32)
            for q, p in enumerate(which):
                packed = jnp.where(lane // 8 == q, pltpu.roll(near[a, p], WIDTH + 8 * q, 1), packed)
            lane_out[a, 0] = packed[:8]
            lane_out[a, 1] = packed[8:]
            for t in range(len(which) // 2):
                q = 4 * (t // 2) + t % 2
                one, two = near[a, which[q]], near[a, which[q + 2]]
                row_out[a, 0, t] = jnp.where(row8 < WIDTH, one[:8], pltpu.roll(two[:8], 4, 0))
                row_out[a, 1, t] = jnp.where(row8 < WIDTH, pltpu.roll(one[8:], 4, 0), two[8:])

    def send_edges(g, step):
        row_out, lane_out, rows_in, lanes_in, corner_in = (
            (row_own, lane_own, rows_own, lanes_own, corner_own),
            (row_ghost, lane_ghost, rows_ghost, lanes_ghost, corner_ghost),
        )[step]
        some = group(g)
        for side, dm in ((0, -1), (1, 1)):
            remote(row_out.at[some, side], rows_in.at[some, side], h_sems(g, step, 2), beside(0, dm, 0)).start()
        for side, dn in ((0, -1), (1, 1)):
            remote(lane_out.at[some], lanes_in.at[some, side], h_sems(g, step, 3), beside(0, 0, dn)).start()
            for tile, dm in ((0, -1), (1, 1)):
                remote(
                    lane_out.at[some, tile], corner_in.at[some, side, tile], h_sems(g, step, 4), beside(0, dm, dn)
                ).start()

    def take_edges(g, step, places):
        which, rows_in, lanes_in, corner_in = (
            (own_planes, rows_own, lanes_own, corner_own), (ghost_planes, rows_ghost, lanes_ghost, corner_ghost),
        )[step]
        some = group(g)
        for kind, region in ((2, rows_in), (3, lanes_in), (4, corner_in)):
            wait_recv(region.at[some], h_sems(g, step, kind))
        for a, dst in zip(arrays[g], places):
            sides = []
            for side in range(2):
                corner = jnp.where(row8 < WIDTH, corner_in[a, side, 0], corner_in[a, side, 1])
                sides.append(jnp.concatenate([lanes_in[a, side, 0], lanes_in[a, side, 1], corner], axis=0))
            comb = jnp.where(lane24 % 8 >= WIDTH, sides[0], sides[1])
            for t in range(len(which) // 2):
                q = 4 * (t // 2) + t % 2
                after, before = rows_in[a, 0, t], rows_in[a, 1, t]
                ghosts = (
                    (q, jnp.where(row8 < WIDTH, after, pltpu.roll(before, 4, 0))),
                    (q + 2, jnp.where(row8 < WIDTH, pltpu.roll(after, 4, 0), before)),
                )
                for at, ghost in ghosts:
                    p = which[at]
                    dst[p, 0:cy, 0:cz] = near[a, p]
                    dst[p, cy:24, 0:cz] = ghost
                    dst[p, :, cz:2 * cz] = pltpu.roll(comb, cz - (8 * at + WIDTH), 1)

    def wide_arrived(g):
        wait_recv(near.at[group(g), pl.ds(WIDTH + cx, WIDTH)], h_sems(g, 0, 0))
        wait_recv(near.at[group(g), pl.ds(0, WIDTH)], h_sems(g, 0, 1))
        pack_edges(g, 1)
        send_edges(g, 1)

    def prepare():
        row_at = lax.broadcasted_iota(jnp.int32, (24, 2 * cz), 0)
        row_at = jnp.where(row_at < cy + WIDTH, row_at, row_at - 24) + m * cy
        lane_at = lax.broadcasted_iota(jnp.int32, (24, 2 * cz), 1)
        lane_real = (lane_at < cz + WIDTH) | (lane_at >= 2 * cz - WIDTH)
        lane_at = jnp.where(lane_at < cz + WIDTH, lane_at, lane_at - 2 * cz) + n * cz
        inside = lane_real & (row_at >= 0) & (row_at < n_m * cy) & (lane_at >= 0) & (lane_at < n_n * cz)
        inside = jnp.where(inside, 1.0, 0.0)
        for p in range(planes):
            here = inside
            if p < WIDTH:
                here = jnp.where(w > 0, inside, 0.0)
            elif p >= WIDTH + cx:
                here = jnp.where(w < n_w - 1, inside, 0.0)
            capacity, start = inv[p], ext[0, p]
            base[p] = capacity * start
            inv[p] = here / (capacity + 6.0 * CONDUCT)
            ext[0, p] = jnp.where(here > 0.0, start, 0.0)

    def around(plane):
        rows = pltpu.roll(plane, 1, 0) + pltpu.roll(plane, 23, 0)
        return rows + (pltpu.roll(plane, 1, 1) + pltpu.roll(plane, 2 * cz - 1, 1))

    def plain_sweeps():
        for k in range(SWEEPS):
            now, later = k % 2, (k + 1) % 2
            edge = k + 1
            for p in range(edge, planes - edge):
                total = (ext[now, p - 1] + ext[now, p + 1]) + around(ext[now, p]) + base[p]
                new = total * inv[p]
                if k == SWEEPS - 1:
                    plain[p - WIDTH] = new[:cy, :cz]
                else:
                    ext[later, p] = new

    def edge_sems(it, side):
        return (xsend_sem.at[it, side], xrecv_sem.at[it, side])

    def source_start(it, source):
        srcb[it, 0] = source[:8]
        srcb[it, 1] = source[8:]

        def send(side, parts):
            for src, place_at, count, dm, dn in parts:
                remote(
                    srcb.at[it, pl.ds(src, count)], src_in.at[it, pl.ds(place_at, count)],
                    edge_sems(it, side), beside(0, dm, dn),
                ).start()

        send(0, ((0, 0, 1, -1, 0), (1, 1, 1, 1, 0)))

        @pl.when(n > 0)
        def _():
            send(1, ((0, 2, 2, 0, -1), (0, 4, 1, -1, -1), (1, 5, 1, 1, -1)))

        @pl.when(n < n_n - 1)
        def _():
            send(2, ((0, 6, 2, 0, 1), (0, 8, 1, -1, 1), (1, 9, 1, 1, 1)))

    def source_done(it):
        wait_recv(src_in.at[it, pl.ds(0, 2)], edge_sems(it, 0))

        @pl.when(n < n_n - 1)
        def _():
            wait_recv(src_in.at[it, pl.ds(2, 4)], edge_sems(it, 1))

        @pl.when(n > 0)
        def _():
            wait_recv(src_in.at[it, pl.ds(6, 4)], edge_sems(it, 2))

        def corner(up, down):
            return jnp.where(row8 < WIDTH, src_in[it, up], src_in[it, down])

        def lanes(after, before):
            return jnp.where(lane8 < WIDTH, after, before)

        main = jnp.concatenate([srcb[it, 0], srcb[it, 1], corner(0, 1)], axis=0)
        sides = jnp.concatenate(
            [lanes(src_in[it, 2], src_in[it, 6]), lanes(src_in[it, 3], src_in[it, 7]), lanes(corner(4, 5), corner(8, 9))],
            axis=0,
        )
        return jnp.concatenate([main, sides], axis=1)

    def grown(wide_source, have, p):
        total = jnp.zeros((24, 2 * cz), F32)
        if p == 0:
            total = wide_source
        for q in (p - 1, p + 1):
            if q in have:
                total = total + have[q]
        if p in have:
            total = total + around(have[p])
        return total * inv[WIDTH + p]

    def first_sweeps(wide_source):
        one = {0: wide_source * inv[WIDTH]}
        two = {p: grown(wide_source, one, p) for p in (0, -1, 1)}
        three = {p: grown(wide_source, two, p) for p in (0, -1, 1)}
        wall = grown(wide_source, three, 0)[:cy, :cz]
        return two, three, wall

    def last_sweeps(it, wide_source, two, three):
        three.update({p: grown(wide_source, two, p) for p in (-2, 2)})
        for p in (-3, -2, -1):
            lower[it, p + 3] = grown(wide_source, three, p)[:cy, :cz]
        remote(lower.at[it], lower_in.at[it], (lsend_sem.at[it], lrecv_sem.at[it]), beside(-1, 0, 0)).start()
        return [grown(wide_source, three, p)[:cy, :cz] for p in (1, 2, 3)]

    def lower_arrived(it):
        wait_recv(lower_in.at[it], (lsend_sem.at[it], lrecv_sem.at[it]))

    def apply(v16):
        v = v16.astype(F32)
        linked = jnp.dot(v16, col_hot[...], preferred_element_type=F32)
        near0, near1 = linked[:, :128], linked[:, 128:]

        def rows(t, carry):
            sums = []
            for u in range(8):
                i = t * 8 + u
                prod = selfb[i].astype(F32) * v + linkb[0, i].astype(F32) * near0 + linkb[1, i].astype(F32) * near1
                sums.append(jnp.sum(prod, axis=0, keepdims=True))
            kv[pl.ds(pl.multiple_of(t * 8, 8), 8), :] = jnp.concatenate(sums, axis=0)
            return carry

        lax.fori_loop(0, BLOCK // 8, rows, 0)
        return kv[...]

    def newton_start():
        mt, st = melt[...], state[...]
        bulk = BULK_BASE * jnp.exp(-BULK_SLOPE * mt)
        growth = jnp.exp(st)
        press = bulk * (growth - 1.0)
        base_volume = jnp.exp(EXPAND * mt)
        volume = base_volume * (1.0 - TAIT_C * st)
        sl = bulk * growth
        slope[...] = sl
        jd = diag[...] * sl + TAIT_C * base_volume
        jdiag[...] = jd
        rounded = press.astype(BF16)
        res = apply(rounded) + diag[...] * rounded.astype(F32) + (target[...] - volume) - inflow[...]
        resid[...] = res
        upd[...] = -res / jd

    def newton_step():
        weighted = (slope[...] * upd[...]).astype(BF16)
        upd[...] = (-resid[...] - apply(weighted)) / jdiag[...]

    for load in loads[:4]:
        load.wait()
    rel = jnp.bitwise_xor(owner[...], w)
    rel_z = rel // 8
    place = ((rel % 8) * 4 + jnp.bitwise_xor(rel_z, rel_z // 2)) * 16 + slot[...] // 2
    half = slot[...] % 2
    faces = lax.broadcasted_iota(jnp.int32, (512, 128), 0)
    hot32 = jnp.where(faces == place, 1.0, 0.0)
    hot[...] = hot32.astype(BF16)
    scatter_fill(0, scatter_terms((coef[...] * melt[...], coef[...])))
    for it in range(ITERS):
        src_in[it] = jnp.zeros((10, 8, cz), F32)
    loads[4].wait()
    loads[5].wait()
    tab[0, 0, 0] = near[0, WIDTH]
    pack_edges(0, 0)
    pl.semaphore_wait(barrier, len(peers))

    scatter_start(0, 0)
    scatter_start(0, 1)
    send_low(0)
    send_high(0)
    gather_start(0)
    send_edges(0, 0)
    scatter_start(0, 2)
    hot_t[...] = hot32.T.astype(BF16)
    for load in loads[6:]:
        load.wait()
    froms = lax.broadcasted_iota(jnp.int32, (128, 128), 0)
    for k in range(2):
        col_hot[:, k * 128:(k + 1) * 128] = jnp.where(froms == columns[k:k + 1, :], 1.0, 0.0).astype(BF16)

    def pick(t, carry):
        sums = []
        for u in range(8):
            i = t * 8 + u
            mask = lax.broadcasted_iota(jnp.int32, (BLOCK, 128), 0) == i
            block = selfb[i].astype(F32)
            sums.append(jnp.sum(jnp.where(mask, block, 0.0), axis=0, keepdims=True))
            selfb[i] = jnp.where(mask, 0.0, block).astype(BF16)
        diag[pl.ds(pl.multiple_of(t * 8, 8), 8), :] = jnp.concatenate(sums, axis=0)
        return carry

    lax.fori_loop(0, BLOCK // 8, pick, 0)
    scatter_on(0, 0)
    scatter_on(0, 1)
    square = coef[...] * coef[...]
    scatter_fill(1, scatter_terms((square * melt[...], square)))
    gather_on(0, 0)
    wide_arrived(0)
    for part in range(3):
        scatter_start(1, part)
    take_edges(0, 0, (ext.at[0], inv))
    scatter_on(0, 2)

    sum_a, sum_b = scatter_done(0)
    first_wall = near[0, WIDTH]
    source_start(0, sum_a - sum_b * first_wall)
    gather_on(0, 1)
    take_edges(0, 1, (ext.at[0], inv))
    prepare()
    plain_sweeps()
    for part in range(3):
        scatter_on(1, part)
    spread_source = source_done(0)
    two, three, wall_part = first_sweeps(spread_source)
    second_wall = plain[0] + wall_part
    tab[1, 0, 0] = second_wall
    gather_start(1)
    upper = last_sweeps(0, spread_source, two, three)
    near[2, WIDTH] = second_wall
    for p in range(1, 4):
        near[2, WIDTH + p] = plain[p] + upper[p - 1]
    send_low(1)
    for p in range(4, cx - 3):
        near[2, WIDTH + p] = plain[p]

    cool(0)
    newton_start()
    gather_on(1, 0)
    lower_arrived(0)
    for p in range(3):
        near[2, WIDTH + cx - 3 + p] = plain[cx - 3 + p] + lower_in[0, p]
    send_high(1)
    pack_edges(1, 0)
    send_edges(1, 0)
    newton_step()
    sum_c, sum_d = scatter_done(1)
    source_start(1, sum_a - COOLING * sum_c + COOLING * sum_d * first_wall - sum_b * second_wall)
    gather_on(1, 1)
    newton_step()
    state[...] = state[...] + upd[...]
    wide_arrived(1)
    take_edges(1, 0, (ext.at[0],))
    spread_source = source_done(1)
    two, three, wall_part = first_sweeps(spread_source)
    upper = last_sweeps(1, spread_source, two, three)

    cool(1)
    newton_start()
    take_edges(1, 1, (ext.at[0],))
    for p in range(planes):
        ext[0, p] = jnp.where(inv[p] > 0.0, ext[0, p], 0.0)
    plain_sweeps()
    out_field[0] = plain[0] + wall_part
    for p in range(1, 4):
        out_field[p] = plain[p] + upper[p - 1]
    for p in range(4, cx - 3):
        out_field[p] = plain[p]
    newton_step()
    lower_arrived(1)
    for p in range(3):
        out_field[cx - 3 + p] = plain[cx - 3 + p] + lower_in[1, p]
    newton_step()
    mt, st = melt[...], state[...] + upd[...]
    out_press[...] = BULK_BASE * jnp.exp(-BULK_SLOPE * mt) * (jnp.exp(st) - 1.0)
    out_shrink[...] = 1.0 - jnp.exp(EXPAND * mt) * (1.0 - TAIT_C * st)

    def wait_send(region, sems):
        remote(region, region, sems, beside(0, 1, 0)).wait_send()

    for it in range(ITERS):
        for k in range(1, 4):
            wait_send(tab.at[it, 0, k], z_sems(it, k))
            wait_send(psum.at[it, k], sum_sems(it, k))
        for part, (first, count) in enumerate(gather_parts):
            wait_send(tab.at[it, pl.ds(1, 7), pl.ds(first, count)], gather_sems(it, part))
        for part, (first, count) in enumerate(scatter_parts):
            wait_send(spread.at[it, pl.ds(1, 7), pl.ds(first, count)], scatter_sems(it, part))
        wait_send(src_in.at[it, pl.ds(0, 2)], edge_sems(it, 0))

        @pl.when(n > 0)
        def _():
            wait_send(src_in.at[it, pl.ds(2, 4)], edge_sems(it, 1))

        @pl.when(n < n_n - 1)
        def _():
            wait_send(src_in.at[it, pl.ds(6, 4)], edge_sems(it, 2))

        wait_send(lower.at[it], (lsend_sem.at[it], lrecv_sem.at[it]))
    for g in range(2):
        some = group(g)
        wait_send(near.at[some, pl.ds(0, WIDTH)], h_sems(g, 0, 0))
        wait_send(near.at[some, pl.ds(0, WIDTH)], h_sems(g, 0, 1))
        for step, regions in ((0, (rows_own, lanes_own, corner_own)), (1, (rows_ghost, lanes_ghost, corner_ghost))):
            for kind, region in enumerate(regions):
                wait_send(region.at[some], h_sems(g, step, 2 + kind))


def per_device(
    mold_temp, capacity, melt_temp, log_pressure, target_volume, inflow, self_blocks, link_blocks,
    link_columns, wall_owner, wall_slot, transfer_coef,
):
    cx, cy, cz = mold_temp.shape
    cells, blocks = melt_temp.shape
    planes = cx + 2 * WIDTH
    vmem = pl.BlockSpec(memory_space=pltpu.VMEM)
    hbm = pl.BlockSpec(memory_space=pltpu.HBM)

    def scratch(*shape):
        return pltpu.VMEM(shape, F32)

    cav = scratch(cells, blocks)
    return pl.pallas_call(
        kernel,
        out_shape=(
            pltpu.VMEM(mold_temp.shape, F32),
            pltpu.VMEM(melt_temp.shape, F32),
            pltpu.VMEM(melt_temp.shape, F32),
        ),
        in_specs=[hbm] * 12,
        out_specs=(vmem, vmem, vmem),
        scratch_shapes=[
            pltpu.VMEM(self_blocks.shape, BF16),
            pltpu.VMEM(link_blocks.shape, BF16),
            scratch(ITERS, 8, 4, 16, 128),
            scratch(2, 8, 4, 2, 16, 128),
            scratch(2, 8, 4, 2, 16, 128),
            scratch(2, 4, 2, 16, 128),
            scratch(2, 4, 2, 16, 128),
            scratch(3, planes, cy, cz),
            scratch(3, 2, 8, 8, cz),
            scratch(3, 2, 4, 8, cz),
            scratch(3, 2, 8, cz),
            scratch(3, 2, 8, cz),
            scratch(3, 2, 8, 8, cz),
            scratch(3, 2, 4, 8, cz),
            scratch(3, 2, 2, 8, cz),
            scratch(3, 2, 2, 8, cz),
            scratch(3, 2, 2, 8, cz),
            scratch(3, 2, 2, 8, cz),
            scratch(2, planes, 24, 2 * cz),
            scratch(planes, 24, 2 * cz),
            scratch(planes, 24, 2 * cz),
            scratch(cx, cy, cz),
            scratch(ITERS, 2, 8, cz),
            scratch(ITERS, 10, 8, cz),
            scratch(ITERS, 3, cy, cz),
            scratch(ITERS, 3, cy, cz),
            pltpu.VMEM((512, 128), BF16),
            pltpu.VMEM((128, 512), BF16),
            pltpu.VMEM((128, 256), BF16),
            cav, cav, cav, cav, cav, cav, cav, cav, cav, cav, cav,
            pltpu.VMEM((2, blocks), jnp.int32),
            pltpu.VMEM((1, blocks), jnp.int32),
            pltpu.VMEM((1, blocks), jnp.int32),
            pltpu.SemaphoreType.DMA((12,)),
            *[pltpu.SemaphoreType.DMA((ITERS, 4))] * 8,
            *[pltpu.SemaphoreType.DMA((ITERS, 3))] * 2,
            *[pltpu.SemaphoreType.DMA((ITERS,))] * 2,
            *[pltpu.SemaphoreType.DMA((2, 2, 5))] * 2,
        ],
        compiler_params=pltpu.CompilerParams(
            collective_id=0, has_side_effects=True, vmem_limit_bytes=56 * 1024 * 1024
        ),
    )(
        mold_temp, capacity, melt_temp, log_pressure, target_volume, inflow, transfer_coef,
        link_columns, wall_owner.reshape(1, blocks), wall_slot.reshape(1, blocks), self_blocks, link_blocks,
    )


def solution(mesh):
    cavity = P(None, ("wide", "mid", "narrow"))
    brick = P("wide", "mid", "narrow")
    flat = P(("wide", "mid", "narrow"))
    return jax.shard_map(
        per_device,
        mesh=mesh,
        in_specs=(
            brick, brick, cavity, cavity, cavity, cavity,
            P(None, None, ("wide", "mid", "narrow")),
            P(None, None, None, ("wide", "mid", "narrow")),
            cavity, flat, flat, cavity,
        ),
        out_specs=(brick, cavity, cavity),
        check_vma=False,
    )
```

```python
import functools

import jax
import jax.numpy as jnp
from jax import lax
from jax.experimental import pallas as pl
from jax.experimental.pallas import tpu as pltpu
from jax.sharding import PartitionSpec as P

BLOCK = 64
ITERS = 2
SWEEPS = 4
INNER = 2
WIDTH = 4
FAR_FIRST = (2, 1, 3)

CONDUCT = 1.0
COOLING = 0.5
TAIT_C = 0.3
EXPAND = 0.25
BULK_BASE = 0.5
BULK_SLOPE = 0.3

MESH = pl.DeviceIdType.MESH
F32 = jnp.float32
BF16 = jnp.bfloat16


def flip(v, k):
    if k == 0:
        return v
    if k == 1:
        return v + 1 - 2 * (v % 2)
    if k == 2:
        return (v + 2) % 4
    return 3 - v


def split_terms(x):
    hi = x.astype(BF16)
    lo = (x - hi.astype(F32)).astype(BF16)
    return hi, lo


def kernel(
    mold, cap, melt_in, logp, target_in, inflow_in, coef_in, columns_in, owner_in, slot_in, self_in, link_in,
    out_field, out_press, out_shrink,
    selfb, linkb, wide_blocks, tab, spread, rs1, psum, rs2, near,
    row_own, row_ghost, lane_own, lane_ghost, rows_own, rows_ghost, lanes_own, lanes_ghost, corner_own, corner_ghost,
    ext, inv, base, plain, srcb, src_in, lower, lower_in,
    hot, hot_t, col_hot, diag, kv, resid, jdiag, slope, upd, state, melt, target, inflow, coef,
    columns, owner, slot,
    load_sem, zsend_sem, zrecv_sem, gsend_sem, grecv_sem, csend_sem, crecv_sem, ysend_sem, yrecv_sem,
    xsend_sem, xrecv_sem, lsend_sem, lrecv_sem, hsend_sem, hrecv_sem,
):
    cx, cy, cz = mold.shape
    planes = near.shape[1]
    w = lax.axis_index("wide")
    m = lax.axis_index("mid")
    n = lax.axis_index("narrow")
    n_w, n_m, n_n = lax.axis_size("wide"), lax.axis_size("mid"), lax.axis_size("narrow")
    zh, x, c = w // 8, (w // 2) % 4, w % 2

    def z_peer(k):
        return (flip(zh, k) * 8 + x * 2 + c, m, n)

    def xc_peer(j):
        return (zh * 8 + flip(x, j // 2) * 2 + flip(c, j % 2), m, n)

    def beside(dw, dm, dn):
        return ((w + n_w + dw) % n_w, (m + n_m + dm) % n_m, (n + n_n + dn) % n_n)

    barrier = pltpu.get_barrier_semaphore()
    peers = [z_peer(k) for k in range(1, 4)] + [xc_peer(j) for j in range(1, 8)]
    peers += [beside(-1, 0, 0), beside(1, 0, 0)]
    peers += [beside(0, dm, dn) for dm in (-1, 0, 1) for dn in (-1, 0, 1) if (dm, dn) != (0, 0)]
    for peer in peers:
        pl.semaphore_signal(barrier, inc=1, device_id=peer, device_id_type=MESH)

    loads = [
        pltpu.make_async_copy(src, dst, load_sem.at[i])
        for i, (src, dst) in enumerate((
            (owner_in, owner), (slot_in, slot), (coef_in, coef), (melt_in, melt),
            (mold, near.at[0, pl.ds(WIDTH, cx)]), (cap, near.at[1, pl.ds(WIDTH, cx)]), (columns_in, columns),
            (self_in, selfb), (link_in, linkb), (logp, state), (target_in, target), (inflow_in, inflow),
        ))
    ]
    for load in loads:
        load.start()

    def remote(src, dst, sems, peer):
        return pltpu.make_async_remote_copy(
            src_ref=src, dst_ref=dst, send_sem=sems[0], recv_sem=sems[1],
            device_id=peer, device_id_type=MESH,
        )

    def wait_recv(region, sems):
        remote(region, region, sems, beside(0, 1, 0)).wait_recv()

    def z_sems(it, k):
        return (zsend_sem.at[it, k], zrecv_sem.at[it, k])

    def gather_sems(it, k):
        return (gsend_sem.at[it, k], grecv_sem.at[it, k])

    def gather_on(it, k):
        for j in range(1, 8):
            remote(tab.at[it, k, 0], tab.at[it, k, j], gather_sems(it, k), xc_peer(j)).start()

    def gather_start(it):
        for k in FAR_FIRST:
            remote(tab.at[it, 0, 0], tab.at[it, k, 0], z_sems(it, k), z_peer(k)).start()

    def z_arrived(it, k):
        wait_recv(tab.at[it, k, 0], z_sems(it, k))
        gather_on(it, k)

    def cool(it):
        found = jnp.zeros((128, 256), F32)
        for k in (0, 1, 3, 2):
            wait_recv(tab.at[it, k, pl.ds(1, 7)], gather_sems(it, k))
            hi, lo = split_terms(tab[it, k].reshape(128, 128))
            found = found + jnp.dot(
                hot_t[:, k * 128:(k + 1) * 128], jnp.concatenate([hi, lo], axis=1), preferred_element_type=F32
            )
        found = (found[:, :128] + found[:, 128:]).T
        wall = jnp.where(half == 1, found[BLOCK:], found[:BLOCK])
        melt[...] = melt[...] - COOLING * (coef[...] * (melt[...] - wall))

    def scatter_sems(a, k):
        return (csend_sem.at[a, k], crecv_sem.at[a, k])

    def sum_sems(a, k):
        return (ysend_sem.at[a, k], yrecv_sem.at[a, k])

    def scatter_terms(values):
        parts = []
        for value in values:
            placed = jnp.concatenate([jnp.where(half == 0, value, 0.0), jnp.where(half == 1, value, 0.0)], axis=0)
            parts.extend(split_terms(placed))
        return jnp.concatenate(parts, axis=0)

    def scatter_fill(a, terms):
        for k in range(4):
            summed = lax.dot_general(
                hot[k * 128:(k + 1) * 128, :], terms, (((1,), (1,)), ((), ())), preferred_element_type=F32
            )
            for q in range(2):
                one = summed[:, 256 * q:256 * q + 128] + summed[:, 256 * q + 128:256 * q + 256]
                spread[a, k, :, q] = one.reshape(8, 16, 128)

    def scatter_start(a, k):
        for j in range(1, 8):
            remote(spread.at[a, k, j], rs1.at[a, k, j], scatter_sems(a, k), xc_peer(j)).start()

    def scatter_on(a, k):
        wait_recv(rs1.at[a, k, pl.ds(1, 7)], scatter_sems(a, k))
        for q in range(2):
            total = spread[a, k, 0, q]
            for j in range(1, 8):
                total = total + rs1[a, k, j, q]
            psum[a, k, q] = total
        if k > 0:
            remote(psum.at[a, k], rs2.at[a, k], sum_sems(a, k), z_peer(k)).start()

    def scatter_done(a):
        for k in (1, 3, 2):
            wait_recv(rs2.at[a, k], sum_sems(a, k))
        return [((psum[a, 0, q] + rs2[a, 1, q]) + (rs2[a, 3, q] + rs2[a, 2, q])) for q in range(2)]

    lane = lax.broadcasted_iota(jnp.int32, (cy, cz), 1)
    lane24 = lax.broadcasted_iota(jnp.int32, (24, cz), 1)
    row8 = lax.broadcasted_iota(jnp.int32, (8, cz), 0)
    lane8 = lax.broadcasted_iota(jnp.int32, (8, cz), 1)
    own_planes = list(range(WIDTH, WIDTH + cx))
    ghost_planes = list(range(WIDTH)) + list(range(WIDTH + cx, planes))
    arrays = ((0, 1), (2,))

    def h_sems(g, step, kind):
        return (hsend_sem.at[g, step, kind], hrecv_sem.at[g, step, kind])

    def group(g):
        return pl.ds(arrays[g][0], len(arrays[g]))

    def send_low(g):
        remote(
            near.at[group(g), pl.ds(WIDTH, WIDTH)], near.at[group(g), pl.ds(WIDTH + cx, WIDTH)],
            h_sems(g, 0, 0), beside(-1, 0, 0),
        ).start()

    def send_high(g):
        remote(
            near.at[group(g), pl.ds(cx, WIDTH)], near.at[group(g), pl.ds(0, WIDTH)], h_sems(g, 0, 1), beside(1, 0, 0)
        ).start()

    def pack_edges(g, step):
        which, row_out, lane_out = ((own_planes, row_own, lane_own), (ghost_planes, row_ghost, lane_ghost))[step]
        for a in arrays[g]:
            packed = jnp.zeros((cy, cz), F32)
            for q, p in enumerate(which):
                packed = jnp.where(lane // 8 == q, pltpu.roll(near[a, p], WIDTH + 8 * q, 1), packed)
            lane_out[a, 0] = packed[:8]
            lane_out[a, 1] = packed[8:]
            for t in range(len(which) // 2):
                q = 4 * (t // 2) + t % 2
                one, two = near[a, which[q]], near[a, which[q + 2]]
                row_out[a, 0, t] = jnp.where(row8 < WIDTH, one[:8], pltpu.roll(two[:8], 4, 0))
                row_out[a, 1, t] = jnp.where(row8 < WIDTH, pltpu.roll(one[8:], 4, 0), two[8:])

    def send_edges(g, step):
        row_out, lane_out, rows_in, lanes_in, corner_in = (
            (row_own, lane_own, rows_own, lanes_own, corner_own),
            (row_ghost, lane_ghost, rows_ghost, lanes_ghost, corner_ghost),
        )[step]
        some = group(g)
        for side, dm in ((0, -1), (1, 1)):
            remote(row_out.at[some, side], rows_in.at[some, side], h_sems(g, step, 2), beside(0, dm, 0)).start()
        for side, dn in ((0, -1), (1, 1)):
            remote(lane_out.at[some], lanes_in.at[some, side], h_sems(g, step, 3), beside(0, 0, dn)).start()
            for tile, dm in ((0, -1), (1, 1)):
                remote(
                    lane_out.at[some, tile], corner_in.at[some, side, tile], h_sems(g, step, 4), beside(0, dm, dn)
                ).start()

    def take_edges(g, step, places):
        which, rows_in, lanes_in, corner_in = (
            (own_planes, rows_own, lanes_own, corner_own), (ghost_planes, rows_ghost, lanes_ghost, corner_ghost),
        )[step]
        some = group(g)
        for kind, region in ((2, rows_in), (3, lanes_in), (4, corner_in)):
            wait_recv(region.at[some], h_sems(g, step, kind))
        for a, dst in zip(arrays[g], places):
            sides = []
            for side in range(2):
                corner = jnp.where(row8 < WIDTH, corner_in[a, side, 0], corner_in[a, side, 1])
                sides.append(jnp.concatenate([lanes_in[a, side, 0], lanes_in[a, side, 1], corner], axis=0))
            comb = jnp.where(lane24 % 8 >= WIDTH, sides[0], sides[1])
            for t in range(len(which) // 2):
                q = 4 * (t // 2) + t % 2
                after, before = rows_in[a, 0, t], rows_in[a, 1, t]
                ghosts = (
                    (q, jnp.where(row8 < WIDTH, after, pltpu.roll(before, 4, 0))),
                    (q + 2, jnp.where(row8 < WIDTH, pltpu.roll(after, 4, 0), before)),
                )
                for at, ghost in ghosts:
                    p = which[at]
                    dst[p, 0:cy, 0:cz] = near[a, p]
                    dst[p, cy:24, 0:cz] = ghost
                    dst[p, :, cz:2 * cz] = pltpu.roll(comb, cz - (8 * at + WIDTH), 1)

    def wide_arrived(g):
        wait_recv(near.at[group(g), pl.ds(WIDTH + cx, WIDTH)], h_sems(g, 0, 0))
        wait_recv(near.at[group(g), pl.ds(0, WIDTH)], h_sems(g, 0, 1))
        pack_edges(g, 1)
        send_edges(g, 1)

    def prepare(which):
        row_at = lax.broadcasted_iota(jnp.int32, (24, 2 * cz), 0)
        row_at = jnp.where(row_at < cy + WIDTH, row_at, row_at - 24) + m * cy
        lane_at = lax.broadcasted_iota(jnp.int32, (24, 2 * cz), 1)
        lane_real = (lane_at < cz + WIDTH) | (lane_at >= 2 * cz - WIDTH)
        lane_at = jnp.where(lane_at < cz + WIDTH, lane_at, lane_at - 2 * cz) + n * cz
        inside = lane_real & (row_at >= 0) & (row_at < n_m * cy) & (lane_at >= 0) & (lane_at < n_n * cz)
        inside = jnp.where(inside, 1.0, 0.0)
        for p in which:
            here = inside
            if p < WIDTH:
                here = jnp.where(w > 0, inside, 0.0)
            elif p >= WIDTH + cx:
                here = jnp.where(w < n_w - 1, inside, 0.0)
            capacity, start = inv[p], ext[0, p]
            base[p] = capacity * start
            inv[p] = here / (capacity + 6.0 * CONDUCT)
            ext[0, p] = jnp.where(here > 0.0, start, 0.0)

    def keep_inside(which):
        for p in which:
            ext[0, p] = jnp.where(inv[p] > 0.0, ext[0, p], 0.0)

    def around(plane):
        rows = pltpu.roll(plane, 1, 0) + pltpu.roll(plane, 23, 0)
        return rows + (pltpu.roll(plane, 1, 1) + pltpu.roll(plane, 2 * cz - 1, 1))

    def plain_sweeps(inner):
        for k in range(SWEEPS):
            now, later = k % 2, (k + 1) % 2
            edge = k + 1
            inside = range(edge + WIDTH, planes - edge - WIDTH)
            for p in inside if inner else [p for p in range(edge, planes - edge) if p not in inside]:
                total = (ext[now, p - 1] + ext[now, p + 1]) + around(ext[now, p]) + base[p]
                new = total * inv[p]
                if k == SWEEPS - 1:
                    plain[p - WIDTH] = new[:cy, :cz]
                else:
                    ext[later, p] = new

    def edge_sems(it, side):
        return (xsend_sem.at[it, side], xrecv_sem.at[it, side])

    def source_start(it, source):
        srcb[it, 0] = source[:8]
        srcb[it, 1] = source[8:]

        def send(side, parts):
            for src, place_at, count, dm, dn in parts:
                remote(
                    srcb.at[it, pl.ds(src, count)], src_in.at[it, pl.ds(place_at, count)],
                    edge_sems(it, side), beside(0, dm, dn),
                ).start()

        send(0, ((0, 0, 1, -1, 0), (1, 1, 1, 1, 0)))

        @pl.when(n > 0)
        def _():
            send(1, ((0, 2, 2, 0, -1), (0, 4, 1, -1, -1), (1, 5, 1, 1, -1)))

        @pl.when(n < n_n - 1)
        def _():
            send(2, ((0, 6, 2, 0, 1), (0, 8, 1, -1, 1), (1, 9, 1, 1, 1)))

    def source_done(it):
        wait_recv(src_in.at[it, pl.ds(0, 2)], edge_sems(it, 0))

        @pl.when(n < n_n - 1)
        def _():
            wait_recv(src_in.at[it, pl.ds(2, 4)], edge_sems(it, 1))

        @pl.when(n > 0)
        def _():
            wait_recv(src_in.at[it, pl.ds(6, 4)], edge_sems(it, 2))

        def corner(up, down):
            return jnp.where(row8 < WIDTH, src_in[it, up], src_in[it, down])

        def lanes(after, before):
            return jnp.where(lane8 < WIDTH, after, before)

        main = jnp.concatenate([srcb[it, 0], srcb[it, 1], corner(0, 1)], axis=0)
        sides = jnp.concatenate(
            [lanes(src_in[it, 2], src_in[it, 6]), lanes(src_in[it, 3], src_in[it, 7]), lanes(corner(4, 5), corner(8, 9))],
            axis=0,
        )
        return jnp.concatenate([main, sides], axis=1)

    def grown(wide_source, have, p):
        total = jnp.zeros((24, 2 * cz), F32)
        if p == 0:
            total = wide_source
        for q in (p - 1, p + 1):
            if q in have:
                total = total + have[q]
        if p in have:
            total = total + around(have[p])
        return total * inv[WIDTH + p]

    def first_sweeps(wide_source):
        one = {0: wide_source * inv[WIDTH]}
        two = {p: grown(wide_source, one, p) for p in (0, -1, 1)}
        three = {p: grown(wide_source, two, p) for p in (0, -1, 1)}
        wall = grown(wide_source, three, 0)[:cy, :cz]
        return two, three, wall

    def last_sweeps(it, wide_source, two, three):
        three.update({p: grown(wide_source, two, p) for p in (-2, 2)})
        for p in (-3, -2, -1):
            lower[it, p + 3] = grown(wide_source, three, p)[:cy, :cz]
        remote(lower.at[it], lower_in.at[it], (lsend_sem.at[it], lrecv_sem.at[it]), beside(-1, 0, 0)).start()
        return [grown(wide_source, three, p)[:cy, :cz] for p in (1, 2, 3)]

    def lower_arrived(it):
        wait_recv(lower_in.at[it], (lsend_sem.at[it], lrecv_sem.at[it]))

    def apply(v16):
        v = v16.astype(F32)
        linked = jnp.dot(v16, col_hot[...], preferred_element_type=F32)
        near0, near1 = linked[:, :128], linked[:, 128:]

        def rows(t, carry):
            sums = []
            for u in range(8):
                i = t * 8 + u
                prod = wide_blocks[0, i] * v + wide_blocks[1, i] * near0 + wide_blocks[2, i] * near1
                sums.append(jnp.sum(prod, axis=0, keepdims=True))
            kv[pl.ds(pl.multiple_of(t * 8, 8), 8), :] = jnp.concatenate(sums, axis=0)
            return carry

        lax.fori_loop(0, BLOCK // 8, rows, 0)
        return kv[...]

    def newton_start():
        mt, st = melt[...], state[...]
        bulk = BULK_BASE * jnp.exp(-BULK_SLOPE * mt)
        growth = jnp.exp(st)
        press = bulk * (growth - 1.0)
        base_volume = jnp.exp(EXPAND * mt)
        volume = base_volume * (1.0 - TAIT_C * st)
        sl = bulk * growth
        slope[...] = sl
        jd = diag[...] * sl + TAIT_C * base_volume
        jdiag[...] = jd
        rounded = press.astype(BF16)
        res = apply(rounded) + diag[...] * rounded.astype(F32) + (target[...] - volume) - inflow[...]
        resid[...] = res
        upd[...] = -res / jd

    def newton_step():
        weighted = (slope[...] * upd[...]).astype(BF16)
        upd[...] = (-resid[...] - apply(weighted)) / jdiag[...]

    for load in loads[:4]:
        load.wait()
    rel = jnp.bitwise_xor(owner[...], w)
    place = rel * 16 + slot[...] // 2
    half = slot[...] % 2
    faces = lax.broadcasted_iota(jnp.int32, (512, 128), 0)
    hot32 = jnp.where(faces == place, 1.0, 0.0)
    hot[...] = hot32.astype(BF16)
    scatter_fill(0, scatter_terms((coef[...] * melt[...], coef[...])))
    for it in range(ITERS):
        src_in[it] = jnp.zeros((10, 8, cz), F32)
    loads[4].wait()
    loads[5].wait()
    tab[0, 0, 0] = near[0, WIDTH]
    pack_edges(0, 0)
    pl.semaphore_wait(barrier, len(peers))

    for k in FAR_FIRST:
        scatter_start(0, k)
    send_low(0)
    send_high(0)
    gather_start(0)
    send_edges(0, 0)
    scatter_start(0, 0)
    gather_on(0, 0)
    hot_t[...] = hot32.T.astype(BF16)
    for load in loads[6:]:
        load.wait()
    froms = lax.broadcasted_iota(jnp.int32, (128, 128), 0)
    for k in range(2):
        col_hot[:, k * 128:(k + 1) * 128] = jnp.where(froms == columns[k:k + 1, :], 1.0, 0.0).astype(BF16)

    def pick(t, carry):
        sums = []
        for u in range(8):
            i = t * 8 + u
            mask = lax.broadcasted_iota(jnp.int32, (BLOCK, 128), 0) == i
            block = selfb[i].astype(F32)
            sums.append(jnp.sum(jnp.where(mask, block, 0.0), axis=0, keepdims=True))
            wide_blocks[0, i] = jnp.where(mask, 0.0, block)
            wide_blocks[1, i] = linkb[0, i].astype(F32)
            wide_blocks[2, i] = linkb[1, i].astype(F32)
        diag[pl.ds(pl.multiple_of(t * 8, 8), 8), :] = jnp.concatenate(sums, axis=0)
        return carry

    lax.fori_loop(0, BLOCK // 8, pick, 0)
    for k in FAR_FIRST:
        scatter_on(0, k)
    square = coef[...] * coef[...]
    scatter_fill(1, scatter_terms((square * melt[...], square)))
    z_arrived(0, 1)
    z_arrived(0, 3)
    wide_arrived(0)
    for k in FAR_FIRST + (0,):
        scatter_start(1, k)
    take_edges(0, 0, (ext.at[0], inv))
    prepare(own_planes)
    scatter_on(0, 0)
    plain_sweeps(True)

    sum_a, sum_b = scatter_done(0)
    first_wall = near[0, WIDTH]
    source_start(0, sum_a - sum_b * first_wall)
    z_arrived(0, 2)
    take_edges(0, 1, (ext.at[0], inv))
    prepare(ghost_planes)
    plain_sweeps(False)
    for k in FAR_FIRST + (0,):
        scatter_on(1, k)
    spread_source = source_done(0)
    two, three, wall_part = first_sweeps(spread_source)
    second_wall = plain[0] + wall_part
    tab[1, 0, 0] = second_wall
    gather_start(1)
    gather_on(1, 0)
    upper = last_sweeps(0, spread_source, two, three)
    near[2, WIDTH] = second_wall
    for p in range(1, 4):
        near[2, WIDTH + p] = plain[p] + upper[p - 1]
    send_low(1)
    for p in range(4, cx - 3):
        near[2, WIDTH + p] = plain[p]

    cool(0)
    newton_start()
    z_arrived(1, 1)
    z_arrived(1, 3)
    lower_arrived(0)
    for p in range(3):
        near[2, WIDTH + cx - 3 + p] = plain[cx - 3 + p] + lower_in[0, p]
    send_high(1)
    pack_edges(1, 0)
    send_edges(1, 0)
    newton_step()
    sum_c, sum_d = scatter_done(1)
    source_start(1, sum_a - COOLING * sum_c + COOLING * sum_d * first_wall - sum_b * second_wall)
    z_arrived(1, 2)
    newton_step()
    state[...] = state[...] + upd[...]
    wide_arrived(1)
    take_edges(1, 0, (ext.at[0],))
    keep_inside(own_planes)
    plain_sweeps(True)
    spread_source = source_done(1)
    two, three, wall_part = first_sweeps(spread_source)
    upper = last_sweeps(1, spread_source, two, three)

    cool(1)
    newton_start()
    newton_step()
    take_edges(1, 1, (ext.at[0],))
    keep_inside(ghost_planes)
    plain_sweeps(False)
    out_field[0] = plain[0] + wall_part
    for p in range(1, 4):
        out_field[p] = plain[p] + upper[p - 1]
    for p in range(4, cx - 3):
        out_field[p] = plain[p]
    lower_arrived(1)
    for p in range(3):
        out_field[cx - 3 + p] = plain[cx - 3 + p] + lower_in[1, p]
    newton_step()
    mt, st = melt[...], state[...] + upd[...]
    out_press[...] = BULK_BASE * jnp.exp(-BULK_SLOPE * mt) * (jnp.exp(st) - 1.0)
    out_shrink[...] = 1.0 - jnp.exp(EXPAND * mt) * (1.0 - TAIT_C * st)

    def wait_send(region, sems):
        remote(region, region, sems, beside(0, 1, 0)).wait_send()

    for it in range(ITERS):
        for k in range(4):
            if k > 0:
                wait_send(tab.at[it, k, 0], z_sems(it, k))
                wait_send(psum.at[it, k], sum_sems(it, k))
            wait_send(tab.at[it, k, pl.ds(1, 7)], gather_sems(it, k))
            wait_send(spread.at[it, k, pl.ds(1, 7)], scatter_sems(it, k))
        wait_send(src_in.at[it, pl.ds(0, 2)], edge_sems(it, 0))

        @pl.when(n > 0)
        def _():
            wait_send(src_in.at[it, pl.ds(2, 4)], edge_sems(it, 1))

        @pl.when(n < n_n - 1)
        def _():
            wait_send(src_in.at[it, pl.ds(6, 4)], edge_sems(it, 2))

        wait_send(lower.at[it], (lsend_sem.at[it], lrecv_sem.at[it]))
    for g in range(2):
        some = group(g)
        wait_send(near.at[some, pl.ds(0, WIDTH)], h_sems(g, 0, 0))
        wait_send(near.at[some, pl.ds(0, WIDTH)], h_sems(g, 0, 1))
        for step, regions in ((0, (rows_own, lanes_own, corner_own)), (1, (rows_ghost, lanes_ghost, corner_ghost))):
            for kind, region in enumerate(regions):
                wait_send(region.at[some], h_sems(g, step, 2 + kind))


def per_device(
    mold_temp, capacity, melt_temp, log_pressure, target_volume, inflow, self_blocks, link_blocks,
    link_columns, wall_owner, wall_slot, transfer_coef,
):
    cx, cy, cz = mold_temp.shape
    cells, blocks = melt_temp.shape
    planes = cx + 2 * WIDTH
    vmem = pl.BlockSpec(memory_space=pltpu.VMEM)
    hbm = pl.BlockSpec(memory_space=pltpu.HBM)

    def scratch(*shape):
        return pltpu.VMEM(shape, F32)

    cav = scratch(cells, blocks)
    return pl.pallas_call(
        kernel,
        out_shape=(
            pltpu.VMEM(mold_temp.shape, F32),
            pltpu.VMEM(melt_temp.shape, F32),
            pltpu.VMEM(melt_temp.shape, F32),
        ),
        in_specs=[hbm] * 12,
        out_specs=(vmem, vmem, vmem),
        scratch_shapes=[
            pltpu.VMEM(self_blocks.shape, BF16),
            pltpu.VMEM(link_blocks.shape, BF16),
            scratch(3, *self_blocks.shape),
            scratch(ITERS, 4, 8, 16, 128),
            scratch(2, 4, 8, 2, 16, 128),
            scratch(2, 4, 8, 2, 16, 128),
            scratch(2, 4, 2, 16, 128),
            scratch(2, 4, 2, 16, 128),
            scratch(3, planes, cy, cz),
            scratch(3, 2, 8, 8, cz),
            scratch(3, 2, 4, 8, cz),
            scratch(3, 2, 8, cz),
            scratch(3, 2, 8, cz),
            scratch(3, 2, 8, 8, cz),
            scratch(3, 2, 4, 8, cz),
            scratch(3, 2, 2, 8, cz),
            scratch(3, 2, 2, 8, cz),
            scratch(3, 2, 2, 8, cz),
            scratch(3, 2, 2, 8, cz),
            scratch(2, planes, 24, 2 * cz),
            scratch(planes, 24, 2 * cz),
            scratch(planes, 24, 2 * cz),
            scratch(cx, cy, cz),
            scratch(ITERS, 2, 8, cz),
            scratch(ITERS, 10, 8, cz),
            scratch(ITERS, 3, cy, cz),
            scratch(ITERS, 3, cy, cz),
            pltpu.VMEM((512, 128), BF16),
            pltpu.VMEM((128, 512), BF16),
            pltpu.VMEM((128, 256), BF16),
            cav, cav, cav, cav, cav, cav, cav, cav, cav, cav, cav,
            pltpu.VMEM((2, blocks), jnp.int32),
            pltpu.VMEM((1, blocks), jnp.int32),
            pltpu.VMEM((1, blocks), jnp.int32),
            pltpu.SemaphoreType.DMA((12,)),
            *[pltpu.SemaphoreType.DMA((ITERS, 4))] * 8,
            *[pltpu.SemaphoreType.DMA((ITERS, 3))] * 2,
            *[pltpu.SemaphoreType.DMA((ITERS,))] * 2,
            *[pltpu.SemaphoreType.DMA((2, 2, 5))] * 2,
        ],
        compiler_params=pltpu.CompilerParams(
            collective_id=0, has_side_effects=True, vmem_limit_bytes=56 * 1024 * 1024
        ),
    )(
        mold_temp, capacity, melt_temp, log_pressure, target_volume, inflow, transfer_coef,
        link_columns, wall_owner.reshape(1, blocks), wall_slot.reshape(1, blocks), self_blocks, link_blocks,
    )


def solution(mesh):
    cavity = P(None, ("wide", "mid", "narrow"))
    brick = P("wide", "mid", "narrow")
    flat = P(("wide", "mid", "narrow"))
    return jax.shard_map(
        per_device,
        mesh=mesh,
        in_specs=(
            brick, brick, cavity, cavity, cavity, cavity,
            P(None, None, ("wide", "mid", "narrow")),
            P(None, None, None, ("wide", "mid", "narrow")),
            cavity, flat, flat, cavity,
        ),
        out_specs=(brick, cavity, cavity),
        check_vma=False,
    )
```

```python
import functools

import jax
import jax.numpy as jnp
from jax import lax
from jax.experimental import pallas as pl
from jax.experimental.pallas import tpu as pltpu
from jax.sharding import PartitionSpec as P

BLOCK = 64
ITERS = 2
SWEEPS = 4
INNER = 2
WIDTH = 4
FAR_FIRST = (2, 1, 3)

CONDUCT = 1.0
COOLING = 0.5
TAIT_C = 0.3
EXPAND = 0.25
BULK_BASE = 0.5
BULK_SLOPE = 0.3

MESH = pl.DeviceIdType.MESH
F32 = jnp.float32
BF16 = jnp.bfloat16


def flip(v, k):
    if k == 0:
        return v
    if k == 1:
        return v + 1 - 2 * (v % 2)
    if k == 2:
        return (v + 2) % 4
    return 3 - v


def split_terms(x):
    hi = x.astype(BF16)
    lo = (x - hi.astype(F32)).astype(BF16)
    return hi, lo


def kernel(
    mold, cap, melt_in, logp, target_in, inflow_in, coef_in, columns_in, owner_in, slot_in, self_in, link_in,
    out_field, out_press, out_shrink,
    selfb, linkb, wide_blocks, tab, spread, rs1, psum, rs2, near,
    row_own, row_ghost, lane_own, lane_ghost, rows_own, rows_ghost, lanes_own, lanes_ghost, corner_own, corner_ghost,
    ext, inv, base, plain, srcb, src_in, lower, lower_in,
    hot, hot_t, col_hot, diag, kv, resid, jdiag, slope, upd, state, melt, target, inflow, coef,
    columns, owner, slot,
    load_sem, zsend_sem, zrecv_sem, gsend_sem, grecv_sem, csend_sem, crecv_sem, ysend_sem, yrecv_sem,
    xsend_sem, xrecv_sem, lsend_sem, lrecv_sem, hsend_sem, hrecv_sem,
):
    cx, cy, cz = mold.shape
    planes = near.shape[1]
    w = lax.axis_index("wide")
    m = lax.axis_index("mid")
    n = lax.axis_index("narrow")
    n_w, n_m, n_n = lax.axis_size("wide"), lax.axis_size("mid"), lax.axis_size("narrow")
    zh, x, c = w // 8, (w // 2) % 4, w % 2

    def z_peer(k):
        return (flip(zh, k) * 8 + x * 2 + c, m, n)

    def xc_peer(j):
        return (zh * 8 + flip(x, j // 2) * 2 + flip(c, j % 2), m, n)

    def beside(dw, dm, dn):
        return ((w + n_w + dw) % n_w, (m + n_m + dm) % n_m, (n + n_n + dn) % n_n)

    barrier = pltpu.get_barrier_semaphore()
    peers = [z_peer(k) for k in range(1, 4)] + [xc_peer(j) for j in range(1, 8)]
    peers += [beside(-1, 0, 0), beside(1, 0, 0)]
    peers += [beside(0, dm, dn) for dm in (-1, 0, 1) for dn in (-1, 0, 1) if (dm, dn) != (0, 0)]
    for peer in peers:
        pl.semaphore_signal(barrier, inc=1, device_id=peer, device_id_type=MESH)

    loads = [
        pltpu.make_async_copy(src, dst, load_sem.at[i])
        for i, (src, dst) in enumerate((
            (owner_in, owner), (slot_in, slot), (coef_in, coef), (melt_in, melt),
            (mold, near.at[0, pl.ds(WIDTH, cx)]), (cap, near.at[1, pl.ds(WIDTH, cx)]), (columns_in, columns),
            (self_in, selfb), (link_in, linkb), (logp, state), (target_in, target), (inflow_in, inflow),
        ))
    ]
    for load in loads:
        load.start()

    def remote(src, dst, sems, peer):
        return pltpu.make_async_remote_copy(
            src_ref=src, dst_ref=dst, send_sem=sems[0], recv_sem=sems[1],
            device_id=peer, device_id_type=MESH,
        )

    def wait_recv(region, sems):
        remote(region, region, sems, beside(0, 1, 0)).wait_recv()

    def z_sems(it, k):
        return (zsend_sem.at[it, k], zrecv_sem.at[it, k])

    def gather_sems(it, k):
        return (gsend_sem.at[it, k], grecv_sem.at[it, k])

    def gather_on(it, k):
        for j in range(1, 8):
            remote(tab.at[it, k, 0], tab.at[it, k, j], gather_sems(it, k), xc_peer(j)).start()

    def gather_start(it):
        for k in FAR_FIRST:
            remote(tab.at[it, 0, 0], tab.at[it, k, 0], z_sems(it, k), z_peer(k)).start()

    def z_arrived(it, k):
        wait_recv(tab.at[it, k, 0], z_sems(it, k))
        gather_on(it, k)

    def cool(it):
        found = jnp.zeros((128, 256), F32)
        for k in (0, 1, 3, 2):
            wait_recv(tab.at[it, k, pl.ds(1, 7)], gather_sems(it, k))
            hi, lo = split_terms(tab[it, k].reshape(128, 128))
            found = found + jnp.dot(
                hot_t[:, k * 128:(k + 1) * 128], jnp.concatenate([hi, lo], axis=1), preferred_element_type=F32
            )
        found = (found[:, :128] + found[:, 128:]).T
        wall = jnp.where(half == 1, found[BLOCK:], found[:BLOCK])
        melt[...] = melt[...] - COOLING * (coef[...] * (melt[...] - wall))

    def scatter_sems(a, k):
        return (csend_sem.at[a, k], crecv_sem.at[a, k])

    def sum_sems(a, k):
        return (ysend_sem.at[a, k], yrecv_sem.at[a, k])

    def scatter_terms(values):
        parts = []
        for value in values:
            placed = jnp.concatenate([jnp.where(half == 0, value, 0.0), jnp.where(half == 1, value, 0.0)], axis=0)
            parts.extend(split_terms(placed))
        return jnp.concatenate(parts, axis=0)

    def scatter_fill(a, terms):
        for k in range(4):
            summed = lax.dot_general(
                hot[k * 128:(k + 1) * 128, :], terms, (((1,), (1,)), ((), ())), preferred_element_type=F32
            )
            for q in range(2):
                one = summed[:, 256 * q:256 * q + 128] + summed[:, 256 * q + 128:256 * q + 256]
                spread[a, k, :, q] = one.reshape(8, 16, 128)

    def scatter_start(a, k):
        for j in range(1, 8):
            remote(spread.at[a, k, j], rs1.at[a, k, j], scatter_sems(a, k), xc_peer(j)).start()

    def scatter_on(a, k):
        wait_recv(rs1.at[a, k, pl.ds(1, 7)], scatter_sems(a, k))
        for q in range(2):
            total = spread[a, k, 0, q]
            for j in range(1, 8):
                total = total + rs1[a, k, j, q]
            psum[a, k, q] = total
        if k > 0:
            remote(psum.at[a, k], rs2.at[a, k], sum_sems(a, k), z_peer(k)).start()

    def scatter_done(a):
        for k in (1, 3, 2):
            wait_recv(rs2.at[a, k], sum_sems(a, k))
        return [((psum[a, 0, q] + rs2[a, 1, q]) + (rs2[a, 3, q] + rs2[a, 2, q])) for q in range(2)]

    lane = lax.broadcasted_iota(jnp.int32, (cy, cz), 1)
    lane24 = lax.broadcasted_iota(jnp.int32, (24, cz), 1)
    row8 = lax.broadcasted_iota(jnp.int32, (8, cz), 0)
    lane8 = lax.broadcasted_iota(jnp.int32, (8, cz), 1)
    own_planes = list(range(WIDTH, WIDTH + cx))
    ghost_planes = list(range(WIDTH)) + list(range(WIDTH + cx, planes))
    arrays = ((0, 1), (2,))

    def h_sems(g, step, kind):
        return (hsend_sem.at[g, step, kind], hrecv_sem.at[g, step, kind])

    def group(g):
        return pl.ds(arrays[g][0], len(arrays[g]))

    def send_low(g):
        remote(
            near.at[group(g), pl.ds(WIDTH, WIDTH)], near.at[group(g), pl.ds(WIDTH + cx, WIDTH)],
            h_sems(g, 0, 0), beside(-1, 0, 0),
        ).start()

    def send_high(g):
        src = near.at[group(0), pl.ds(cx, WIDTH)] if g == 0 else plain.at[pl.ds(0, 1), pl.ds(cx - WIDTH, WIDTH)]
        remote(src, near.at[group(g), pl.ds(0, WIDTH)], h_sems(g, 0, 1), beside(1, 0, 0)).start()

    def pack_edges(g, step):
        which, row_out, lane_out = ((own_planes, row_own, lane_own), (ghost_planes, row_ghost, lane_ghost))[step]
        for a in arrays[g]:
            packed = jnp.zeros((cy, cz), F32)
            for q, p in enumerate(which):
                packed = jnp.where(lane // 8 == q, pltpu.roll(near[a, p], WIDTH + 8 * q, 1), packed)
            lane_out[a, 0] = packed[:8]
            lane_out[a, 1] = packed[8:]
            for t in range(len(which) // 2):
                q = 4 * (t // 2) + t % 2
                one, two = near[a, which[q]], near[a, which[q + 2]]
                row_out[a, 0, t] = jnp.where(row8 < WIDTH, one[:8], pltpu.roll(two[:8], 4, 0))
                row_out[a, 1, t] = jnp.where(row8 < WIDTH, pltpu.roll(one[8:], 4, 0), two[8:])

    def send_edges(g, step):
        row_out, lane_out, rows_in, lanes_in, corner_in = (
            (row_own, lane_own, rows_own, lanes_own, corner_own),
            (row_ghost, lane_ghost, rows_ghost, lanes_ghost, corner_ghost),
        )[step]
        some = group(g)
        for side, dm in ((0, -1), (1, 1)):
            remote(row_out.at[some, side], rows_in.at[some, side], h_sems(g, step, 2), beside(0, dm, 0)).start()
        for side, dn in ((0, -1), (1, 1)):
            remote(lane_out.at[some], lanes_in.at[some, side], h_sems(g, step, 3), beside(0, 0, dn)).start()
            for tile, dm in ((0, -1), (1, 1)):
                remote(
                    lane_out.at[some, tile], corner_in.at[some, side, tile], h_sems(g, step, 4), beside(0, dm, dn)
                ).start()

    def take_edges(g, step, places):
        which, rows_in, lanes_in, corner_in = (
            (own_planes, rows_own, lanes_own, corner_own), (ghost_planes, rows_ghost, lanes_ghost, corner_ghost),
        )[step]
        some = group(g)
        for kind, region in ((2, rows_in), (3, lanes_in), (4, corner_in)):
            wait_recv(region.at[some], h_sems(g, step, kind))
        for a, dst in zip(arrays[g], places):
            sides = []
            for side in range(2):
                corner = jnp.where(row8 < WIDTH, corner_in[a, side, 0], corner_in[a, side, 1])
                sides.append(jnp.concatenate([lanes_in[a, side, 0], lanes_in[a, side, 1], corner], axis=0))
            comb = jnp.where(lane24 % 8 >= WIDTH, sides[0], sides[1])
            for t in range(len(which) // 2):
                q = 4 * (t // 2) + t % 2
                after, before = rows_in[a, 0, t], rows_in[a, 1, t]
                ghosts = (
                    (q, jnp.where(row8 < WIDTH, after, pltpu.roll(before, 4, 0))),
                    (q + 2, jnp.where(row8 < WIDTH, pltpu.roll(after, 4, 0), before)),
                )
                for at, ghost in ghosts:
                    p = which[at]
                    dst[p, 0:cy, 0:cz] = near[a, p]
                    dst[p, cy:24, 0:cz] = ghost
                    dst[p, :, cz:2 * cz] = pltpu.roll(comb, cz - (8 * at + WIDTH), 1)

    def wide_arrived(g):
        wait_recv(near.at[group(g), pl.ds(WIDTH + cx, WIDTH)], h_sems(g, 0, 0))
        wait_recv(near.at[group(g), pl.ds(0, WIDTH)], h_sems(g, 0, 1))
        if g == 1:
            for p in range(3):
                near[2, p + 1] = near[2, p + 1] + lower[0, p]
        pack_edges(g, 1)
        send_edges(g, 1)

    def prepare(which):
        row_at = lax.broadcasted_iota(jnp.int32, (24, 2 * cz), 0)
        row_at = jnp.where(row_at < cy + WIDTH, row_at, row_at - 24) + m * cy
        lane_at = lax.broadcasted_iota(jnp.int32, (24, 2 * cz), 1)
        lane_real = (lane_at < cz + WIDTH) | (lane_at >= 2 * cz - WIDTH)
        lane_at = jnp.where(lane_at < cz + WIDTH, lane_at, lane_at - 2 * cz) + n * cz
        inside = lane_real & (row_at >= 0) & (row_at < n_m * cy) & (lane_at >= 0) & (lane_at < n_n * cz)
        inside = jnp.where(inside, 1.0, 0.0)
        for p in which:
            here = inside
            if p < WIDTH:
                here = jnp.where(w > 0, inside, 0.0)
            elif p >= WIDTH + cx:
                here = jnp.where(w < n_w - 1, inside, 0.0)
            capacity, start = inv[p], ext[0, p]
            base[p] = capacity * start
            inv[p] = here / (capacity + 6.0 * CONDUCT)
            ext[0, p] = jnp.where(here > 0.0, start, 0.0)

    def keep_inside(which):
        for p in which:
            ext[0, p] = jnp.where(inv[p] > 0.0, ext[0, p], 0.0)

    def around(plane):
        rows = pltpu.roll(plane, 1, 0) + pltpu.roll(plane, 23, 0)
        return rows + (pltpu.roll(plane, 1, 1) + pltpu.roll(plane, 2 * cz - 1, 1))

    def plain_sweeps(it, inner):
        for k in range(SWEEPS):
            now, later = k % 2, (k + 1) % 2
            edge = k + 1
            inside = range(edge + WIDTH, planes - edge - WIDTH)
            for p in inside if inner else [p for p in range(edge, planes - edge) if p not in inside]:
                total = (ext[now, p - 1] + ext[now, p + 1]) + around(ext[now, p]) + base[p]
                new = total * inv[p]
                if k == SWEEPS - 1:
                    plain[it, p - WIDTH] = new[:cy, :cz]
                else:
                    ext[later, p] = new

    def edge_sems(it, side):
        return (xsend_sem.at[it, side], xrecv_sem.at[it, side])

    def source_start(it, source):
        srcb[it, 0] = source[:8]
        srcb[it, 1] = source[8:]

        def send(side, parts):
            for src, place_at, count, dm, dn in parts:
                remote(
                    srcb.at[it, pl.ds(src, count)], src_in.at[it, pl.ds(place_at, count)],
                    edge_sems(it, side), beside(0, dm, dn),
                ).start()

        send(0, ((0, 0, 1, -1, 0), (1, 1, 1, 1, 0)))

        @pl.when(n > 0)
        def _():
            send(1, ((0, 2, 2, 0, -1), (0, 4, 1, -1, -1), (1, 5, 1, 1, -1)))

        @pl.when(n < n_n - 1)
        def _():
            send(2, ((0, 6, 2, 0, 1), (0, 8, 1, -1, 1), (1, 9, 1, 1, 1)))

    def source_done(it):
        wait_recv(src_in.at[it, pl.ds(0, 2)], edge_sems(it, 0))

        @pl.when(n < n_n - 1)
        def _():
            wait_recv(src_in.at[it, pl.ds(2, 4)], edge_sems(it, 1))

        @pl.when(n > 0)
        def _():
            wait_recv(src_in.at[it, pl.ds(6, 4)], edge_sems(it, 2))

        def corner(up, down):
            return jnp.where(row8 < WIDTH, src_in[it, up], src_in[it, down])

        def lanes(after, before):
            return jnp.where(lane8 < WIDTH, after, before)

        main = jnp.concatenate([srcb[it, 0], srcb[it, 1], corner(0, 1)], axis=0)
        sides = jnp.concatenate(
            [lanes(src_in[it, 2], src_in[it, 6]), lanes(src_in[it, 3], src_in[it, 7]), lanes(corner(4, 5), corner(8, 9))],
            axis=0,
        )
        return jnp.concatenate([main, sides], axis=1)

    def grown(wide_source, have, p):
        total = jnp.zeros((24, 2 * cz), F32)
        if p == 0:
            total = wide_source
        for q in (p - 1, p + 1):
            if q in have:
                total = total + have[q]
        if p in have:
            total = total + around(have[p])
        return total * inv[WIDTH + p]

    def first_sweeps(wide_source):
        one = {0: wide_source * inv[WIDTH]}
        two = {p: grown(wide_source, one, p) for p in (0, -1, 1)}
        three = {p: grown(wide_source, two, p) for p in (0, -1, 1)}
        wall = grown(wide_source, three, 0)[:cy, :cz]
        return two, three, wall

    def last_sweeps(it, wide_source, two, three):
        three.update({p: grown(wide_source, two, p) for p in (-2, 2)})
        for p in (-3, -2, -1):
            lower[it, p + 3] = grown(wide_source, three, p)[:cy, :cz]
        remote(lower.at[it], lower_in.at[it], (lsend_sem.at[it], lrecv_sem.at[it]), beside(-1, 0, 0)).start()
        return [grown(wide_source, three, p)[:cy, :cz] for p in (1, 2, 3)]

    def lower_arrived(it):
        wait_recv(lower_in.at[it], (lsend_sem.at[it], lrecv_sem.at[it]))

    def apply(v16):
        v = v16.astype(F32)
        linked = jnp.dot(v16, col_hot[...], preferred_element_type=F32)
        near0, near1 = linked[:, :128], linked[:, 128:]

        def rows(t, carry):
            sums = []
            for u in range(8):
                i = t * 8 + u
                prod = wide_blocks[0, i] * v + wide_blocks[1, i] * near0 + wide_blocks[2, i] * near1
                sums.append(jnp.sum(prod, axis=0, keepdims=True))
            kv[pl.ds(pl.multiple_of(t * 8, 8), 8), :] = jnp.concatenate(sums, axis=0)
            return carry

        lax.fori_loop(0, BLOCK // 8, rows, 0)
        return kv[...]

    def newton_start():
        mt, st = melt[...], state[...]
        bulk = BULK_BASE * jnp.exp(-BULK_SLOPE * mt)
        growth = jnp.exp(st)
        press = bulk * (growth - 1.0)
        base_volume = jnp.exp(EXPAND * mt)
        volume = base_volume * (1.0 - TAIT_C * st)
        sl = bulk * growth
        slope[...] = sl
        jd = diag[...] * sl + TAIT_C * base_volume
        jdiag[...] = jd
        rounded = press.astype(BF16)
        res = apply(rounded) + diag[...] * rounded.astype(F32) + (target[...] - volume) - inflow[...]
        resid[...] = res
        upd[...] = -res / jd

    def newton_step():
        weighted = (slope[...] * upd[...]).astype(BF16)
        upd[...] = (-resid[...] - apply(weighted)) / jdiag[...]

    for load in loads[:4]:
        load.wait()
    rel = jnp.bitwise_xor(owner[...], w)
    place = rel * 16 + slot[...] // 2
    half = slot[...] % 2
    faces = lax.broadcasted_iota(jnp.int32, (512, 128), 0)
    hot32 = jnp.where(faces == place, 1.0, 0.0)
    hot[...] = hot32.astype(BF16)
    scatter_fill(0, scatter_terms((coef[...] * melt[...], coef[...])))
    for it in range(ITERS):
        src_in[it] = jnp.zeros((10, 8, cz), F32)
    loads[4].wait()
    loads[5].wait()
    tab[0, 0, 0] = near[0, WIDTH]
    pack_edges(0, 0)
    pl.semaphore_wait(barrier, len(peers))

    for k in FAR_FIRST:
        scatter_start(0, k)
    send_low(0)
    send_high(0)
    gather_start(0)
    send_edges(0, 0)
    scatter_start(0, 0)
    gather_on(0, 0)
    hot_t[...] = hot32.T.astype(BF16)
    for load in loads[6:]:
        load.wait()
    froms = lax.broadcasted_iota(jnp.int32, (128, 128), 0)
    for k in range(2):
        col_hot[:, k * 128:(k + 1) * 128] = jnp.where(froms == columns[k:k + 1, :], 1.0, 0.0).astype(BF16)

    def pick(t, carry):
        sums = []
        for u in range(8):
            i = t * 8 + u
            mask = lax.broadcasted_iota(jnp.int32, (BLOCK, 128), 0) == i
            block = selfb[i].astype(F32)
            sums.append(jnp.sum(jnp.where(mask, block, 0.0), axis=0, keepdims=True))
            wide_blocks[0, i] = jnp.where(mask, 0.0, block)
            wide_blocks[1, i] = linkb[0, i].astype(F32)
            wide_blocks[2, i] = linkb[1, i].astype(F32)
        diag[pl.ds(pl.multiple_of(t * 8, 8), 8), :] = jnp.concatenate(sums, axis=0)
        return carry

    lax.fori_loop(0, BLOCK // 8, pick, 0)
    for k in FAR_FIRST:
        scatter_on(0, k)
    square = coef[...] * coef[...]
    scatter_fill(1, scatter_terms((square * melt[...], square)))
    z_arrived(0, 1)
    z_arrived(0, 3)
    wide_arrived(0)
    for k in FAR_FIRST + (0,):
        scatter_start(1, k)
    take_edges(0, 0, (ext.at[0], inv))
    prepare(own_planes)
    scatter_on(0, 0)
    plain_sweeps(0, True)

    sum_a, sum_b = scatter_done(0)
    first_wall = near[0, WIDTH]
    source_start(0, sum_a - sum_b * first_wall)
    z_arrived(0, 2)
    take_edges(0, 1, (ext.at[0], inv))
    prepare(ghost_planes)
    plain_sweeps(0, False)
    send_high(1)
    for k in FAR_FIRST + (0,):
        scatter_on(1, k)
    spread_source = source_done(0)
    two, three, wall_part = first_sweeps(spread_source)
    second_wall = plain[0, 0] + wall_part
    tab[1, 0, 0] = second_wall
    gather_start(1)
    gather_on(1, 0)
    upper = last_sweeps(0, spread_source, two, three)
    near[2, WIDTH] = second_wall
    for p in range(1, 4):
        near[2, WIDTH + p] = plain[0, p] + upper[p - 1]
    send_low(1)
    for p in range(4, cx - 3):
        near[2, WIDTH + p] = plain[0, p]

    cool(0)
    newton_start()
    z_arrived(1, 1)
    z_arrived(1, 3)
    sum_c, sum_d = scatter_done(1)
    source_start(1, sum_a - COOLING * sum_c + COOLING * sum_d * first_wall - sum_b * second_wall)
    lower_arrived(0)
    for p in range(3):
        near[2, WIDTH + cx - 3 + p] = plain[0, cx - 3 + p] + lower_in[0, p]
    pack_edges(1, 0)
    send_edges(1, 0)
    newton_step()
    z_arrived(1, 2)
    wide_arrived(1)
    newton_step()
    state[...] = state[...] + upd[...]
    spread_source = source_done(1)
    two, three, wall_part = first_sweeps(spread_source)
    upper = last_sweeps(1, spread_source, two, three)
    take_edges(1, 0, (ext.at[0],))
    keep_inside(own_planes)
    plain_sweeps(1, True)

    cool(1)
    newton_start()
    take_edges(1, 1, (ext.at[0],))
    keep_inside(ghost_planes)
    plain_sweeps(1, False)
    out_field[0] = plain[1, 0] + wall_part
    for p in range(1, 4):
        out_field[p] = plain[1, p] + upper[p - 1]
    for p in range(4, cx - 3):
        out_field[p] = plain[1, p]
    newton_step()
    lower_arrived(1)
    for p in range(3):
        out_field[cx - 3 + p] = plain[1, cx - 3 + p] + lower_in[1, p]
    newton_step()
    mt, st = melt[...], state[...] + upd[...]
    out_press[...] = BULK_BASE * jnp.exp(-BULK_SLOPE * mt) * (jnp.exp(st) - 1.0)
    out_shrink[...] = 1.0 - jnp.exp(EXPAND * mt) * (1.0 - TAIT_C * st)

    def wait_send(region, sems):
        remote(region, region, sems, beside(0, 1, 0)).wait_send()

    for it in range(ITERS):
        for k in range(4):
            if k > 0:
                wait_send(tab.at[it, k, 0], z_sems(it, k))
                wait_send(psum.at[it, k], sum_sems(it, k))
            wait_send(tab.at[it, k, pl.ds(1, 7)], gather_sems(it, k))
            wait_send(spread.at[it, k, pl.ds(1, 7)], scatter_sems(it, k))
        wait_send(src_in.at[it, pl.ds(0, 2)], edge_sems(it, 0))

        @pl.when(n > 0)
        def _():
            wait_send(src_in.at[it, pl.ds(2, 4)], edge_sems(it, 1))

        @pl.when(n < n_n - 1)
        def _():
            wait_send(src_in.at[it, pl.ds(6, 4)], edge_sems(it, 2))

        wait_send(lower.at[it], (lsend_sem.at[it], lrecv_sem.at[it]))
    for g in range(2):
        some = group(g)
        wait_send(near.at[some, pl.ds(0, WIDTH)], h_sems(g, 0, 0))
        wait_send(near.at[some, pl.ds(0, WIDTH)], h_sems(g, 0, 1))
        for step, regions in ((0, (rows_own, lanes_own, corner_own)), (1, (rows_ghost, lanes_ghost, corner_ghost))):
            for kind, region in enumerate(regions):
                wait_send(region.at[some], h_sems(g, step, 2 + kind))


def per_device(
    mold_temp, capacity, melt_temp, log_pressure, target_volume, inflow, self_blocks, link_blocks,
    link_columns, wall_owner, wall_slot, transfer_coef,
):
    cx, cy, cz = mold_temp.shape
    cells, blocks = melt_temp.shape
    planes = cx + 2 * WIDTH
    vmem = pl.BlockSpec(memory_space=pltpu.VMEM)
    hbm = pl.BlockSpec(memory_space=pltpu.HBM)

    def scratch(*shape):
        return pltpu.VMEM(shape, F32)

    cav = scratch(cells, blocks)
    return pl.pallas_call(
        kernel,
        out_shape=(
            pltpu.VMEM(mold_temp.shape, F32),
            pltpu.VMEM(melt_temp.shape, F32),
            pltpu.VMEM(melt_temp.shape, F32),
        ),
        in_specs=[hbm] * 12,
        out_specs=(vmem, vmem, vmem),
        scratch_shapes=[
            pltpu.VMEM(self_blocks.shape, BF16),
            pltpu.VMEM(link_blocks.shape, BF16),
            scratch(3, *self_blocks.shape),
            scratch(ITERS, 4, 8, 16, 128),
            scratch(2, 4, 8, 2, 16, 128),
            scratch(2, 4, 8, 2, 16, 128),
            scratch(2, 4, 2, 16, 128),
            scratch(2, 4, 2, 16, 128),
            scratch(3, planes, cy, cz),
            scratch(3, 2, 8, 8, cz),
            scratch(3, 2, 4, 8, cz),
            scratch(3, 2, 8, cz),
            scratch(3, 2, 8, cz),
            scratch(3, 2, 8, 8, cz),
            scratch(3, 2, 4, 8, cz),
            scratch(3, 2, 2, 8, cz),
            scratch(3, 2, 2, 8, cz),
            scratch(3, 2, 2, 8, cz),
            scratch(3, 2, 2, 8, cz),
            scratch(2, planes, 24, 2 * cz),
            scratch(planes, 24, 2 * cz),
            scratch(planes, 24, 2 * cz),
            scratch(ITERS, cx, cy, cz),
            scratch(ITERS, 2, 8, cz),
            scratch(ITERS, 10, 8, cz),
            scratch(ITERS, 3, cy, cz),
            scratch(ITERS, 3, cy, cz),
            pltpu.VMEM((512, 128), BF16),
            pltpu.VMEM((128, 512), BF16),
            pltpu.VMEM((128, 256), BF16),
            cav, cav, cav, cav, cav, cav, cav, cav, cav, cav, cav,
            pltpu.VMEM((2, blocks), jnp.int32),
            pltpu.VMEM((1, blocks), jnp.int32),
            pltpu.VMEM((1, blocks), jnp.int32),
            pltpu.SemaphoreType.DMA((12,)),
            *[pltpu.SemaphoreType.DMA((ITERS, 4))] * 8,
            *[pltpu.SemaphoreType.DMA((ITERS, 3))] * 2,
            *[pltpu.SemaphoreType.DMA((ITERS,))] * 2,
            *[pltpu.SemaphoreType.DMA((2, 2, 5))] * 2,
        ],
        compiler_params=pltpu.CompilerParams(
            collective_id=0, has_side_effects=True, vmem_limit_bytes=56 * 1024 * 1024
        ),
    )(
        mold_temp, capacity, melt_temp, log_pressure, target_volume, inflow, transfer_coef,
        link_columns, wall_owner.reshape(1, blocks), wall_slot.reshape(1, blocks), self_blocks, link_blocks,
    )


def solution(mesh):
    cavity = P(None, ("wide", "mid", "narrow"))
    brick = P("wide", "mid", "narrow")
    flat = P(("wide", "mid", "narrow"))
    return jax.shard_map(
        per_device,
        mesh=mesh,
        in_specs=(
            brick, brick, cavity, cavity, cavity, cavity,
            P(None, None, ("wide", "mid", "narrow")),
            P(None, None, None, ("wide", "mid", "narrow")),
            cavity, flat, flat, cavity,
        ),
        out_specs=(brick, cavity, cavity),
        check_vma=False,
    )
```

```python
import functools

import jax
import jax.numpy as jnp
from jax import lax
from jax.experimental import pallas as pl
from jax.experimental.pallas import tpu as pltpu
from jax.sharding import PartitionSpec as P

BLOCK = 64
ITERS = 2
SWEEPS = 4
INNER = 2
WIDTH = 4
FAR_FIRST = (2, 1, 3)

CONDUCT = 1.0
COOLING = 0.5
TAIT_C = 0.3
EXPAND = 0.25
BULK_BASE = 0.5
BULK_SLOPE = 0.3

MESH = pl.DeviceIdType.MESH
F32 = jnp.float32
BF16 = jnp.bfloat16


def flip(v, k):
    if k == 0:
        return v
    if k == 1:
        return v + 1 - 2 * (v % 2)
    if k == 2:
        return (v + 2) % 4
    return 3 - v


def split_terms(x):
    hi = x.astype(BF16)
    lo = (x - hi.astype(F32)).astype(BF16)
    return hi, lo


def kernel(
    mold, cap, melt_in, logp, target_in, inflow_in, coef_in, columns_in, owner_in, slot_in, self_in, link_in,
    out_field, out_press, out_shrink,
    selfb, linkb, wide_blocks, tab, spread, rs1, psum, rs2, near,
    row_own, row_ghost, lane_own, lane_ghost, rows_own, rows_ghost, lanes_own, lanes_ghost, corner_own, corner_ghost,
    ext, inv, base, plain, srcb, src_in, lower, lower_in,
    hot, hot_t, col_hot, diag, kv, resid, jdiag, slope, upd, state, melt, target, inflow, coef,
    columns, owner, slot,
    load_sem, zsend_sem, zrecv_sem, gsend_sem, grecv_sem, csend_sem, crecv_sem, ysend_sem, yrecv_sem,
    xsend_sem, xrecv_sem, lsend_sem, lrecv_sem, hsend_sem, hrecv_sem,
):
    cx, cy, cz = mold.shape
    planes = near.shape[1]
    w = lax.axis_index("wide")
    m = lax.axis_index("mid")
    n = lax.axis_index("narrow")
    n_w, n_m, n_n = lax.axis_size("wide"), lax.axis_size("mid"), lax.axis_size("narrow")
    zh, x, c = w // 8, (w // 2) % 4, w % 2

    def z_peer(k):
        return (flip(zh, k) * 8 + x * 2 + c, m, n)

    def xc_peer(j):
        return (zh * 8 + flip(x, j // 2) * 2 + flip(c, j % 2), m, n)

    def beside(dw, dm, dn):
        return ((w + n_w + dw) % n_w, (m + n_m + dm) % n_m, (n + n_n + dn) % n_n)

    barrier = pltpu.get_barrier_semaphore()
    peers = [z_peer(k) for k in range(1, 4)] + [xc_peer(j) for j in range(1, 8)]
    peers += [beside(-1, 0, 0), beside(1, 0, 0)]
    peers += [beside(0, dm, dn) for dm in (-1, 0, 1) for dn in (-1, 0, 1) if (dm, dn) != (0, 0)]
    for peer in peers:
        pl.semaphore_signal(barrier, inc=1, device_id=peer, device_id_type=MESH)

    loads = [
        pltpu.make_async_copy(src, dst, load_sem.at[i])
        for i, (src, dst) in enumerate((
            (owner_in, owner), (slot_in, slot), (coef_in, coef), (melt_in, melt),
            (mold, near.at[0, pl.ds(WIDTH, cx)]), (cap, near.at[1, pl.ds(WIDTH, cx)]), (columns_in, columns),
            (self_in, selfb), (link_in, linkb), (logp, state), (target_in, target), (inflow_in, inflow),
        ))
    ]
    for load in loads:
        load.start()

    def remote(src, dst, sems, peer):
        return pltpu.make_async_remote_copy(
            src_ref=src, dst_ref=dst, send_sem=sems[0], recv_sem=sems[1],
            device_id=peer, device_id_type=MESH,
        )

    def wait_recv(region, sems):
        remote(region, region, sems, beside(0, 1, 0)).wait_recv()

    def z_sems(it, k):
        return (zsend_sem.at[it, k], zrecv_sem.at[it, k])

    def gather_sems(it, k):
        return (gsend_sem.at[it, k], grecv_sem.at[it, k])

    def gather_on(it, k):
        for j in range(1, 8):
            remote(tab.at[it, k, 0], tab.at[it, k, j], gather_sems(it, k), xc_peer(j)).start()

    def gather_start(it):
        for k in FAR_FIRST:
            remote(tab.at[it, 0, 0], tab.at[it, k, 0], z_sems(it, k), z_peer(k)).start()

    def z_arrived(it, k):
        wait_recv(tab.at[it, k, 0], z_sems(it, k))
        gather_on(it, k)

    def cool(it):
        found = jnp.zeros((128, 256), F32)
        for k in (0, 1, 3, 2):
            wait_recv(tab.at[it, k, pl.ds(1, 7)], gather_sems(it, k))
            hi, lo = split_terms(tab[it, k].reshape(128, 128))
            found = found + jnp.dot(
                hot_t[:, k * 128:(k + 1) * 128], jnp.concatenate([hi, lo], axis=1), preferred_element_type=F32
            )
        found = (found[:, :128] + found[:, 128:]).T
        wall = jnp.where(half == 1, found[BLOCK:], found[:BLOCK])
        melt[...] = melt[...] - COOLING * (coef[...] * (melt[...] - wall))

    def scatter_sems(a, k):
        return (csend_sem.at[a, k], crecv_sem.at[a, k])

    def sum_sems(a, k):
        return (ysend_sem.at[a, k], yrecv_sem.at[a, k])

    sums = (pl.ds(0, 2), pl.ds(0, 1))

    def scatter_terms(values):
        parts = []
        for value in values:
            placed = jnp.concatenate([jnp.where(half == 0, value, 0.0), jnp.where(half == 1, value, 0.0)], axis=0)
            parts.extend(split_terms(placed))
        return jnp.concatenate(parts, axis=0)

    def scatter_fill(a, terms):
        for k in range(4):
            summed = lax.dot_general(
                hot[k * 128:(k + 1) * 128, :], terms, (((1,), (1,)), ((), ())), preferred_element_type=F32
            )
            for q in range(2):
                one = summed[:, 256 * q:256 * q + 128] + summed[:, 256 * q + 128:256 * q + 256]
                spread[a, k, :, q] = one.reshape(8, 16, 128)

    def scatter_start(a, k):
        for j in range(1, 8):
            remote(spread.at[a, k, j], rs1.at[a, k, j], scatter_sems(a, k), xc_peer(j)).start()

    def scatter_on(a, k):
        wait_recv(rs1.at[a, k, pl.ds(1, 7)], scatter_sems(a, k))
        totals = []
        for q in range(2):
            total = spread[a, k, 0, q]
            for j in range(1, 8):
                total = total + rs1[a, k, j, q]
            totals.append(total)
        if a == 0:
            psum[a, k, 0], psum[a, k, 1] = totals
        else:
            psum[a, k, 0] = COOLING * (totals[0] - totals[1] * tab[0, k, 0])
        if k > 0:
            remote(psum.at[a, k, sums[a]], rs2.at[a, k, sums[a]], sum_sems(a, k), z_peer(k)).start()

    def scatter_done(a):
        for k in (1, 3, 2):
            wait_recv(rs2.at[a, k, sums[a]], sum_sems(a, k))
        return [
            ((psum[a, 0, q] + rs2[a, 1, q]) + (rs2[a, 3, q] + rs2[a, 2, q])) for q in range(2 - a)
        ]

    lane = lax.broadcasted_iota(jnp.int32, (cy, cz), 1)
    lane24 = lax.broadcasted_iota(jnp.int32, (24, cz), 1)
    row8 = lax.broadcasted_iota(jnp.int32, (8, cz), 0)
    lane8 = lax.broadcasted_iota(jnp.int32, (8, cz), 1)
    own_planes = list(range(WIDTH, WIDTH + cx))
    ghost_planes = list(range(WIDTH)) + list(range(WIDTH + cx, planes))
    arrays = ((0, 1), (2,))

    def h_sems(g, step, kind):
        return (hsend_sem.at[g, step, kind], hrecv_sem.at[g, step, kind])

    def group(g):
        return pl.ds(arrays[g][0], len(arrays[g]))

    def send_low(g):
        remote(
            near.at[group(g), pl.ds(WIDTH, WIDTH)], near.at[group(g), pl.ds(WIDTH + cx, WIDTH)],
            h_sems(g, 0, 0), beside(-1, 0, 0),
        ).start()

    def send_high(g):
        src = near.at[group(0), pl.ds(cx, WIDTH)] if g == 0 else plain.at[pl.ds(0, 1), pl.ds(cx - WIDTH, WIDTH)]
        remote(src, near.at[group(g), pl.ds(0, WIDTH)], h_sems(g, 0, 1), beside(1, 0, 0)).start()

    def pack_edges(g, step):
        which, row_out, lane_out = ((own_planes, row_own, lane_own), (ghost_planes, row_ghost, lane_ghost))[step]
        for a in arrays[g]:
            packed = jnp.zeros((cy, cz), F32)
            for q, p in enumerate(which):
                packed = jnp.where(lane // 8 == q, pltpu.roll(near[a, p], WIDTH + 8 * q, 1), packed)
            lane_out[a, 0] = packed[:8]
            lane_out[a, 1] = packed[8:]
            for t in range(len(which) // 2):
                q = 4 * (t // 2) + t % 2
                one, two = near[a, which[q]], near[a, which[q + 2]]
                row_out[a, 0, t] = jnp.where(row8 < WIDTH, one[:8], pltpu.roll(two[:8], 4, 0))
                row_out[a, 1, t] = jnp.where(row8 < WIDTH, pltpu.roll(one[8:], 4, 0), two[8:])

    def send_edges(g, step):
        row_out, lane_out, rows_in, lanes_in, corner_in = (
            (row_own, lane_own, rows_own, lanes_own, corner_own),
            (row_ghost, lane_ghost, rows_ghost, lanes_ghost, corner_ghost),
        )[step]
        some = group(g)
        for side, dm in ((0, -1), (1, 1)):
            remote(row_out.at[some, side], rows_in.at[some, side], h_sems(g, step, 2), beside(0, dm, 0)).start()
        for side, dn in ((0, -1), (1, 1)):
            remote(lane_out.at[some], lanes_in.at[some, side], h_sems(g, step, 3), beside(0, 0, dn)).start()
            for tile, dm in ((0, -1), (1, 1)):
                remote(
                    lane_out.at[some, tile], corner_in.at[some, side, tile], h_sems(g, step, 4), beside(0, dm, dn)
                ).start()

    def take_edges(g, step, places):
        which, rows_in, lanes_in, corner_in = (
            (own_planes, rows_own, lanes_own, corner_own), (ghost_planes, rows_ghost, lanes_ghost, corner_ghost),
        )[step]
        some = group(g)
        for kind, region in ((2, rows_in), (3, lanes_in), (4, corner_in)):
            wait_recv(region.at[some], h_sems(g, step, kind))
        for a, dst in zip(arrays[g], places):
            sides = []
            for side in range(2):
                corner = jnp.where(row8 < WIDTH, corner_in[a, side, 0], corner_in[a, side, 1])
                sides.append(jnp.concatenate([lanes_in[a, side, 0], lanes_in[a, side, 1], corner], axis=0))
            comb = jnp.where(lane24 % 8 >= WIDTH, sides[0], sides[1])
            for t in range(len(which) // 2):
                q = 4 * (t // 2) + t % 2
                after, before = rows_in[a, 0, t], rows_in[a, 1, t]
                ghosts = (
                    (q, jnp.where(row8 < WIDTH, after, pltpu.roll(before, 4, 0))),
                    (q + 2, jnp.where(row8 < WIDTH, pltpu.roll(after, 4, 0), before)),
                )
                for at, ghost in ghosts:
                    p = which[at]
                    dst[p, 0:cy, 0:cz] = near[a, p]
                    dst[p, cy:24, 0:cz] = ghost
                    dst[p, :, cz:2 * cz] = pltpu.roll(comb, cz - (8 * at + WIDTH), 1)

    def wide_arrived(g):
        wait_recv(near.at[group(g), pl.ds(WIDTH + cx, WIDTH)], h_sems(g, 0, 0))
        wait_recv(near.at[group(g), pl.ds(0, WIDTH)], h_sems(g, 0, 1))
        if g == 1:
            for p in range(3):
                near[2, p + 1] = near[2, p + 1] + lower[0, p]
        pack_edges(g, 1)
        send_edges(g, 1)

    def prepare(which):
        row_at = lax.broadcasted_iota(jnp.int32, (24, 2 * cz), 0)
        row_at = jnp.where(row_at < cy + WIDTH, row_at, row_at - 24) + m * cy
        lane_at = lax.broadcasted_iota(jnp.int32, (24, 2 * cz), 1)
        lane_real = (lane_at < cz + WIDTH) | (lane_at >= 2 * cz - WIDTH)
        lane_at = jnp.where(lane_at < cz + WIDTH, lane_at, lane_at - 2 * cz) + n * cz
        inside = lane_real & (row_at >= 0) & (row_at < n_m * cy) & (lane_at >= 0) & (lane_at < n_n * cz)
        inside = jnp.where(inside, 1.0, 0.0)
        for p in which:
            here = inside
            if p < WIDTH:
                here = jnp.where(w > 0, inside, 0.0)
            elif p >= WIDTH + cx:
                here = jnp.where(w < n_w - 1, inside, 0.0)
            capacity, start = inv[p], ext[0, p]
            base[p] = capacity * start
            inv[p] = here / (capacity + 6.0 * CONDUCT)
            ext[0, p] = jnp.where(here > 0.0, start, 0.0)

    def keep_inside(which):
        for p in which:
            ext[0, p] = jnp.where(inv[p] > 0.0, ext[0, p], 0.0)

    def around(plane):
        rows = pltpu.roll(plane, 1, 0) + pltpu.roll(plane, 23, 0)
        return rows + (pltpu.roll(plane, 1, 1) + pltpu.roll(plane, 2 * cz - 1, 1))

    def plain_sweeps(it, inner):
        for k in range(SWEEPS):
            now, later = k % 2, (k + 1) % 2
            edge = k + 1
            inside = range(edge + WIDTH, planes - edge - WIDTH)
            for p in inside if inner else [p for p in range(edge, planes - edge) if p not in inside]:
                total = (ext[now, p - 1] + ext[now, p + 1]) + around(ext[now, p]) + base[p]
                new = total * inv[p]
                if k == SWEEPS - 1:
                    plain[it, p - WIDTH] = new[:cy, :cz]
                else:
                    ext[later, p] = new

    def edge_sems(it, side):
        return (xsend_sem.at[it, side], xrecv_sem.at[it, side])

    def source_start(it, source):
        srcb[it, 0] = source[:8]
        srcb[it, 1] = source[8:]

        def send(side, parts):
            for src, place_at, count, dm, dn in parts:
                remote(
                    srcb.at[it, pl.ds(src, count)], src_in.at[it, pl.ds(place_at, count)],
                    edge_sems(it, side), beside(0, dm, dn),
                ).start()

        send(0, ((0, 0, 1, -1, 0), (1, 1, 1, 1, 0)))

        @pl.when(n > 0)
        def _():
            send(1, ((0, 2, 2, 0, -1), (0, 4, 1, -1, -1), (1, 5, 1, 1, -1)))

        @pl.when(n < n_n - 1)
        def _():
            send(2, ((0, 6, 2, 0, 1), (0, 8, 1, -1, 1), (1, 9, 1, 1, 1)))

    def source_done(it):
        wait_recv(src_in.at[it, pl.ds(0, 2)], edge_sems(it, 0))

        @pl.when(n < n_n - 1)
        def _():
            wait_recv(src_in.at[it, pl.ds(2, 4)], edge_sems(it, 1))

        @pl.when(n > 0)
        def _():
            wait_recv(src_in.at[it, pl.ds(6, 4)], edge_sems(it, 2))

        def corner(up, down):
            return jnp.where(row8 < WIDTH, src_in[it, up], src_in[it, down])

        def lanes(after, before):
            return jnp.where(lane8 < WIDTH, after, before)

        main = jnp.concatenate([srcb[it, 0], srcb[it, 1], corner(0, 1)], axis=0)
        sides = jnp.concatenate(
            [lanes(src_in[it, 2], src_in[it, 6]), lanes(src_in[it, 3], src_in[it, 7]), lanes(corner(4, 5), corner(8, 9))],
            axis=0,
        )
        return jnp.concatenate([main, sides], axis=1)

    def grown(wide_source, have, p):
        total = jnp.zeros((24, 2 * cz), F32)
        if p == 0:
            total = wide_source
        for q in (p - 1, p + 1):
            if q in have:
                total = total + have[q]
        if p in have:
            total = total + around(have[p])
        return total * inv[WIDTH + p]

    def first_sweeps(wide_source):
        one = {0: wide_source * inv[WIDTH]}
        two = {p: grown(wide_source, one, p) for p in (0, -1, 1)}
        three = {p: grown(wide_source, two, p) for p in (0, -1, 1)}
        wall = grown(wide_source, three, 0)[:cy, :cz]
        return two, three, wall

    def last_sweeps(it, wide_source, two, three):
        three.update({p: grown(wide_source, two, p) for p in (-2, 2)})
        for p in (-3, -2, -1):
            lower[it, p + 3] = grown(wide_source, three, p)[:cy, :cz]
        remote(lower.at[it], lower_in.at[it], (lsend_sem.at[it], lrecv_sem.at[it]), beside(-1, 0, 0)).start()
        return [grown(wide_source, three, p)[:cy, :cz] for p in (1, 2, 3)]

    def lower_arrived(it):
        wait_recv(lower_in.at[it], (lsend_sem.at[it], lrecv_sem.at[it]))

    def apply(v16):
        v = v16.astype(F32)
        linked = jnp.dot(v16, col_hot[...], preferred_element_type=F32)
        near0, near1 = linked[:, :128], linked[:, 128:]

        def rows(t, carry):
            sums = []
            for u in range(8):
                i = t * 8 + u
                prod = wide_blocks[0, i] * v + wide_blocks[1, i] * near0 + wide_blocks[2, i] * near1
                sums.append(jnp.sum(prod, axis=0, keepdims=True))
            kv[pl.ds(pl.multiple_of(t * 8, 8), 8), :] = jnp.concatenate(sums, axis=0)
            return carry

        lax.fori_loop(0, BLOCK // 8, rows, 0)
        return kv[...]

    def newton_start():
        mt, st = melt[...], state[...]
        bulk = BULK_BASE * jnp.exp(-BULK_SLOPE * mt)
        growth = jnp.exp(st)
        press = bulk * (growth - 1.0)
        base_volume = jnp.exp(EXPAND * mt)
        volume = base_volume * (1.0 - TAIT_C * st)
        sl = bulk * growth
        slope[...] = sl
        jd = diag[...] * sl + TAIT_C * base_volume
        jdiag[...] = jd
        rounded = press.astype(BF16)
        res = apply(rounded) + diag[...] * rounded.astype(F32) + (target[...] - volume) - inflow[...]
        resid[...] = res
        upd[...] = -res / jd

    def newton_step():
        weighted = (slope[...] * upd[...]).astype(BF16)
        upd[...] = (-resid[...] - apply(weighted)) / jdiag[...]

    for load in loads[:4]:
        load.wait()
    rel = jnp.bitwise_xor(owner[...], w)
    place = rel * 16 + slot[...] // 2
    half = slot[...] % 2
    faces = lax.broadcasted_iota(jnp.int32, (512, 128), 0)
    hot32 = jnp.where(faces == place, 1.0, 0.0)
    hot[...] = hot32.astype(BF16)
    scatter_fill(0, scatter_terms((coef[...] * melt[...], coef[...])))
    for it in range(ITERS):
        src_in[it] = jnp.zeros((10, 8, cz), F32)
    loads[4].wait()
    loads[5].wait()
    tab[0, 0, 0] = near[0, WIDTH]
    pack_edges(0, 0)
    pl.semaphore_wait(barrier, len(peers))

    for k in FAR_FIRST:
        scatter_start(0, k)
    send_low(0)
    send_high(0)
    gather_start(0)
    send_edges(0, 0)
    scatter_start(0, 0)
    square = coef[...] * coef[...]
    scatter_fill(1, scatter_terms((square * melt[...], square)))
    for k in FAR_FIRST + (0,):
        scatter_start(1, k)
    hot_t[...] = hot32.T.astype(BF16)
    for load in loads[6:]:
        load.wait()
    froms = lax.broadcasted_iota(jnp.int32, (128, 128), 0)
    for k in range(2):
        col_hot[:, k * 128:(k + 1) * 128] = jnp.where(froms == columns[k:k + 1, :], 1.0, 0.0).astype(BF16)

    def pick(t, carry):
        sums = []
        for u in range(8):
            i = t * 8 + u
            mask = lax.broadcasted_iota(jnp.int32, (BLOCK, 128), 0) == i
            block = selfb[i].astype(F32)
            sums.append(jnp.sum(jnp.where(mask, block, 0.0), axis=0, keepdims=True))
            wide_blocks[0, i] = jnp.where(mask, 0.0, block)
            wide_blocks[1, i] = linkb[0, i].astype(F32)
            wide_blocks[2, i] = linkb[1, i].astype(F32)
        diag[pl.ds(pl.multiple_of(t * 8, 8), 8), :] = jnp.concatenate(sums, axis=0)
        return carry

    lax.fori_loop(0, BLOCK // 8, pick, 0)
    for k in FAR_FIRST:
        scatter_on(0, k)
    gather_on(0, 0)
    z_arrived(0, 1)
    z_arrived(0, 3)
    wide_arrived(0)
    take_edges(0, 0, (ext.at[0], inv))
    prepare(own_planes)
    scatter_on(0, 0)
    plain_sweeps(0, True)

    sum_a, sum_b = scatter_done(0)
    first_wall = near[0, WIDTH]
    source_start(0, sum_a - sum_b * first_wall)
    z_arrived(0, 2)
    take_edges(0, 1, (ext.at[0], inv))
    prepare(ghost_planes)
    plain_sweeps(0, False)
    send_high(1)
    for k in FAR_FIRST + (0,):
        scatter_on(1, k)
    spread_source = source_done(0)
    two, three, wall_part = first_sweeps(spread_source)
    second_wall = plain[0, 0] + wall_part
    tab[1, 0, 0] = second_wall
    gather_start(1)
    gather_on(1, 0)
    upper = last_sweeps(0, spread_source, two, three)
    near[2, WIDTH] = second_wall
    for p in range(1, 4):
        near[2, WIDTH + p] = plain[0, p] + upper[p - 1]
    send_low(1)
    for p in range(4, cx - 3):
        near[2, WIDTH + p] = plain[0, p]

    cool(0)
    newton_start()
    z_arrived(1, 1)
    z_arrived(1, 3)
    (cooled,) = scatter_done(1)
    source_start(1, (sum_a - cooled) - sum_b * second_wall)
    lower_arrived(0)
    for p in range(3):
        near[2, WIDTH + cx - 3 + p] = plain[0, cx - 3 + p] + lower_in[0, p]
    pack_edges(1, 0)
    send_edges(1, 0)
    newton_step()
    z_arrived(1, 2)
    wide_arrived(1)
    newton_step()
    state[...] = state[...] + upd[...]
    spread_source = source_done(1)
    two, three, wall_part = first_sweeps(spread_source)
    upper = last_sweeps(1, spread_source, two, three)
    take_edges(1, 0, (ext.at[0],))
    keep_inside(own_planes)
    plain_sweeps(1, True)

    cool(1)
    newton_start()
    take_edges(1, 1, (ext.at[0],))
    keep_inside(ghost_planes)
    plain_sweeps(1, False)
    out_field[0] = plain[1, 0] + wall_part
    for p in range(1, 4):
        out_field[p] = plain[1, p] + upper[p - 1]
    for p in range(4, cx - 3):
        out_field[p] = plain[1, p]
    newton_step()
    lower_arrived(1)
    for p in range(3):
        out_field[cx - 3 + p] = plain[1, cx - 3 + p] + lower_in[1, p]
    newton_step()
    mt, st = melt[...], state[...] + upd[...]
    out_press[...] = BULK_BASE * jnp.exp(-BULK_SLOPE * mt) * (jnp.exp(st) - 1.0)
    out_shrink[...] = 1.0 - jnp.exp(EXPAND * mt) * (1.0 - TAIT_C * st)

    def wait_send(region, sems):
        remote(region, region, sems, beside(0, 1, 0)).wait_send()

    for it in range(ITERS):
        for k in range(4):
            if k > 0:
                wait_send(tab.at[it, k, 0], z_sems(it, k))
                wait_send(psum.at[it, k, sums[it]], sum_sems(it, k))
            wait_send(tab.at[it, k, pl.ds(1, 7)], gather_sems(it, k))
            wait_send(spread.at[it, k, pl.ds(1, 7)], scatter_sems(it, k))
        wait_send(src_in.at[it, pl.ds(0, 2)], edge_sems(it, 0))

        @pl.when(n > 0)
        def _():
            wait_send(src_in.at[it, pl.ds(2, 4)], edge_sems(it, 1))

        @pl.when(n < n_n - 1)
        def _():
            wait_send(src_in.at[it, pl.ds(6, 4)], edge_sems(it, 2))

        wait_send(lower.at[it], (lsend_sem.at[it], lrecv_sem.at[it]))
    for g in range(2):
        some = group(g)
        wait_send(near.at[some, pl.ds(0, WIDTH)], h_sems(g, 0, 0))
        wait_send(near.at[some, pl.ds(0, WIDTH)], h_sems(g, 0, 1))
        for step, regions in ((0, (rows_own, lanes_own, corner_own)), (1, (rows_ghost, lanes_ghost, corner_ghost))):
            for kind, region in enumerate(regions):
                wait_send(region.at[some], h_sems(g, step, 2 + kind))


def store(field, press, shrink, out_field, out_press, out_shrink, sem):
    copies = [
        pltpu.make_async_copy(src, dst, sem.at[i])
        for i, (src, dst) in enumerate(((field, out_field), (press, out_press), (shrink, out_shrink)))
    ]
    for copy in copies:
        copy.start()
    for copy in copies:
        copy.wait()


def per_device(
    mold_temp, capacity, melt_temp, log_pressure, target_volume, inflow, self_blocks, link_blocks,
    link_columns, wall_owner, wall_slot, transfer_coef,
):
    cx, cy, cz = mold_temp.shape
    cells, blocks = melt_temp.shape
    planes = cx + 2 * WIDTH
    vmem = pl.BlockSpec(memory_space=pltpu.VMEM)
    hbm = pl.BlockSpec(memory_space=pltpu.HBM)

    def scratch(*shape):
        return pltpu.VMEM(shape, F32)

    cav = scratch(cells, blocks)
    results = pl.pallas_call(
        kernel,
        out_shape=(
            pltpu.VMEM(mold_temp.shape, F32),
            pltpu.VMEM(melt_temp.shape, F32),
            pltpu.VMEM(melt_temp.shape, F32),
        ),
        in_specs=[hbm] * 12,
        out_specs=(vmem, vmem, vmem),
        scratch_shapes=[
            pltpu.VMEM(self_blocks.shape, BF16),
            pltpu.VMEM(link_blocks.shape, BF16),
            scratch(3, *self_blocks.shape),
            scratch(ITERS, 4, 8, 16, 128),
            scratch(2, 4, 8, 2, 16, 128),
            scratch(2, 4, 8, 2, 16, 128),
            scratch(2, 4, 2, 16, 128),
            scratch(2, 4, 2, 16, 128),
            scratch(3, planes, cy, cz),
            scratch(3, 2, 8, 8, cz),
            scratch(3, 2, 4, 8, cz),
            scratch(3, 2, 8, cz),
            scratch(3, 2, 8, cz),
            scratch(3, 2, 8, 8, cz),
            scratch(3, 2, 4, 8, cz),
            scratch(3, 2, 2, 8, cz),
            scratch(3, 2, 2, 8, cz),
            scratch(3, 2, 2, 8, cz),
            scratch(3, 2, 2, 8, cz),
            scratch(2, planes, 24, 2 * cz),
            scratch(planes, 24, 2 * cz),
            scratch(planes, 24, 2 * cz),
            scratch(ITERS, cx, cy, cz),
            scratch(ITERS, 2, 8, cz),
            scratch(ITERS, 10, 8, cz),
            scratch(ITERS, 3, cy, cz),
            scratch(ITERS, 3, cy, cz),
            pltpu.VMEM((512, 128), BF16),
            pltpu.VMEM((128, 512), BF16),
            pltpu.VMEM((128, 256), BF16),
            cav, cav, cav, cav, cav, cav, cav, cav, cav, cav, cav,
            pltpu.VMEM((2, blocks), jnp.int32),
            pltpu.VMEM((1, blocks), jnp.int32),
            pltpu.VMEM((1, blocks), jnp.int32),
            pltpu.SemaphoreType.DMA((12,)),
            *[pltpu.SemaphoreType.DMA((ITERS, 4))] * 8,
            *[pltpu.SemaphoreType.DMA((ITERS, 3))] * 2,
            *[pltpu.SemaphoreType.DMA((ITERS,))] * 2,
            *[pltpu.SemaphoreType.DMA((2, 2, 5))] * 2,
        ],
        compiler_params=pltpu.CompilerParams(
            collective_id=0, has_side_effects=True, vmem_limit_bytes=56 * 1024 * 1024
        ),
    )(
        mold_temp, capacity, melt_temp, log_pressure, target_volume, inflow, transfer_coef,
        link_columns, wall_owner.reshape(1, blocks), wall_slot.reshape(1, blocks), self_blocks, link_blocks,
    )
    anywhere = pl.BlockSpec(memory_space=pl.ANY)
    return pl.pallas_call(
        store,
        out_shape=[pltpu.HBM(result.shape, F32) for result in results],
        in_specs=[anywhere] * 3,
        out_specs=[anywhere] * 3,
        scratch_shapes=[pltpu.SemaphoreType.DMA((3,))],
    )(*results)


def solution(mesh):
    cavity = P(None, ("wide", "mid", "narrow"))
    brick = P("wide", "mid", "narrow")
    flat = P(("wide", "mid", "narrow"))
    return jax.shard_map(
        per_device,
        mesh=mesh,
        in_specs=(
            brick, brick, cavity, cavity, cavity, cavity,
            P(None, None, ("wide", "mid", "narrow")),
            P(None, None, None, ("wide", "mid", "narrow")),
            cavity, flat, flat, cavity,
        ),
        out_specs=(brick, cavity, cavity),
        check_vma=False,
    )
```

```python
import functools

import jax
import jax.numpy as jnp
from jax import lax
from jax.experimental import pallas as pl
from jax.experimental.pallas import tpu as pltpu
from jax.sharding import PartitionSpec as P

BLOCK = 64
ITERS = 2
SWEEPS = 4
INNER = 2
WIDTH = 4
FAR_FIRST = (2, 1, 3)
TWO_HOPS_FIRST = (4, 5, 2, 3, 6, 7, 1)

CONDUCT = 1.0
COOLING = 0.5
TAIT_C = 0.3
EXPAND = 0.25
BULK_BASE = 0.5
BULK_SLOPE = 0.3

MESH = pl.DeviceIdType.MESH
F32 = jnp.float32
BF16 = jnp.bfloat16


def flip(v, k):
    if k == 0:
        return v
    if k == 1:
        return v + 1 - 2 * (v % 2)
    if k == 2:
        return (v + 2) % 4
    return 3 - v


def split_terms(x):
    hi = x.astype(BF16)
    lo = (x - hi.astype(F32)).astype(BF16)
    return hi, lo


def kernel(
    mold, cap, melt_in, logp, target_in, inflow_in, coef_in, columns_in, owner_in, slot_in, self_in, link_in,
    out_field, out_melt, out_state,
    selfb, linkb, wide_blocks, tab, spread, rs1, psum, rs2, near,
    row_own, row_ghost, lane_own, lane_ghost, rows_own, rows_ghost, lanes_own, lanes_ghost, corner_own, corner_ghost,
    ext, inv, base, plain, srcb, src_in, lower, lower_in,
    hot, hot_t, col_hot, diag, kv, resid, jdiag, slope, upd, state, melt, target, inflow, coef,
    columns, owner, slot,
    load_sem, zsend_sem, zrecv_sem, gsend_sem, grecv_sem, csend_sem, crecv_sem, ysend_sem, yrecv_sem,
    xsend_sem, xrecv_sem, lsend_sem, lrecv_sem, hsend_sem, hrecv_sem,
):
    cx, cy, cz = mold.shape
    planes = near.shape[1]
    w = lax.axis_index("wide")
    m = lax.axis_index("mid")
    n = lax.axis_index("narrow")
    n_w, n_m, n_n = lax.axis_size("wide"), lax.axis_size("mid"), lax.axis_size("narrow")
    zh, x, c = w // 8, (w // 2) % 4, w % 2

    def z_peer(k):
        return (flip(zh, k) * 8 + x * 2 + c, m, n)

    def xc_peer(j):
        return (zh * 8 + flip(x, j // 2) * 2 + flip(c, j % 2), m, n)

    def beside(dw, dm, dn):
        return ((w + n_w + dw) % n_w, (m + n_m + dm) % n_m, (n + n_n + dn) % n_n)

    barrier = pltpu.get_barrier_semaphore()
    peers = [z_peer(k) for k in range(1, 4)] + [xc_peer(j) for j in range(1, 8)]
    peers += [beside(-1, 0, 0), beside(1, 0, 0)]
    peers += [beside(0, dm, dn) for dm in (-1, 0, 1) for dn in (-1, 0, 1) if (dm, dn) != (0, 0)]
    for peer in peers:
        pl.semaphore_signal(barrier, inc=1, device_id=peer, device_id_type=MESH)

    loads = [
        pltpu.make_async_copy(src, dst, load_sem.at[i])
        for i, (src, dst) in enumerate((
            (owner_in, owner), (slot_in, slot), (coef_in, coef), (melt_in, melt),
            (mold, near.at[0, pl.ds(WIDTH, cx)]), (cap, near.at[1, pl.ds(WIDTH, cx)]), (columns_in, columns),
            (self_in, selfb), (link_in, linkb), (logp, state), (target_in, target), (inflow_in, inflow),
        ))
    ]
    for load in loads:
        load.start()

    def remote(src, dst, sems, peer):
        return pltpu.make_async_remote_copy(
            src_ref=src, dst_ref=dst, send_sem=sems[0], recv_sem=sems[1],
            device_id=peer, device_id_type=MESH,
        )

    def wait_recv(region, sems):
        remote(region, region, sems, beside(0, 1, 0)).wait_recv()

    def z_sems(it, k):
        return (zsend_sem.at[it, k], zrecv_sem.at[it, k])

    def gather_sems(it, k):
        return (gsend_sem.at[it, k], grecv_sem.at[it, k])

    def gather_on(it, k):
        for j in TWO_HOPS_FIRST:
            remote(tab.at[it, k, 0], tab.at[it, k, j], gather_sems(it, k), xc_peer(j)).start()

    def gather_start(it):
        for k in FAR_FIRST:
            remote(tab.at[it, 0, 0], tab.at[it, k, 0], z_sems(it, k), z_peer(k)).start()

    def z_arrived(it, k):
        wait_recv(tab.at[it, k, 0], z_sems(it, k))
        gather_on(it, k)

    def cool(it):
        found = jnp.zeros((128, 256), F32)
        for k in (0, 1, 3, 2):
            wait_recv(tab.at[it, k, pl.ds(1, 7)], gather_sems(it, k))
            hi, lo = split_terms(tab[it, k].reshape(128, 128))
            found = found + jnp.dot(
                hot_t[:, k * 128:(k + 1) * 128], jnp.concatenate([hi, lo], axis=1), preferred_element_type=F32
            )
        found = (found[:, :128] + found[:, 128:]).T
        wall = jnp.where(half == 1, found[BLOCK:], found[:BLOCK])
        melt[...] = melt[...] - COOLING * (coef[...] * (melt[...] - wall))

    def scatter_sems(a, k):
        return (csend_sem.at[a, k], crecv_sem.at[a, k])

    def sum_sems(a, k):
        return (ysend_sem.at[a, k], yrecv_sem.at[a, k])

    sums = (pl.ds(0, 2), pl.ds(0, 1))

    def scatter_terms(values):
        parts = []
        for value in values:
            placed = jnp.concatenate([jnp.where(half == 0, value, 0.0), jnp.where(half == 1, value, 0.0)], axis=0)
            parts.extend(split_terms(placed))
        return jnp.concatenate(parts, axis=0)

    def scatter_fill(a, terms):
        for k in range(4):
            summed = lax.dot_general(
                hot[k * 128:(k + 1) * 128, :], terms, (((1,), (1,)), ((), ())), preferred_element_type=F32
            )
            for q in range(2):
                one = summed[:, 256 * q:256 * q + 128] + summed[:, 256 * q + 128:256 * q + 256]
                spread[a, k, :, q] = one.reshape(8, 16, 128)

    def scatter_start(a, k):
        for j in TWO_HOPS_FIRST:
            remote(spread.at[a, k, j], rs1.at[a, k, j], scatter_sems(a, k), xc_peer(j)).start()

    def scatter_on(a, k):
        wait_recv(rs1.at[a, k, pl.ds(1, 7)], scatter_sems(a, k))
        totals = []
        for q in range(2):
            total = spread[a, k, 0, q]
            for j in range(1, 8):
                total = total + rs1[a, k, j, q]
            totals.append(total)
        if a == 0:
            psum[a, k, 0], psum[a, k, 1] = totals
        else:
            psum[a, k, 0] = COOLING * (totals[0] - totals[1] * tab[0, k, 0])
        if k > 0:
            remote(psum.at[a, k, sums[a]], rs2.at[a, k, sums[a]], sum_sems(a, k), z_peer(k)).start()

    def scatter_done(a):
        for k in (1, 3, 2):
            wait_recv(rs2.at[a, k, sums[a]], sum_sems(a, k))
        return [
            ((psum[a, 0, q] + rs2[a, 1, q]) + (rs2[a, 3, q] + rs2[a, 2, q])) for q in range(2 - a)
        ]

    lane = lax.broadcasted_iota(jnp.int32, (cy, cz), 1)
    lane24 = lax.broadcasted_iota(jnp.int32, (24, cz), 1)
    row8 = lax.broadcasted_iota(jnp.int32, (8, cz), 0)
    lane8 = lax.broadcasted_iota(jnp.int32, (8, cz), 1)
    own_planes = list(range(WIDTH, WIDTH + cx))
    ghost_planes = list(range(WIDTH)) + list(range(WIDTH + cx, planes))
    arrays = ((0, 1), (2,))

    def h_sems(g, step, kind):
        return (hsend_sem.at[g, step, kind], hrecv_sem.at[g, step, kind])

    def group(g):
        return pl.ds(arrays[g][0], len(arrays[g]))

    def send_low(g):
        remote(
            near.at[group(g), pl.ds(WIDTH, WIDTH)], near.at[group(g), pl.ds(WIDTH + cx, WIDTH)],
            h_sems(g, 0, 0), beside(-1, 0, 0),
        ).start()

    def send_high(g):
        src = near.at[group(0), pl.ds(cx, WIDTH)] if g == 0 else plain.at[pl.ds(0, 1), pl.ds(cx - WIDTH, WIDTH)]
        remote(src, near.at[group(g), pl.ds(0, WIDTH)], h_sems(g, 0, 1), beside(1, 0, 0)).start()

    def pack_edges(g, step):
        which, row_out, lane_out = ((own_planes, row_own, lane_own), (ghost_planes, row_ghost, lane_ghost))[step]
        for a in arrays[g]:
            packed = jnp.zeros((cy, cz), F32)
            for q, p in enumerate(which):
                packed = jnp.where(lane // 8 == q, pltpu.roll(near[a, p], WIDTH + 8 * q, 1), packed)
            lane_out[a, 0] = packed[:8]
            lane_out[a, 1] = packed[8:]
            for t in range(len(which) // 2):
                q = 4 * (t // 2) + t % 2
                one, two = near[a, which[q]], near[a, which[q + 2]]
                row_out[a, 0, t] = jnp.where(row8 < WIDTH, one[:8], pltpu.roll(two[:8], 4, 0))
                row_out[a, 1, t] = jnp.where(row8 < WIDTH, pltpu.roll(one[8:], 4, 0), two[8:])

    def send_edges(g, step):
        row_out, lane_out, rows_in, lanes_in, corner_in = (
            (row_own, lane_own, rows_own, lanes_own, corner_own),
            (row_ghost, lane_ghost, rows_ghost, lanes_ghost, corner_ghost),
        )[step]
        some = group(g)
        for side, dm in ((0, -1), (1, 1)):
            remote(row_out.at[some, side], rows_in.at[some, side], h_sems(g, step, 2), beside(0, dm, 0)).start()
        for side, dn in ((0, -1), (1, 1)):
            remote(lane_out.at[some], lanes_in.at[some, side], h_sems(g, step, 3), beside(0, 0, dn)).start()
            for tile, dm in ((0, -1), (1, 1)):
                remote(
                    lane_out.at[some, tile], corner_in.at[some, side, tile], h_sems(g, step, 4), beside(0, dm, dn)
                ).start()

    def take_edges(g, step, places):
        which, rows_in, lanes_in, corner_in = (
            (own_planes, rows_own, lanes_own, corner_own), (ghost_planes, rows_ghost, lanes_ghost, corner_ghost),
        )[step]
        some = group(g)
        for kind, region in ((2, rows_in), (3, lanes_in), (4, corner_in)):
            wait_recv(region.at[some], h_sems(g, step, kind))
        for a, dst in zip(arrays[g], places):
            sides = []
            for side in range(2):
                corner = jnp.where(row8 < WIDTH, corner_in[a, side, 0], corner_in[a, side, 1])
                sides.append(jnp.concatenate([lanes_in[a, side, 0], lanes_in[a, side, 1], corner], axis=0))
            comb = jnp.where(lane24 % 8 >= WIDTH, sides[0], sides[1])
            for t in range(len(which) // 2):
                q = 4 * (t // 2) + t % 2
                after, before = rows_in[a, 0, t], rows_in[a, 1, t]
                ghosts = (
                    (q, jnp.where(row8 < WIDTH, after, pltpu.roll(before, 4, 0))),
                    (q + 2, jnp.where(row8 < WIDTH, pltpu.roll(after, 4, 0), before)),
                )
                for at, ghost in ghosts:
                    p = which[at]
                    dst[p, 0:cy, 0:cz] = near[a, p]
                    dst[p, cy:24, 0:cz] = ghost
                    dst[p, :, cz:2 * cz] = pltpu.roll(comb, cz - (8 * at + WIDTH), 1)

    def wide_arrived(g):
        wait_recv(near.at[group(g), pl.ds(WIDTH + cx, WIDTH)], h_sems(g, 0, 0))
        wait_recv(near.at[group(g), pl.ds(0, WIDTH)], h_sems(g, 0, 1))
        if g == 1:
            for p in range(3):
                near[2, p + 1] = near[2, p + 1] + lower[0, p]
        pack_edges(g, 1)
        send_edges(g, 1)

    def prepare(which):
        row_at = lax.broadcasted_iota(jnp.int32, (24, 2 * cz), 0)
        row_at = jnp.where(row_at < cy + WIDTH, row_at, row_at - 24) + m * cy
        lane_at = lax.broadcasted_iota(jnp.int32, (24, 2 * cz), 1)
        lane_real = (lane_at < cz + WIDTH) | (lane_at >= 2 * cz - WIDTH)
        lane_at = jnp.where(lane_at < cz + WIDTH, lane_at, lane_at - 2 * cz) + n * cz
        inside = lane_real & (row_at >= 0) & (row_at < n_m * cy) & (lane_at >= 0) & (lane_at < n_n * cz)
        inside = jnp.where(inside, 1.0, 0.0)
        for p in which:
            here = inside
            if p < WIDTH:
                here = jnp.where(w > 0, inside, 0.0)
            elif p >= WIDTH + cx:
                here = jnp.where(w < n_w - 1, inside, 0.0)
            capacity, start = inv[p], ext[0, p]
            base[p] = capacity * start
            inv[p] = here / (capacity + 6.0 * CONDUCT)
            ext[0, p] = jnp.where(here > 0.0, start, 0.0)

    def keep_inside(which):
        for p in which:
            ext[0, p] = jnp.where(inv[p] > 0.0, ext[0, p], 0.0)

    def around(plane):
        rows = pltpu.roll(plane, 1, 0) + pltpu.roll(plane, 23, 0)
        return rows + (pltpu.roll(plane, 1, 1) + pltpu.roll(plane, 2 * cz - 1, 1))

    def plain_sweeps(it, inner):
        for k in range(SWEEPS):
            now, later = k % 2, (k + 1) % 2
            edge = k + 1
            inside = range(edge + WIDTH, planes - edge - WIDTH)
            for p in inside if inner else [p for p in range(edge, planes - edge) if p not in inside]:
                total = (ext[now, p - 1] + ext[now, p + 1]) + around(ext[now, p]) + base[p]
                new = total * inv[p]
                if k == SWEEPS - 1:
                    plain[it, p - WIDTH] = new[:cy, :cz]
                else:
                    ext[later, p] = new

    def edge_sems(it, side):
        return (xsend_sem.at[it, side], xrecv_sem.at[it, side])

    def source_start(it, source):
        srcb[it, 0] = source[:8]
        srcb[it, 1] = source[8:]

        def send(side, parts):
            for src, place_at, count, dm, dn in parts:
                remote(
                    srcb.at[it, pl.ds(src, count)], src_in.at[it, pl.ds(place_at, count)],
                    edge_sems(it, side), beside(0, dm, dn),
                ).start()

        send(0, ((0, 0, 1, -1, 0), (1, 1, 1, 1, 0)))

        @pl.when(n > 0)
        def _():
            send(1, ((0, 2, 2, 0, -1), (0, 4, 1, -1, -1), (1, 5, 1, 1, -1)))

        @pl.when(n < n_n - 1)
        def _():
            send(2, ((0, 6, 2, 0, 1), (0, 8, 1, -1, 1), (1, 9, 1, 1, 1)))

    def source_done(it):
        wait_recv(src_in.at[it, pl.ds(0, 2)], edge_sems(it, 0))

        @pl.when(n < n_n - 1)
        def _():
            wait_recv(src_in.at[it, pl.ds(2, 4)], edge_sems(it, 1))

        @pl.when(n > 0)
        def _():
            wait_recv(src_in.at[it, pl.ds(6, 4)], edge_sems(it, 2))

        def corner(up, down):
            return jnp.where(row8 < WIDTH, src_in[it, up], src_in[it, down])

        def lanes(after, before):
            return jnp.where(lane8 < WIDTH, after, before)

        main = jnp.concatenate([srcb[it, 0], srcb[it, 1], corner(0, 1)], axis=0)
        sides = jnp.concatenate(
            [lanes(src_in[it, 2], src_in[it, 6]), lanes(src_in[it, 3], src_in[it, 7]), lanes(corner(4, 5), corner(8, 9))],
            axis=0,
        )
        return jnp.concatenate([main, sides], axis=1)

    def grown(wide_source, have, p):
        total = jnp.zeros((24, 2 * cz), F32)
        if p == 0:
            total = wide_source
        for q in (p - 1, p + 1):
            if q in have:
                total = total + have[q]
        if p in have:
            total = total + around(have[p])
        return total * inv[WIDTH + p]

    def first_sweeps(wide_source):
        one = {0: wide_source * inv[WIDTH]}
        two = {p: grown(wide_source, one, p) for p in (0, -1, 1)}
        three = {p: grown(wide_source, two, p) for p in (0, -1, 1)}
        wall = grown(wide_source, three, 0)[:cy, :cz]
        return two, three, wall

    def last_sweeps(it, wide_source, two, three):
        three.update({p: grown(wide_source, two, p) for p in (-2, 2)})
        for p in (-3, -2, -1):
            lower[it, p + 3] = grown(wide_source, three, p)[:cy, :cz]
        remote(lower.at[it], lower_in.at[it], (lsend_sem.at[it], lrecv_sem.at[it]), beside(-1, 0, 0)).start()
        return [grown(wide_source, three, p)[:cy, :cz] for p in (1, 2, 3)]

    def lower_arrived(it):
        wait_recv(lower_in.at[it], (lsend_sem.at[it], lrecv_sem.at[it]))

    def apply(v16):
        v = v16.astype(F32)
        linked = jnp.dot(v16, col_hot[...], preferred_element_type=F32)
        near0, near1 = linked[:, :128], linked[:, 128:]

        def rows(t, carry):
            sums = []
            for u in range(8):
                i = t * 8 + u
                prod = wide_blocks[0, i] * v + wide_blocks[1, i] * near0 + wide_blocks[2, i] * near1
                sums.append(jnp.sum(prod, axis=0, keepdims=True))
            kv[pl.ds(pl.multiple_of(t * 8, 8), 8), :] = jnp.concatenate(sums, axis=0)
            return carry

        lax.fori_loop(0, BLOCK // 8, rows, 0)
        return kv[...]

    def newton_start():
        mt, st = melt[...], state[...]
        bulk = BULK_BASE * jnp.exp(-BULK_SLOPE * mt)
        growth = jnp.exp(st)
        press = bulk * (growth - 1.0)
        base_volume = jnp.exp(EXPAND * mt)
        volume = base_volume * (1.0 - TAIT_C * st)
        sl = bulk * growth
        slope[...] = sl
        jd = diag[...] * sl + TAIT_C * base_volume
        jdiag[...] = jd
        rounded = press.astype(BF16)
        res = apply(rounded) + diag[...] * rounded.astype(F32) + (target[...] - volume) - inflow[...]
        resid[...] = res
        upd[...] = -res / jd

    def newton_step():
        weighted = (slope[...] * upd[...]).astype(BF16)
        upd[...] = (-resid[...] - apply(weighted)) / jdiag[...]

    def sends_left(it):
        def wait_send(region, sems):
            remote(region, region, sems, beside(0, 1, 0)).wait_send()

        for k in range(4):
            if k > 0:
                wait_send(tab.at[it, k, 0], z_sems(it, k))
                wait_send(psum.at[it, k, sums[it]], sum_sems(it, k))
            wait_send(tab.at[it, k, pl.ds(1, 7)], gather_sems(it, k))
            wait_send(spread.at[it, k, pl.ds(1, 7)], scatter_sems(it, k))
        wait_send(src_in.at[it, pl.ds(0, 2)], edge_sems(it, 0))

        @pl.when(n > 0)
        def _():
            wait_send(src_in.at[it, pl.ds(2, 4)], edge_sems(it, 1))

        @pl.when(n < n_n - 1)
        def _():
            wait_send(src_in.at[it, pl.ds(6, 4)], edge_sems(it, 2))

        wait_send(lower.at[it], (lsend_sem.at[it], lrecv_sem.at[it]))
        some = group(it)
        wait_send(near.at[some, pl.ds(0, WIDTH)], h_sems(it, 0, 0))
        wait_send(near.at[some, pl.ds(0, WIDTH)], h_sems(it, 0, 1))
        for step, regions in ((0, (rows_own, lanes_own, corner_own)), (1, (rows_ghost, lanes_ghost, corner_ghost))):
            for kind, region in enumerate(regions):
                wait_send(region.at[some], h_sems(it, step, 2 + kind))

    for load in loads[:4]:
        load.wait()
    rel = jnp.bitwise_xor(owner[...], w)
    place = rel * 16 + slot[...] // 2
    half = slot[...] % 2
    faces = lax.broadcasted_iota(jnp.int32, (512, 128), 0)
    hot32 = jnp.where(faces == place, 1.0, 0.0)
    hot[...] = hot32.astype(BF16)
    scatter_fill(0, scatter_terms((coef[...] * melt[...], coef[...])))
    for it in range(ITERS):
        src_in[it] = jnp.zeros((10, 8, cz), F32)
    loads[4].wait()
    loads[5].wait()
    tab[0, 0, 0] = near[0, WIDTH]
    pack_edges(0, 0)
    pl.semaphore_wait(barrier, len(peers))

    for k in FAR_FIRST:
        scatter_start(0, k)
    send_low(0)
    send_high(0)
    gather_start(0)
    send_edges(0, 0)
    scatter_start(0, 0)
    square = coef[...] * coef[...]
    scatter_fill(1, scatter_terms((square * melt[...], square)))
    for k in FAR_FIRST + (0,):
        scatter_start(1, k)
    hot_t[...] = hot32.T.astype(BF16)
    for load in loads[6:]:
        load.wait()
    froms = lax.broadcasted_iota(jnp.int32, (128, 128), 0)
    for k in range(2):
        col_hot[:, k * 128:(k + 1) * 128] = jnp.where(froms == columns[k:k + 1, :], 1.0, 0.0).astype(BF16)

    def pick(t, carry):
        sums = []
        for u in range(8):
            i = t * 8 + u
            mask = lax.broadcasted_iota(jnp.int32, (BLOCK, 128), 0) == i
            block = selfb[i].astype(F32)
            sums.append(jnp.sum(jnp.where(mask, block, 0.0), axis=0, keepdims=True))
            wide_blocks[0, i] = jnp.where(mask, 0.0, block)
            wide_blocks[1, i] = linkb[0, i].astype(F32)
            wide_blocks[2, i] = linkb[1, i].astype(F32)
        diag[pl.ds(pl.multiple_of(t * 8, 8), 8), :] = jnp.concatenate(sums, axis=0)
        return carry

    lax.fori_loop(0, BLOCK // 8, pick, 0)
    for k in FAR_FIRST:
        scatter_on(0, k)
    gather_on(0, 0)
    z_arrived(0, 1)
    z_arrived(0, 3)
    wide_arrived(0)
    take_edges(0, 0, (ext.at[0], inv))
    prepare(own_planes)
    scatter_on(0, 0)
    plain_sweeps(0, True)

    sum_a, sum_b = scatter_done(0)
    first_wall = near[0, WIDTH]
    source_start(0, sum_a - sum_b * first_wall)
    z_arrived(0, 2)
    take_edges(0, 1, (ext.at[0], inv))
    prepare(ghost_planes)
    plain_sweeps(0, False)
    send_high(1)
    for k in FAR_FIRST + (0,):
        scatter_on(1, k)
    spread_source = source_done(0)
    two, three, wall_part = first_sweeps(spread_source)
    second_wall = plain[0, 0] + wall_part
    tab[1, 0, 0] = second_wall
    gather_start(1)
    gather_on(1, 0)
    upper = last_sweeps(0, spread_source, two, three)
    near[2, WIDTH] = second_wall
    for p in range(1, 4):
        near[2, WIDTH + p] = plain[0, p] + upper[p - 1]
    send_low(1)
    for p in range(4, cx - 3):
        near[2, WIDTH + p] = plain[0, p]

    cool(0)
    newton_start()
    z_arrived(1, 1)
    z_arrived(1, 3)
    (cooled,) = scatter_done(1)
    source_start(1, (sum_a - cooled) - sum_b * second_wall)
    lower_arrived(0)
    for p in range(3):
        near[2, WIDTH + cx - 3 + p] = plain[0, cx - 3 + p] + lower_in[0, p]
    pack_edges(1, 0)
    send_edges(1, 0)
    newton_step()
    z_arrived(1, 2)
    wide_arrived(1)
    newton_step()
    state[...] = state[...] + upd[...]
    spread_source = source_done(1)
    two, three, wall_part = first_sweeps(spread_source)
    upper = last_sweeps(1, spread_source, two, three)
    take_edges(1, 0, (ext.at[0],))
    keep_inside(own_planes)
    plain_sweeps(1, True)
    sends_left(0)

    cool(1)
    newton_start()
    take_edges(1, 1, (ext.at[0],))
    keep_inside(ghost_planes)
    plain_sweeps(1, False)
    out_field[0] = plain[1, 0] + wall_part
    for p in range(1, 4):
        out_field[p] = plain[1, p] + upper[p - 1]
    for p in range(4, cx - 3):
        out_field[p] = plain[1, p]
    newton_step()
    lower_arrived(1)
    for p in range(3):
        out_field[cx - 3 + p] = plain[1, cx - 3 + p] + lower_in[1, p]
    newton_step()
    out_melt[...] = melt[...]
    out_state[...] = state[...] + upd[...]
    sends_left(1)


def per_device(
    mold_temp, capacity, melt_temp, log_pressure, target_volume, inflow, self_blocks, link_blocks,
    link_columns, wall_owner, wall_slot, transfer_coef,
):
    cx, cy, cz = mold_temp.shape
    cells, blocks = melt_temp.shape
    planes = cx + 2 * WIDTH
    vmem = pl.BlockSpec(memory_space=pltpu.VMEM)
    hbm = pl.BlockSpec(memory_space=pltpu.HBM)

    def scratch(*shape):
        return pltpu.VMEM(shape, F32)

    cav = scratch(cells, blocks)
    field, melt, state = pl.pallas_call(
        kernel,
        out_shape=(
            pltpu.VMEM(mold_temp.shape, F32),
            pltpu.VMEM(melt_temp.shape, F32),
            pltpu.VMEM(melt_temp.shape, F32),
        ),
        in_specs=[hbm] * 12,
        out_specs=(vmem, vmem, vmem),
        scratch_shapes=[
            pltpu.VMEM(self_blocks.shape, BF16),
            pltpu.VMEM(link_blocks.shape, BF16),
            scratch(3, *self_blocks.shape),
            scratch(ITERS, 4, 8, 16, 128),
            scratch(2, 4, 8, 2, 16, 128),
            scratch(2, 4, 8, 2, 16, 128),
            scratch(2, 4, 2, 16, 128),
            scratch(2, 4, 2, 16, 128),
            scratch(3, planes, cy, cz),
            scratch(3, 2, 8, 8, cz),
            scratch(3, 2, 4, 8, cz),
            scratch(3, 2, 8, cz),
            scratch(3, 2, 8, cz),
            scratch(3, 2, 8, 8, cz),
            scratch(3, 2, 4, 8, cz),
            scratch(3, 2, 2, 8, cz),
            scratch(3, 2, 2, 8, cz),
            scratch(3, 2, 2, 8, cz),
            scratch(3, 2, 2, 8, cz),
            scratch(2, planes, 24, 2 * cz),
            scratch(planes, 24, 2 * cz),
            scratch(planes, 24, 2 * cz),
            scratch(ITERS, cx, cy, cz),
            scratch(ITERS, 2, 8, cz),
            scratch(ITERS, 10, 8, cz),
            scratch(ITERS, 3, cy, cz),
            scratch(ITERS, 3, cy, cz),
            pltpu.VMEM((512, 128), BF16),
            pltpu.VMEM((128, 512), BF16),
            pltpu.VMEM((128, 256), BF16),
            cav, cav, cav, cav, cav, cav, cav, cav, cav, cav, cav,
            pltpu.VMEM((2, blocks), jnp.int32),
            pltpu.VMEM((1, blocks), jnp.int32),
            pltpu.VMEM((1, blocks), jnp.int32),
            pltpu.SemaphoreType.DMA((12,)),
            *[pltpu.SemaphoreType.DMA((ITERS, 4))] * 8,
            *[pltpu.SemaphoreType.DMA((ITERS, 3))] * 2,
            *[pltpu.SemaphoreType.DMA((ITERS,))] * 2,
            *[pltpu.SemaphoreType.DMA((2, 2, 5))] * 2,
        ],
        compiler_params=pltpu.CompilerParams(
            collective_id=0, has_side_effects=True, vmem_limit_bytes=56 * 1024 * 1024
        ),
    )(
        mold_temp, capacity, melt_temp, log_pressure, target_volume, inflow, transfer_coef,
        link_columns, wall_owner.reshape(1, blocks), wall_slot.reshape(1, blocks), self_blocks, link_blocks,
    )
    pressure = BULK_BASE * jnp.exp(-BULK_SLOPE * melt) * (jnp.exp(state) - 1.0)
    shrinkage = 1.0 - jnp.exp(EXPAND * melt) * (1.0 - TAIT_C * state)
    return field, pressure, shrinkage


def solution(mesh):
    cavity = P(None, ("wide", "mid", "narrow"))
    brick = P("wide", "mid", "narrow")
    flat = P(("wide", "mid", "narrow"))
    return jax.shard_map(
        per_device,
        mesh=mesh,
        in_specs=(
            brick, brick, cavity, cavity, cavity, cavity,
            P(None, None, ("wide", "mid", "narrow")),
            P(None, None, None, ("wide", "mid", "narrow")),
            cavity, flat, flat, cavity,
        ),
        out_specs=(brick, cavity, cavity),
        check_vma=False,
    )
```

```python
import functools

import jax
import jax.numpy as jnp
from jax import lax
from jax.experimental import pallas as pl
from jax.experimental.pallas import tpu as pltpu
from jax.sharding import PartitionSpec as P

BLOCK = 64
ITERS = 2
SWEEPS = 4
INNER = 2
WIDTH = 4
FAR_FIRST = (2, 1, 3)
TWO_HOPS_FIRST = (4, 5, 2, 3, 6, 7, 1)

CONDUCT = 1.0
COOLING = 0.5
TAIT_C = 0.3
EXPAND = 0.25
BULK_BASE = 0.5
BULK_SLOPE = 0.3

MESH = pl.DeviceIdType.MESH
F32 = jnp.float32
BF16 = jnp.bfloat16


def flip(v, k):
    if k == 0:
        return v
    if k == 1:
        return v + 1 - 2 * (v % 2)
    if k == 2:
        return (v + 2) % 4
    return 3 - v


def split_terms(x):
    hi = x.astype(BF16)
    lo = (x - hi.astype(F32)).astype(BF16)
    return hi, lo


def kernel(
    mold, cap, melt_in, logp, target_in, inflow_in, coef_in, columns_in, owner_in, slot_in, self_in, link_in,
    out_field, out_melt, out_state,
    selfb, linkb, wide_blocks, tab, spread, rs1, psum, rs2, near,
    row_own, row_ghost, lane_own, lane_ghost, rows_own, rows_ghost, lanes_own, lanes_ghost, corner_own, corner_ghost,
    ext, inv, base, plain, srcb, src_in, lower, lower_in,
    hot, hot_t, col_hot, diag, kv, resid, jdiag, slope, upd, state, melt, target, inflow, coef,
    columns, owner, slot,
    load_sem, zsend_sem, zrecv_sem, gsend_sem, grecv_sem, csend_sem, crecv_sem, ysend_sem, yrecv_sem,
    xsend_sem, xrecv_sem, lsend_sem, lrecv_sem, hsend_sem, hrecv_sem,
):
    cx, cy, cz = mold.shape
    planes = near.shape[1]
    w = lax.axis_index("wide")
    m = lax.axis_index("mid")
    n = lax.axis_index("narrow")
    n_w, n_m, n_n = lax.axis_size("wide"), lax.axis_size("mid"), lax.axis_size("narrow")
    zh, x, c = w // 8, (w // 2) % 4, w % 2

    def z_peer(k):
        return (flip(zh, k) * 8 + x * 2 + c, m, n)

    def xc_peer(j):
        return (zh * 8 + flip(x, j // 2) * 2 + flip(c, j % 2), m, n)

    def beside(dw, dm, dn):
        return ((w + n_w + dw) % n_w, (m + n_m + dm) % n_m, (n + n_n + dn) % n_n)

    for edge in (lanes_own, lanes_ghost, corner_own, corner_ghost):
        for a in range(3):
            edge[a] = jnp.zeros((2, 2, 8, cz), F32)
    barrier = pltpu.get_barrier_semaphore()
    peers = [z_peer(k) for k in range(1, 4)] + [xc_peer(j) for j in range(1, 8)]
    peers += [beside(-1, 0, 0), beside(1, 0, 0)]
    peers += [beside(0, dm, dn) for dm in (-1, 0, 1) for dn in (-1, 0, 1) if (dm, dn) != (0, 0)]
    for peer in peers:
        pl.semaphore_signal(barrier, inc=1, device_id=peer, device_id_type=MESH)

    loads = [
        pltpu.make_async_copy(src, dst, load_sem.at[i])
        for i, (src, dst) in enumerate((
            (owner_in, owner), (slot_in, slot), (coef_in, coef), (melt_in, melt),
            (mold, near.at[0, pl.ds(WIDTH, cx)]), (cap, near.at[1, pl.ds(WIDTH, cx)]), (columns_in, columns),
            (self_in, selfb), (link_in, linkb), (logp, state), (target_in, target), (inflow_in, inflow),
        ))
    ]
    for load in loads:
        load.start()

    def remote(src, dst, sems, peer):
        return pltpu.make_async_remote_copy(
            src_ref=src, dst_ref=dst, send_sem=sems[0], recv_sem=sems[1],
            device_id=peer, device_id_type=MESH,
        )

    def wait_recv(region, sems):
        remote(region, region, sems, beside(0, 1, 0)).wait_recv()

    def z_sems(it, k):
        return (zsend_sem.at[it, k], zrecv_sem.at[it, k])

    def gather_sems(it, k):
        return (gsend_sem.at[it, k], grecv_sem.at[it, k])

    def gather_on(it, k):
        for j in TWO_HOPS_FIRST:
            remote(tab.at[it, k, 0], tab.at[it, k, j], gather_sems(it, k), xc_peer(j)).start()

    def gather_start(it):
        for k in FAR_FIRST:
            remote(tab.at[it, 0, 0], tab.at[it, k, 0], z_sems(it, k), z_peer(k)).start()

    def z_arrived(it, k):
        wait_recv(tab.at[it, k, 0], z_sems(it, k))
        gather_on(it, k)

    def cool(it):
        found = jnp.zeros((128, 256), F32)
        for k in (0, 1, 3, 2):
            wait_recv(tab.at[it, k, pl.ds(1, 7)], gather_sems(it, k))
            hi, lo = split_terms(tab[it, k].reshape(128, 128))
            found = found + jnp.dot(
                hot_t[:, k * 128:(k + 1) * 128], jnp.concatenate([hi, lo], axis=1), preferred_element_type=F32
            )
        found = (found[:, :128] + found[:, 128:]).T
        wall = jnp.where(half == 1, found[BLOCK:], found[:BLOCK])
        melt[...] = melt[...] - COOLING * (coef[...] * (melt[...] - wall))

    def scatter_sems(a, k):
        return (csend_sem.at[a, k], crecv_sem.at[a, k])

    def sum_sems(a, k):
        return (ysend_sem.at[a, k], yrecv_sem.at[a, k])

    sums = (pl.ds(0, 2), pl.ds(0, 1))

    def scatter_terms(values):
        parts = []
        for value in values:
            placed = jnp.concatenate([jnp.where(half == 0, value, 0.0), jnp.where(half == 1, value, 0.0)], axis=0)
            parts.extend(split_terms(placed))
        return jnp.concatenate(parts, axis=0)

    def scatter_fill(a, terms):
        for k in range(4):
            summed = lax.dot_general(
                hot[k * 128:(k + 1) * 128, :], terms, (((1,), (1,)), ((), ())), preferred_element_type=F32
            )
            for q in range(2):
                one = summed[:, 256 * q:256 * q + 128] + summed[:, 256 * q + 128:256 * q + 256]
                spread[a, k, :, q] = one.reshape(8, 16, 128)

    def scatter_start(a, k):
        for j in TWO_HOPS_FIRST:
            remote(spread.at[a, k, j], rs1.at[a, k, j], scatter_sems(a, k), xc_peer(j)).start()

    def scatter_on(a, k):
        wait_recv(rs1.at[a, k, pl.ds(1, 7)], scatter_sems(a, k))
        totals = []
        for q in range(2):
            total = spread[a, k, 0, q]
            for j in range(1, 8):
                total = total + rs1[a, k, j, q]
            totals.append(total)
        if a == 0:
            psum[a, k, 0], psum[a, k, 1] = totals
        else:
            psum[a, k, 0] = COOLING * (totals[0] - totals[1] * tab[0, k, 0])
        if k > 0:
            remote(psum.at[a, k, sums[a]], rs2.at[a, k, sums[a]], sum_sems(a, k), z_peer(k)).start()

    def scatter_done(a):
        for k in (1, 3, 2):
            wait_recv(rs2.at[a, k, sums[a]], sum_sems(a, k))
        return [
            ((psum[a, 0, q] + rs2[a, 1, q]) + (rs2[a, 3, q] + rs2[a, 2, q])) for q in range(2 - a)
        ]

    lane = lax.broadcasted_iota(jnp.int32, (cy, cz), 1)
    lane24 = lax.broadcasted_iota(jnp.int32, (24, cz), 1)
    row8 = lax.broadcasted_iota(jnp.int32, (8, cz), 0)
    lane8 = lax.broadcasted_iota(jnp.int32, (8, cz), 1)
    own_planes = list(range(WIDTH, WIDTH + cx))
    ghost_planes = list(range(WIDTH)) + list(range(WIDTH + cx, planes))
    arrays = ((0, 1), (2,))

    def h_sems(g, step, kind):
        return (hsend_sem.at[g, step, kind], hrecv_sem.at[g, step, kind])

    def group(g):
        return pl.ds(arrays[g][0], len(arrays[g]))

    def send_low(g):
        remote(
            near.at[group(g), pl.ds(WIDTH, WIDTH)], near.at[group(g), pl.ds(WIDTH + cx, WIDTH)],
            h_sems(g, 0, 0), beside(-1, 0, 0),
        ).start()

    def send_high(g):
        src = near.at[group(0), pl.ds(cx, WIDTH)] if g == 0 else plain.at[pl.ds(0, 1), pl.ds(cx - WIDTH, WIDTH)]
        remote(src, near.at[group(g), pl.ds(0, WIDTH)], h_sems(g, 0, 1), beside(1, 0, 0)).start()

    def pack_edges(g, step):
        which, row_out, lane_out = ((own_planes, row_own, lane_own), (ghost_planes, row_ghost, lane_ghost))[step]
        for a in arrays[g]:
            packed = jnp.zeros((cy, cz), F32)
            for q, p in enumerate(which):
                packed = jnp.where(lane // 8 == q, pltpu.roll(near[a, p], WIDTH + 8 * q, 1), packed)
            lane_out[a, 0] = packed[:8]
            lane_out[a, 1] = packed[8:]
            for t in range(len(which) // 2):
                q = 4 * (t // 2) + t % 2
                one, two = near[a, which[q]], near[a, which[q + 2]]
                row_out[a, 0, t] = jnp.where(row8 < WIDTH, one[:8], pltpu.roll(two[:8], 4, 0))
                row_out[a, 1, t] = jnp.where(row8 < WIDTH, pltpu.roll(one[8:], 4, 0), two[8:])

    def send_edges(g, step):
        row_out, lane_out, rows_in, lanes_in, corner_in = (
            (row_own, lane_own, rows_own, lanes_own, corner_own),
            (row_ghost, lane_ghost, rows_ghost, lanes_ghost, corner_ghost),
        )[step]
        some = group(g)
        for side, dm in ((0, -1), (1, 1)):
            remote(row_out.at[some, side], rows_in.at[some, side], h_sems(g, step, 2), beside(0, dm, 0)).start()

        def send_lanes(side, dn):
            remote(lane_out.at[some], lanes_in.at[some, side], h_sems(g, step, 3 + 2 * side), beside(0, 0, dn)).start()
            for tile, dm in ((0, -1), (1, 1)):
                remote(
                    lane_out.at[some, tile], corner_in.at[some, side, tile], h_sems(g, step, 4 + 2 * side), beside(0, dm, dn)
                ).start()

        @pl.when(n > 0)
        def _():
            send_lanes(0, -1)

        @pl.when(n < n_n - 1)
        def _():
            send_lanes(1, 1)

    def take_edges(g, step, places):
        which, rows_in, lanes_in, corner_in = (
            (own_planes, rows_own, lanes_own, corner_own), (ghost_planes, rows_ghost, lanes_ghost, corner_ghost),
        )[step]
        some = group(g)
        wait_recv(rows_in.at[some], h_sems(g, step, 2))

        def wait_lanes(side):
            wait_recv(lanes_in.at[some, side], h_sems(g, step, 3 + 2 * side))
            wait_recv(corner_in.at[some, side], h_sems(g, step, 4 + 2 * side))

        @pl.when(n < n_n - 1)
        def _():
            wait_lanes(0)

        @pl.when(n > 0)
        def _():
            wait_lanes(1)

        for a, dst in zip(arrays[g], places):
            sides = []
            for side in range(2):
                corner = jnp.where(row8 < WIDTH, corner_in[a, side, 0], corner_in[a, side, 1])
                sides.append(jnp.concatenate([lanes_in[a, side, 0], lanes_in[a, side, 1], corner], axis=0))
            comb = jnp.where(lane24 % 8 >= WIDTH, sides[0], sides[1])
            for t in range(len(which) // 2):
                q = 4 * (t // 2) + t % 2
                after, before = rows_in[a, 0, t], rows_in[a, 1, t]
                ghosts = (
                    (q, jnp.where(row8 < WIDTH, after, pltpu.roll(before, 4, 0))),
                    (q + 2, jnp.where(row8 < WIDTH, pltpu.roll(after, 4, 0), before)),
                )
                for at, ghost in ghosts:
                    p = which[at]
                    dst[p, 0:cy, 0:cz] = near[a, p]
                    dst[p, cy:24, 0:cz] = ghost
                    dst[p, :, cz:2 * cz] = pltpu.roll(comb, cz - (8 * at + WIDTH), 1)

    def wide_arrived(g):
        wait_recv(near.at[group(g), pl.ds(WIDTH + cx, WIDTH)], h_sems(g, 0, 0))
        wait_recv(near.at[group(g), pl.ds(0, WIDTH)], h_sems(g, 0, 1))
        if g == 1:
            for p in range(3):
                near[2, p + 1] = near[2, p + 1] + lower[0, p]
        pack_edges(g, 1)
        send_edges(g, 1)

    def prepare(which):
        row_at = lax.broadcasted_iota(jnp.int32, (24, 2 * cz), 0)
        row_at = jnp.where(row_at < cy + WIDTH, row_at, row_at - 24) + m * cy
        lane_at = lax.broadcasted_iota(jnp.int32, (24, 2 * cz), 1)
        lane_real = (lane_at < cz + WIDTH) | (lane_at >= 2 * cz - WIDTH)
        lane_at = jnp.where(lane_at < cz + WIDTH, lane_at, lane_at - 2 * cz) + n * cz
        inside = lane_real & (row_at >= 0) & (row_at < n_m * cy) & (lane_at >= 0) & (lane_at < n_n * cz)
        inside = jnp.where(inside, 1.0, 0.0)
        for p in which:
            here = inside
            if p < WIDTH:
                here = jnp.where(w > 0, inside, 0.0)
            elif p >= WIDTH + cx:
                here = jnp.where(w < n_w - 1, inside, 0.0)
            capacity, start = inv[p], ext[0, p]
            base[p] = capacity * start
            inv[p] = here / (capacity + 6.0 * CONDUCT)
            ext[0, p] = jnp.where(here > 0.0, start, 0.0)

    def keep_inside(which):
        for p in which:
            ext[0, p] = jnp.where(inv[p] > 0.0, ext[0, p], 0.0)

    def around(plane):
        rows = pltpu.roll(plane, 1, 0) + pltpu.roll(plane, 23, 0)
        return rows + (pltpu.roll(plane, 1, 1) + pltpu.roll(plane, 2 * cz - 1, 1))

    def plain_sweeps(it, inner):
        for k in range(SWEEPS):
            now, later = k % 2, (k + 1) % 2
            edge = k + 1
            inside = range(edge + WIDTH, planes - edge - WIDTH)
            for p in inside if inner else [p for p in range(edge, planes - edge) if p not in inside]:
                total = (ext[now, p - 1] + ext[now, p + 1]) + around(ext[now, p]) + base[p]
                new = total * inv[p]
                if k == SWEEPS - 1:
                    plain[it, p - WIDTH] = new[:cy, :cz]
                else:
                    ext[later, p] = new

    def edge_sems(it, side):
        return (xsend_sem.at[it, side], xrecv_sem.at[it, side])

    def source_start(it, source):
        srcb[it, 0] = source[:8]
        srcb[it, 1] = source[8:]

        def send(side, parts):
            for src, place_at, count, dm, dn in parts:
                remote(
                    srcb.at[it, pl.ds(src, count)], src_in.at[it, pl.ds(place_at, count)],
                    edge_sems(it, side), beside(0, dm, dn),
                ).start()

        send(0, ((0, 0, 1, -1, 0), (1, 1, 1, 1, 0)))

        @pl.when(n > 0)
        def _():
            send(1, ((0, 2, 2, 0, -1), (0, 4, 1, -1, -1), (1, 5, 1, 1, -1)))

        @pl.when(n < n_n - 1)
        def _():
            send(2, ((0, 6, 2, 0, 1), (0, 8, 1, -1, 1), (1, 9, 1, 1, 1)))

    def source_done(it):
        wait_recv(src_in.at[it, pl.ds(0, 2)], edge_sems(it, 0))

        @pl.when(n < n_n - 1)
        def _():
            wait_recv(src_in.at[it, pl.ds(2, 4)], edge_sems(it, 1))

        @pl.when(n > 0)
        def _():
            wait_recv(src_in.at[it, pl.ds(6, 4)], edge_sems(it, 2))

        def corner(up, down):
            return jnp.where(row8 < WIDTH, src_in[it, up], src_in[it, down])

        def lanes(after, before):
            return jnp.where(lane8 < WIDTH, after, before)

        main = jnp.concatenate([srcb[it, 0], srcb[it, 1], corner(0, 1)], axis=0)
        sides = jnp.concatenate(
            [lanes(src_in[it, 2], src_in[it, 6]), lanes(src_in[it, 3], src_in[it, 7]), lanes(corner(4, 5), corner(8, 9))],
            axis=0,
        )
        return jnp.concatenate([main, sides], axis=1)

    def grown(wide_source, have, p):
        total = jnp.zeros((24, 2 * cz), F32)
        if p == 0:
            total = wide_source
        for q in (p - 1, p + 1):
            if q in have:
                total = total + have[q]
        if p in have:
            total = total + around(have[p])
        return total * inv[WIDTH + p]

    def first_sweeps(wide_source):
        one = {0: wide_source * inv[WIDTH]}
        two = {p: grown(wide_source, one, p) for p in (0, -1, 1)}
        three = {p: grown(wide_source, two, p) for p in (0, -1, 1)}
        wall = grown(wide_source, three, 0)[:cy, :cz]
        return two, three, wall

    def last_sweeps(it, wide_source, two, three):
        three.update({p: grown(wide_source, two, p) for p in (-2, 2)})
        for p in (-3, -2, -1):
            lower[it, p + 3] = grown(wide_source, three, p)[:cy, :cz]
        remote(lower.at[it], lower_in.at[it], (lsend_sem.at[it], lrecv_sem.at[it]), beside(-1, 0, 0)).start()
        return [grown(wide_source, three, p)[:cy, :cz] for p in (1, 2, 3)]

    def lower_arrived(it):
        wait_recv(lower_in.at[it], (lsend_sem.at[it], lrecv_sem.at[it]))

    def apply(v16):
        v = v16.astype(F32)
        linked = jnp.dot(v16, col_hot[...], preferred_element_type=F32)
        near0, near1 = linked[:, :128], linked[:, 128:]

        def rows(t, carry):
            sums = []
            for u in range(8):
                i = t * 8 + u
                prod = wide_blocks[0, i] * v + wide_blocks[1, i] * near0 + wide_blocks[2, i] * near1
                sums.append(jnp.sum(prod, axis=0, keepdims=True))
            kv[pl.ds(pl.multiple_of(t * 8, 8), 8), :] = jnp.concatenate(sums, axis=0)
            return carry

        lax.fori_loop(0, BLOCK // 8, rows, 0)
        return kv[...]

    def newton_start():
        mt, st = melt[...], state[...]
        bulk = BULK_BASE * jnp.exp(-BULK_SLOPE * mt)
        growth = jnp.exp(st)
        press = bulk * (growth - 1.0)
        base_volume = jnp.exp(EXPAND * mt)
        volume = base_volume * (1.0 - TAIT_C * st)
        sl = bulk * growth
        slope[...] = sl
        jd = diag[...] * sl + TAIT_C * base_volume
        jdiag[...] = jd
        rounded = press.astype(BF16)
        res = apply(rounded) + diag[...] * rounded.astype(F32) + (target[...] - volume) - inflow[...]
        resid[...] = res
        upd[...] = -res / jd

    def newton_step():
        weighted = (slope[...] * upd[...]).astype(BF16)
        upd[...] = (-resid[...] - apply(weighted)) / jdiag[...]

    def sends_left(it):
        def wait_send(region, sems):
            remote(region, region, sems, beside(0, 1, 0)).wait_send()

        for k in range(4):
            if k > 0:
                wait_send(tab.at[it, k, 0], z_sems(it, k))
                wait_send(psum.at[it, k, sums[it]], sum_sems(it, k))
            wait_send(tab.at[it, k, pl.ds(1, 7)], gather_sems(it, k))
            wait_send(spread.at[it, k, pl.ds(1, 7)], scatter_sems(it, k))
        wait_send(src_in.at[it, pl.ds(0, 2)], edge_sems(it, 0))

        @pl.when(n > 0)
        def _():
            wait_send(src_in.at[it, pl.ds(2, 4)], edge_sems(it, 1))

        @pl.when(n < n_n - 1)
        def _():
            wait_send(src_in.at[it, pl.ds(6, 4)], edge_sems(it, 2))

        wait_send(lower.at[it], (lsend_sem.at[it], lrecv_sem.at[it]))
        some = group(it)
        wait_send(near.at[some, pl.ds(0, WIDTH)], h_sems(it, 0, 0))
        wait_send(near.at[some, pl.ds(0, WIDTH)], h_sems(it, 0, 1))
        for step, regions in ((0, (rows_own, lanes_own, corner_own)), (1, (rows_ghost, lanes_ghost, corner_ghost))):
            rows, lanes, corner = regions
            wait_send(rows.at[some], h_sems(it, step, 2))
            for side, sent in ((0, n > 0), (1, n < n_n - 1)):

                @pl.when(sent)
                def _(step=step, lanes=lanes, corner=corner, side=side):
                    wait_send(lanes.at[some, side], h_sems(it, step, 3 + 2 * side))
                    wait_send(corner.at[some, side], h_sems(it, step, 4 + 2 * side))

    for load in loads[:4]:
        load.wait()
    rel = jnp.bitwise_xor(owner[...], w)
    place = rel * 16 + slot[...] // 2
    half = slot[...] % 2
    faces = lax.broadcasted_iota(jnp.int32, (512, 128), 0)
    hot32 = jnp.where(faces == place, 1.0, 0.0)
    hot[...] = hot32.astype(BF16)
    scatter_fill(0, scatter_terms((coef[...] * melt[...], coef[...])))
    for it in range(ITERS):
        src_in[it] = jnp.zeros((10, 8, cz), F32)
    loads[4].wait()
    loads[5].wait()
    tab[0, 0, 0] = near[0, WIDTH]
    pack_edges(0, 0)
    pl.semaphore_wait(barrier, len(peers))

    for k in FAR_FIRST:
        scatter_start(0, k)
    send_low(0)
    send_high(0)
    gather_start(0)
    send_edges(0, 0)
    scatter_start(0, 0)
    square = coef[...] * coef[...]
    scatter_fill(1, scatter_terms((square * melt[...], square)))
    for k in FAR_FIRST + (0,):
        scatter_start(1, k)
    hot_t[...] = hot32.T.astype(BF16)
    for load in loads[6:]:
        load.wait()
    froms = lax.broadcasted_iota(jnp.int32, (128, 128), 0)
    for k in range(2):
        col_hot[:, k * 128:(k + 1) * 128] = jnp.where(froms == columns[k:k + 1, :], 1.0, 0.0).astype(BF16)

    def pick(t, carry):
        sums = []
        for u in range(8):
            i = t * 8 + u
            mask = lax.broadcasted_iota(jnp.int32, (BLOCK, 128), 0) == i
            block = selfb[i].astype(F32)
            sums.append(jnp.sum(jnp.where(mask, block, 0.0), axis=0, keepdims=True))
            wide_blocks[0, i] = jnp.where(mask, 0.0, block)
            wide_blocks[1, i] = linkb[0, i].astype(F32)
            wide_blocks[2, i] = linkb[1, i].astype(F32)
        diag[pl.ds(pl.multiple_of(t * 8, 8), 8), :] = jnp.concatenate(sums, axis=0)
        return carry

    lax.fori_loop(0, BLOCK // 8, pick, 0)
    for k in FAR_FIRST:
        scatter_on(0, k)
    gather_on(0, 0)
    z_arrived(0, 1)
    z_arrived(0, 3)
    wide_arrived(0)
    take_edges(0, 0, (ext.at[0], inv))
    prepare(own_planes)
    scatter_on(0, 0)
    plain_sweeps(0, True)

    sum_a, sum_b = scatter_done(0)
    first_wall = near[0, WIDTH]
    source_start(0, sum_a - sum_b * first_wall)
    z_arrived(0, 2)
    take_edges(0, 1, (ext.at[0], inv))
    prepare(ghost_planes)
    plain_sweeps(0, False)
    send_high(1)
    for k in FAR_FIRST + (0,):
        scatter_on(1, k)
    spread_source = source_done(0)
    two, three, wall_part = first_sweeps(spread_source)
    second_wall = plain[0, 0] + wall_part
    tab[1, 0, 0] = second_wall
    gather_start(1)
    gather_on(1, 0)
    upper = last_sweeps(0, spread_source, two, three)
    near[2, WIDTH] = second_wall
    for p in range(1, 4):
        near[2, WIDTH + p] = plain[0, p] + upper[p - 1]
    send_low(1)
    for p in range(4, cx - 3):
        near[2, WIDTH + p] = plain[0, p]

    cool(0)
    newton_start()
    z_arrived(1, 1)
    z_arrived(1, 3)
    newton_step()
    (cooled,) = scatter_done(1)
    source_start(1, (sum_a - cooled) - sum_b * second_wall)
    lower_arrived(0)
    for p in range(3):
        near[2, WIDTH + cx - 3 + p] = plain[0, cx - 3 + p] + lower_in[0, p]
    pack_edges(1, 0)
    send_edges(1, 0)
    z_arrived(1, 2)
    wide_arrived(1)
    newton_step()
    state[...] = state[...] + upd[...]
    spread_source = source_done(1)
    two, three, wall_part = first_sweeps(spread_source)
    upper = last_sweeps(1, spread_source, two, three)
    take_edges(1, 0, (ext.at[0],))
    keep_inside(own_planes)
    plain_sweeps(1, True)
    sends_left(0)

    cool(1)
    newton_start()
    take_edges(1, 1, (ext.at[0],))
    keep_inside(ghost_planes)
    plain_sweeps(1, False)
    out_field[0] = plain[1, 0] + wall_part
    for p in range(1, 4):
        out_field[p] = plain[1, p] + upper[p - 1]
    for p in range(4, cx - 3):
        out_field[p] = plain[1, p]
    newton_step()
    newton_step()
    out_melt[...] = melt[...]
    out_state[...] = state[...] + upd[...]
    lower_arrived(1)
    for p in range(3):
        out_field[cx - 3 + p] = plain[1, cx - 3 + p] + lower_in[1, p]
    sends_left(1)


def per_device(
    mold_temp, capacity, melt_temp, log_pressure, target_volume, inflow, self_blocks, link_blocks,
    link_columns, wall_owner, wall_slot, transfer_coef,
):
    cx, cy, cz = mold_temp.shape
    cells, blocks = melt_temp.shape
    planes = cx + 2 * WIDTH
    vmem = pl.BlockSpec(memory_space=pltpu.VMEM)
    hbm = pl.BlockSpec(memory_space=pltpu.HBM)

    def scratch(*shape):
        return pltpu.VMEM(shape, F32)

    cav = scratch(cells, blocks)
    field, melt, state = pl.pallas_call(
        kernel,
        out_shape=(
            pltpu.VMEM(mold_temp.shape, F32),
            pltpu.VMEM(melt_temp.shape, F32),
            pltpu.VMEM(melt_temp.shape, F32),
        ),
        in_specs=[hbm] * 12,
        out_specs=(vmem, vmem, vmem),
        scratch_shapes=[
            pltpu.VMEM(self_blocks.shape, BF16),
            pltpu.VMEM(link_blocks.shape, BF16),
            scratch(3, *self_blocks.shape),
            scratch(ITERS, 4, 8, 16, 128),
            scratch(2, 4, 8, 2, 16, 128),
            scratch(2, 4, 8, 2, 16, 128),
            scratch(2, 4, 2, 16, 128),
            scratch(2, 4, 2, 16, 128),
            scratch(3, planes, cy, cz),
            scratch(3, 2, 8, 8, cz),
            scratch(3, 2, 4, 8, cz),
            scratch(3, 2, 8, cz),
            scratch(3, 2, 8, cz),
            scratch(3, 2, 8, 8, cz),
            scratch(3, 2, 4, 8, cz),
            scratch(3, 2, 2, 8, cz),
            scratch(3, 2, 2, 8, cz),
            scratch(3, 2, 2, 8, cz),
            scratch(3, 2, 2, 8, cz),
            scratch(2, planes, 24, 2 * cz),
            scratch(planes, 24, 2 * cz),
            scratch(planes, 24, 2 * cz),
            scratch(ITERS, cx, cy, cz),
            scratch(ITERS, 2, 8, cz),
            scratch(ITERS, 10, 8, cz),
            scratch(ITERS, 3, cy, cz),
            scratch(ITERS, 3, cy, cz),
            pltpu.VMEM((512, 128), BF16),
            pltpu.VMEM((128, 512), BF16),
            pltpu.VMEM((128, 256), BF16),
            cav, cav, cav, cav, cav, cav, cav, cav, cav, cav, cav,
            pltpu.VMEM((2, blocks), jnp.int32),
            pltpu.VMEM((1, blocks), jnp.int32),
            pltpu.VMEM((1, blocks), jnp.int32),
            pltpu.SemaphoreType.DMA((12,)),
            *[pltpu.SemaphoreType.DMA((ITERS, 4))] * 8,
            *[pltpu.SemaphoreType.DMA((ITERS, 3))] * 2,
            *[pltpu.SemaphoreType.DMA((ITERS,))] * 2,
            *[pltpu.SemaphoreType.DMA((2, 2, 7))] * 2,
        ],
        compiler_params=pltpu.CompilerParams(
            collective_id=0, has_side_effects=True, vmem_limit_bytes=56 * 1024 * 1024
        ),
    )(
        mold_temp, capacity, melt_temp, log_pressure, target_volume, inflow, transfer_coef,
        link_columns, wall_owner.reshape(1, blocks), wall_slot.reshape(1, blocks), self_blocks, link_blocks,
    )
    pressure = BULK_BASE * jnp.exp(-BULK_SLOPE * melt) * (jnp.exp(state) - 1.0)
    shrinkage = 1.0 - jnp.exp(EXPAND * melt) * (1.0 - TAIT_C * state)
    return field, pressure, shrinkage


def solution(mesh):
    cavity = P(None, ("wide", "mid", "narrow"))
    brick = P("wide", "mid", "narrow")
    flat = P(("wide", "mid", "narrow"))
    return jax.shard_map(
        per_device,
        mesh=mesh,
        in_specs=(
            brick, brick, cavity, cavity, cavity, cavity,
            P(None, None, ("wide", "mid", "narrow")),
            P(None, None, None, ("wide", "mid", "narrow")),
            cavity, flat, flat, cavity,
        ),
        out_specs=(brick, cavity, cavity),
        check_vma=False,
    )
```

```python
import functools

import jax
import jax.numpy as jnp
from jax import lax
from jax.experimental import pallas as pl
from jax.experimental.pallas import tpu as pltpu
from jax.sharding import PartitionSpec as P

BLOCK = 64
ITERS = 2
SWEEPS = 4
INNER = 2
WIDTH = 4
FAR_FIRST = (2, 1, 3)
TWO_HOPS_FIRST = (4, 5, 2, 3, 6, 7, 1)

CONDUCT = 1.0
COOLING = 0.5
TAIT_C = 0.3
EXPAND = 0.25
BULK_BASE = 0.5
BULK_SLOPE = 0.3

MESH = pl.DeviceIdType.MESH
F32 = jnp.float32
BF16 = jnp.bfloat16


def flip(v, k):
    if k == 0:
        return v
    if k == 1:
        return v + 1 - 2 * (v % 2)
    if k == 2:
        return (v + 2) % 4
    return 3 - v


def split_terms(x):
    hi = x.astype(BF16)
    lo = (x - hi.astype(F32)).astype(BF16)
    return hi, lo


def kernel(
    mold, cap, melt_in, logp, target_in, inflow_in, coef_in, columns_in, owner_in, slot_in, self_in, link_in,
    out_field, out_melt, out_state,
    selfb, linkb, wide_blocks, tab, spread, rs1, psum, rs2, near,
    row_own, row_ghost, lane_own, lane_ghost, rows_own, rows_ghost, lanes_own, lanes_ghost, corner_own, corner_ghost,
    ext, inv, base, plain, srcb, src_in, lower, lower_in,
    hot, hot_t, col_hot, diag, kv, resid, jdiag, slope, upd, state, melt, target, inflow, coef,
    columns, owner, slot,
    load_sem, zsend_sem, zrecv_sem, gsend_sem, grecv_sem, csend_sem, crecv_sem, ysend_sem, yrecv_sem,
    xsend_sem, xrecv_sem, lsend_sem, lrecv_sem, hsend_sem, hrecv_sem,
):
    cx, cy, cz = mold.shape
    planes = near.shape[1]
    w = lax.axis_index("wide")
    m = lax.axis_index("mid")
    n = lax.axis_index("narrow")
    n_w, n_m, n_n = lax.axis_size("wide"), lax.axis_size("mid"), lax.axis_size("narrow")
    zh, x, c = w // 8, (w // 2) % 4, w % 2

    def z_peer(k):
        return (flip(zh, k) * 8 + x * 2 + c, m, n)

    def xc_peer(j):
        return (zh * 8 + flip(x, j // 2) * 2 + flip(c, j % 2), m, n)

    def beside(dw, dm, dn):
        return ((w + n_w + dw) % n_w, (m + n_m + dm) % n_m, (n + n_n + dn) % n_n)

    for edge in (lanes_own, lanes_ghost, corner_own, corner_ghost):
        for a in range(3):
            edge[a] = jnp.zeros((2, 2, 8, cz), F32)
    barrier = pltpu.get_barrier_semaphore()
    peers = [z_peer(k) for k in range(1, 4)] + [xc_peer(j) for j in range(1, 8)]
    peers += [beside(-1, 0, 0), beside(1, 0, 0)]
    peers += [beside(0, dm, dn) for dm in (-1, 0, 1) for dn in (-1, 0, 1) if (dm, dn) != (0, 0)]
    for peer in peers:
        pl.semaphore_signal(barrier, inc=1, device_id=peer, device_id_type=MESH)

    loads = [
        pltpu.make_async_copy(src, dst, load_sem.at[i])
        for i, (src, dst) in enumerate((
            (owner_in, owner), (slot_in, slot), (coef_in, coef), (melt_in, melt),
            (mold, near.at[0, pl.ds(WIDTH, cx)]), (cap, near.at[1, pl.ds(WIDTH, cx)]), (columns_in, columns),
            (self_in, selfb), (link_in, linkb), (logp, state), (target_in, target), (inflow_in, inflow),
        ))
    ]
    for load in loads:
        load.start()

    def remote(src, dst, sems, peer):
        return pltpu.make_async_remote_copy(
            src_ref=src, dst_ref=dst, send_sem=sems[0], recv_sem=sems[1],
            device_id=peer, device_id_type=MESH,
        )

    def wait_recv(region, sems):
        remote(region, region, sems, beside(0, 1, 0)).wait_recv()

    def z_sems(it, k):
        return (zsend_sem.at[it, k], zrecv_sem.at[it, k])

    def gather_sems(it, k):
        return (gsend_sem.at[it, k], grecv_sem.at[it, k])

    def gather_on(it, k):
        for j in TWO_HOPS_FIRST:
            remote(tab.at[it, k, 0], tab.at[it, k, j], gather_sems(it, k), xc_peer(j)).start()

    def gather_start(it):
        for k in FAR_FIRST:
            remote(tab.at[it, 0, 0], tab.at[it, k, 0], z_sems(it, k), z_peer(k)).start()

    def z_arrived(it, k):
        wait_recv(tab.at[it, k, 0], z_sems(it, k))
        gather_on(it, k)

    def cool(it):
        found = jnp.zeros((128, 256), F32)
        for k in (0, 1, 3, 2):
            wait_recv(tab.at[it, k, pl.ds(1, 7)], gather_sems(it, k))
            hi, lo = split_terms(tab[it, k].reshape(128, 128))
            found = found + jnp.dot(
                hot_t[:, k * 128:(k + 1) * 128], jnp.concatenate([hi, lo], axis=1), preferred_element_type=F32
            )
        found = (found[:, :128] + found[:, 128:]).T
        wall = jnp.where(half == 1, found[BLOCK:], found[:BLOCK])
        melt[...] = melt[...] - COOLING * (coef[...] * (melt[...] - wall))

    def scatter_sems(a, k):
        return (csend_sem.at[a, k], crecv_sem.at[a, k])

    def sum_sems(a, k):
        return (ysend_sem.at[a, k], yrecv_sem.at[a, k])

    sums = (pl.ds(0, 2), pl.ds(0, 1))

    def scatter_terms(values):
        parts = []
        for value in values:
            placed = jnp.concatenate([jnp.where(half == 0, value, 0.0), jnp.where(half == 1, value, 0.0)], axis=0)
            parts.extend(split_terms(placed))
        return jnp.concatenate(parts, axis=0)

    def scatter_fill(a, terms):
        for k in range(4):
            summed = lax.dot_general(
                hot[k * 128:(k + 1) * 128, :], terms, (((1,), (1,)), ((), ())), preferred_element_type=F32
            )
            for q in range(2):
                one = summed[:, 256 * q:256 * q + 128] + summed[:, 256 * q + 128:256 * q + 256]
                spread[a, k, :, q] = one.reshape(8, 16, 128)

    def scatter_start(a, k):
        for j in TWO_HOPS_FIRST:
            remote(spread.at[a, k, j], rs1.at[a, k, j], scatter_sems(a, k), xc_peer(j)).start()

    def scatter_on(a, k):
        wait_recv(rs1.at[a, k, pl.ds(1, 7)], scatter_sems(a, k))
        totals = []
        for q in range(2):
            total = spread[a, k, 0, q]
            for j in range(1, 8):
                total = total + rs1[a, k, j, q]
            totals.append(total)
        if a == 0:
            psum[a, k, 0], psum[a, k, 1] = totals
        else:
            psum[a, k, 0] = COOLING * (totals[0] - totals[1] * tab[0, k, 0])
        if k > 0:
            remote(psum.at[a, k, sums[a]], rs2.at[a, k, sums[a]], sum_sems(a, k), z_peer(k)).start()

    def scatter_done(a):
        for k in (1, 3, 2):
            wait_recv(rs2.at[a, k, sums[a]], sum_sems(a, k))
        return [
            ((psum[a, 0, q] + rs2[a, 1, q]) + (rs2[a, 3, q] + rs2[a, 2, q])) for q in range(2 - a)
        ]

    lane = lax.broadcasted_iota(jnp.int32, (cy, cz), 1)
    lane24 = lax.broadcasted_iota(jnp.int32, (24, cz), 1)
    row8 = lax.broadcasted_iota(jnp.int32, (8, cz), 0)
    lane8 = lax.broadcasted_iota(jnp.int32, (8, cz), 1)
    own_planes = list(range(WIDTH, WIDTH + cx))
    ghost_planes = list(range(WIDTH)) + list(range(WIDTH + cx, planes))
    arrays = ((0, 1), (2,))

    def h_sems(g, step, kind):
        return (hsend_sem.at[g, step, kind], hrecv_sem.at[g, step, kind])

    def group(g):
        return pl.ds(arrays[g][0], len(arrays[g]))

    def send_low(g):
        remote(
            near.at[group(g), pl.ds(WIDTH, WIDTH)], near.at[group(g), pl.ds(WIDTH + cx, WIDTH)],
            h_sems(g, 0, 0), beside(-1, 0, 0),
        ).start()

    def send_high(g):
        src = near.at[group(0), pl.ds(cx, WIDTH)] if g == 0 else plain.at[pl.ds(0, 1), pl.ds(cx - WIDTH, WIDTH)]
        remote(src, near.at[group(g), pl.ds(0, WIDTH)], h_sems(g, 0, 1), beside(1, 0, 0)).start()

    def pack_edges(g, step):
        which, row_out, lane_out = ((own_planes, row_own, lane_own), (ghost_planes, row_ghost, lane_ghost))[step]
        for a in arrays[g]:
            packed = jnp.zeros((cy, cz), F32)
            for q, p in enumerate(which):
                packed = jnp.where(lane // 8 == q, pltpu.roll(near[a, p], WIDTH + 8 * q, 1), packed)
            lane_out[a, 0] = packed[:8]
            lane_out[a, 1] = packed[8:]
            for t in range(len(which) // 2):
                q = 4 * (t // 2) + t % 2
                one, two = near[a, which[q]], near[a, which[q + 2]]
                row_out[a, 0, t] = jnp.where(row8 < WIDTH, one[:8], pltpu.roll(two[:8], 4, 0))
                row_out[a, 1, t] = jnp.where(row8 < WIDTH, pltpu.roll(one[8:], 4, 0), two[8:])

    def send_edges(g, step):
        row_out, lane_out, rows_in, lanes_in, corner_in = (
            (row_own, lane_own, rows_own, lanes_own, corner_own),
            (row_ghost, lane_ghost, rows_ghost, lanes_ghost, corner_ghost),
        )[step]
        some = group(g)
        for side, dm in ((0, -1), (1, 1)):
            remote(row_out.at[some, side], rows_in.at[some, side], h_sems(g, step, 2), beside(0, dm, 0)).start()

        def send_lanes(side, dn):
            remote(lane_out.at[some], lanes_in.at[some, side], h_sems(g, step, 3 + 2 * side), beside(0, 0, dn)).start()
            for tile, dm in ((0, -1), (1, 1)):
                remote(
                    lane_out.at[some, tile], corner_in.at[some, side, tile], h_sems(g, step, 4 + 2 * side), beside(0, dm, dn)
                ).start()

        @pl.when(n > 0)
        def _():
            send_lanes(0, -1)

        @pl.when(n < n_n - 1)
        def _():
            send_lanes(1, 1)

    def take_edges(g, step, places):
        which, rows_in, lanes_in, corner_in = (
            (own_planes, rows_own, lanes_own, corner_own), (ghost_planes, rows_ghost, lanes_ghost, corner_ghost),
        )[step]
        some = group(g)
        wait_recv(rows_in.at[some], h_sems(g, step, 2))

        def wait_lanes(side):
            wait_recv(lanes_in.at[some, side], h_sems(g, step, 3 + 2 * side))
            wait_recv(corner_in.at[some, side], h_sems(g, step, 4 + 2 * side))

        @pl.when(n < n_n - 1)
        def _():
            wait_lanes(0)

        @pl.when(n > 0)
        def _():
            wait_lanes(1)

        for a, dst in zip(arrays[g], places):
            sides = []
            for side in range(2):
                corner = jnp.where(row8 < WIDTH, corner_in[a, side, 0], corner_in[a, side, 1])
                sides.append(jnp.concatenate([lanes_in[a, side, 0], lanes_in[a, side, 1], corner], axis=0))
            comb = jnp.where(lane24 % 8 >= WIDTH, sides[0], sides[1])
            for t in range(len(which) // 2):
                q = 4 * (t // 2) + t % 2
                after, before = rows_in[a, 0, t], rows_in[a, 1, t]
                ghosts = (
                    (q, jnp.where(row8 < WIDTH, after, pltpu.roll(before, 4, 0))),
                    (q + 2, jnp.where(row8 < WIDTH, pltpu.roll(after, 4, 0), before)),
                )
                for at, ghost in ghosts:
                    p = which[at]
                    dst[p, 0:cy, 0:cz] = near[a, p]
                    dst[p, cy:24, 0:cz] = ghost
                    dst[p, :, cz:2 * cz] = pltpu.roll(comb, cz - (8 * at + WIDTH), 1)

    def wide_arrived(g):
        wait_recv(near.at[group(g), pl.ds(WIDTH + cx, WIDTH)], h_sems(g, 0, 0))
        wait_recv(near.at[group(g), pl.ds(0, WIDTH)], h_sems(g, 0, 1))
        if g == 1:
            for p in range(3):
                near[2, p + 1] = near[2, p + 1] + lower[0, p]
        pack_edges(g, 1)
        send_edges(g, 1)

    def prepare(which):
        row_at = lax.broadcasted_iota(jnp.int32, (24, 2 * cz), 0)
        row_at = jnp.where(row_at < cy + WIDTH, row_at, row_at - 24) + m * cy
        lane_at = lax.broadcasted_iota(jnp.int32, (24, 2 * cz), 1)
        lane_real = (lane_at < cz + WIDTH) | (lane_at >= 2 * cz - WIDTH)
        lane_at = jnp.where(lane_at < cz + WIDTH, lane_at, lane_at - 2 * cz) + n * cz
        inside = lane_real & (row_at >= 0) & (row_at < n_m * cy) & (lane_at >= 0) & (lane_at < n_n * cz)
        inside = jnp.where(inside, 1.0, 0.0)
        for p in which:
            here = inside
            if p < WIDTH:
                here = jnp.where(w > 0, inside, 0.0)
            elif p >= WIDTH + cx:
                here = jnp.where(w < n_w - 1, inside, 0.0)
            capacity, start = inv[p], ext[0, p]
            base[p] = capacity * start
            inv[p] = here / (capacity + 6.0 * CONDUCT)
            ext[0, p] = jnp.where(here > 0.0, start, 0.0)

    def keep_inside(which):
        for p in which:
            ext[0, p] = jnp.where(inv[p] > 0.0, ext[0, p], 0.0)

    def around(plane):
        rows = pltpu.roll(plane, 1, 0) + pltpu.roll(plane, 23, 0)
        return rows + (pltpu.roll(plane, 1, 1) + pltpu.roll(plane, 2 * cz - 1, 1))

    def plain_sweeps(it, inner):
        for k in range(SWEEPS):
            now, later = k % 2, (k + 1) % 2
            edge = k + 1
            inside = range(edge + WIDTH, planes - edge - WIDTH)
            for p in inside if inner else [p for p in range(edge, planes - edge) if p not in inside]:
                total = (ext[now, p - 1] + ext[now, p + 1]) + around(ext[now, p]) + base[p]
                new = total * inv[p]
                if k == SWEEPS - 1:
                    plain[it, p - WIDTH] = new[:cy, :cz]
                else:
                    ext[later, p] = new

    def edge_sems(it, side):
        return (xsend_sem.at[it, side], xrecv_sem.at[it, side])

    def source_start(it, source):
        srcb[it, 0] = source[:8]
        srcb[it, 1] = source[8:]

        def send(side, parts):
            for src, place_at, count, dm, dn in parts:
                remote(
                    srcb.at[it, pl.ds(src, count)], src_in.at[it, pl.ds(place_at, count)],
                    edge_sems(it, side), beside(0, dm, dn),
                ).start()

        send(0, ((0, 0, 1, -1, 0), (1, 1, 1, 1, 0)))

        @pl.when(n > 0)
        def _():
            send(1, ((0, 2, 2, 0, -1), (0, 4, 1, -1, -1), (1, 5, 1, 1, -1)))

        @pl.when(n < n_n - 1)
        def _():
            send(2, ((0, 6, 2, 0, 1), (0, 8, 1, -1, 1), (1, 9, 1, 1, 1)))

    def source_done(it):
        wait_recv(src_in.at[it, pl.ds(0, 2)], edge_sems(it, 0))

        @pl.when(n < n_n - 1)
        def _():
            wait_recv(src_in.at[it, pl.ds(2, 4)], edge_sems(it, 1))

        @pl.when(n > 0)
        def _():
            wait_recv(src_in.at[it, pl.ds(6, 4)], edge_sems(it, 2))

        def corner(up, down):
            return jnp.where(row8 < WIDTH, src_in[it, up], src_in[it, down])

        def lanes(after, before):
            return jnp.where(lane8 < WIDTH, after, before)

        main = jnp.concatenate([srcb[it, 0], srcb[it, 1], corner(0, 1)], axis=0)
        sides = jnp.concatenate(
            [lanes(src_in[it, 2], src_in[it, 6]), lanes(src_in[it, 3], src_in[it, 7]), lanes(corner(4, 5), corner(8, 9))],
            axis=0,
        )
        return jnp.concatenate([main, sides], axis=1)

    def grown(wide_source, have, p):
        total = jnp.zeros((24, 2 * cz), F32)
        if p == 0:
            total = wide_source
        for q in (p - 1, p + 1):
            if q in have:
                total = total + have[q]
        if p in have:
            total = total + around(have[p])
        return total * inv[WIDTH + p]

    def first_sweeps(wide_source):
        one = {0: wide_source * inv[WIDTH]}
        two = {p: grown(wide_source, one, p) for p in (0, -1, 1)}
        three = {p: grown(wide_source, two, p) for p in (0, -1, 1)}
        wall = grown(wide_source, three, 0)[:cy, :cz]
        return two, three, wall

    def last_sweeps(it, wide_source, two, three):
        three.update({p: grown(wide_source, two, p) for p in (-2, 2)})
        for p in (-3, -2, -1):
            lower[it, p + 3] = grown(wide_source, three, p)[:cy, :cz]
        remote(lower.at[it], lower_in.at[it], (lsend_sem.at[it], lrecv_sem.at[it]), beside(-1, 0, 0)).start()
        return [grown(wide_source, three, p)[:cy, :cz] for p in (1, 2, 3)]

    def lower_arrived(it):
        wait_recv(lower_in.at[it], (lsend_sem.at[it], lrecv_sem.at[it]))

    def apply(v16):
        v = v16.astype(F32)
        linked = jnp.dot(v16, col_hot[...], preferred_element_type=F32)
        near0, near1 = linked[:, :128], linked[:, 128:]

        def rows(t, carry):
            sums = []
            for u in range(8):
                i = t * 8 + u
                prod = wide_blocks[0, i] * v + wide_blocks[1, i] * near0 + wide_blocks[2, i] * near1
                sums.append(jnp.sum(prod, axis=0, keepdims=True))
            kv[pl.ds(pl.multiple_of(t * 8, 8), 8), :] = jnp.concatenate(sums, axis=0)
            return carry

        lax.fori_loop(0, BLOCK // 8, rows, 0)
        return kv[...]

    def newton_start():
        mt, st = melt[...], state[...]
        bulk = BULK_BASE * jnp.exp(-BULK_SLOPE * mt)
        growth = jnp.exp(st)
        press = bulk * (growth - 1.0)
        base_volume = jnp.exp(EXPAND * mt)
        volume = base_volume * (1.0 - TAIT_C * st)
        sl = bulk * growth
        slope[...] = sl
        jd = diag[...] * sl + TAIT_C * base_volume
        jdiag[...] = jd
        rounded = press.astype(BF16)
        res = apply(rounded) + diag[...] * rounded.astype(F32) + (target[...] - volume) - inflow[...]
        resid[...] = res
        upd[...] = -res / jd

    def newton_step():
        weighted = (slope[...] * upd[...]).astype(BF16)
        upd[...] = (-resid[...] - apply(weighted)) / jdiag[...]

    def sends_left(it):
        def wait_send(region, sems):
            remote(region, region, sems, beside(0, 1, 0)).wait_send()

        for k in range(4):
            if k > 0:
                wait_send(tab.at[it, k, 0], z_sems(it, k))
                wait_send(psum.at[it, k, sums[it]], sum_sems(it, k))
            wait_send(tab.at[it, k, pl.ds(1, 7)], gather_sems(it, k))
            wait_send(spread.at[it, k, pl.ds(1, 7)], scatter_sems(it, k))
        wait_send(src_in.at[it, pl.ds(0, 2)], edge_sems(it, 0))

        @pl.when(n > 0)
        def _():
            wait_send(src_in.at[it, pl.ds(2, 4)], edge_sems(it, 1))

        @pl.when(n < n_n - 1)
        def _():
            wait_send(src_in.at[it, pl.ds(6, 4)], edge_sems(it, 2))

        wait_send(lower.at[it], (lsend_sem.at[it], lrecv_sem.at[it]))
        some = group(it)
        wait_send(near.at[some, pl.ds(0, WIDTH)], h_sems(it, 0, 0))
        wait_send(near.at[some, pl.ds(0, WIDTH)], h_sems(it, 0, 1))
        for step, regions in ((0, (rows_own, lanes_own, corner_own)), (1, (rows_ghost, lanes_ghost, corner_ghost))):
            rows, lanes, corner = regions
            wait_send(rows.at[some], h_sems(it, step, 2))
            for side, sent in ((0, n > 0), (1, n < n_n - 1)):

                @pl.when(sent)
                def _(step=step, lanes=lanes, corner=corner, side=side):
                    wait_send(lanes.at[some, side], h_sems(it, step, 3 + 2 * side))
                    wait_send(corner.at[some, side], h_sems(it, step, 4 + 2 * side))

    for load in loads[:4]:
        load.wait()
    rel = jnp.bitwise_xor(owner[...], w)
    place = rel * 16 + slot[...] // 2
    half = slot[...] % 2
    faces = lax.broadcasted_iota(jnp.int32, (512, 128), 0)
    hot32 = jnp.where(faces == place, 1.0, 0.0)
    hot[...] = hot32.astype(BF16)
    scatter_fill(0, scatter_terms((coef[...] * melt[...], coef[...])))
    for it in range(ITERS):
        src_in[it] = jnp.zeros((10, 8, cz), F32)
    loads[4].wait()
    loads[5].wait()
    tab[0, 0, 0] = near[0, WIDTH]
    pack_edges(0, 0)
    pl.semaphore_wait(barrier, len(peers))

    for k in FAR_FIRST:
        scatter_start(0, k)
    send_low(0)
    send_high(0)
    gather_start(0)
    send_edges(0, 0)
    scatter_start(0, 0)
    square = coef[...] * coef[...]
    scatter_fill(1, scatter_terms((square * melt[...], square)))
    for k in FAR_FIRST + (0,):
        scatter_start(1, k)
    hot_t[...] = hot32.T.astype(BF16)
    for load in loads[6:]:
        load.wait()
    froms = lax.broadcasted_iota(jnp.int32, (128, 128), 0)
    for k in range(2):
        col_hot[:, k * 128:(k + 1) * 128] = jnp.where(froms == columns[k:k + 1, :], 1.0, 0.0).astype(BF16)

    def pick(t, carry):
        sums = []
        for u in range(8):
            i = t * 8 + u
            mask = lax.broadcasted_iota(jnp.int32, (BLOCK, 128), 0) == i
            block = selfb[i].astype(F32)
            sums.append(jnp.sum(jnp.where(mask, block, 0.0), axis=0, keepdims=True))
            wide_blocks[0, i] = jnp.where(mask, 0.0, block)
            wide_blocks[1, i] = linkb[0, i].astype(F32)
            wide_blocks[2, i] = linkb[1, i].astype(F32)
        diag[pl.ds(pl.multiple_of(t * 8, 8), 8), :] = jnp.concatenate(sums, axis=0)
        return carry

    lax.fori_loop(0, BLOCK // 8, pick, 0)
    for k in FAR_FIRST:
        scatter_on(0, k)
    gather_on(0, 0)
    z_arrived(0, 1)
    z_arrived(0, 3)
    wide_arrived(0)
    take_edges(0, 0, (ext.at[0], inv))
    prepare(own_planes)
    scatter_on(0, 0)
    plain_sweeps(0, True)

    sum_a, sum_b = scatter_done(0)
    first_wall = near[0, WIDTH]
    source_start(0, sum_a - sum_b * first_wall)
    z_arrived(0, 2)
    take_edges(0, 1, (ext.at[0], inv))
    prepare(ghost_planes)
    plain_sweeps(0, False)
    send_high(1)
    for k in FAR_FIRST + (0,):
        scatter_on(1, k)
    spread_source = source_done(0)
    two, three, wall_part = first_sweeps(spread_source)
    second_wall = plain[0, 0] + wall_part
    tab[1, 0, 0] = second_wall
    gather_start(1)
    gather_on(1, 0)
    upper = last_sweeps(0, spread_source, two, three)
    near[2, WIDTH] = second_wall
    for p in range(1, 4):
        near[2, WIDTH + p] = plain[0, p] + upper[p - 1]
    send_low(1)
    for p in range(4, cx - 3):
        near[2, WIDTH + p] = plain[0, p]

    cool(0)
    newton_start()
    z_arrived(1, 1)
    z_arrived(1, 3)
    newton_step()
    (cooled,) = scatter_done(1)
    source_start(1, (sum_a - cooled) - sum_b * second_wall)
    lower_arrived(0)
    for p in range(3):
        near[2, WIDTH + cx - 3 + p] = plain[0, cx - 3 + p] + lower_in[0, p]
    pack_edges(1, 0)
    send_edges(1, 0)
    z_arrived(1, 2)
    wide_arrived(1)
    newton_step()
    state[...] = state[...] + upd[...]
    spread_source = source_done(1)
    two, three, wall_part = first_sweeps(spread_source)
    upper = last_sweeps(1, spread_source, two, three)
    take_edges(1, 0, (ext.at[0],))
    keep_inside(own_planes)
    plain_sweeps(1, True)
    sends_left(0)

    cool(1)
    newton_start()
    newton_step()
    newton_step()
    out_melt[...] = melt[...]
    out_state[...] = state[...] + upd[...]
    sends_left(1)
    take_edges(1, 1, (ext.at[0],))
    keep_inside(ghost_planes)
    plain_sweeps(1, False)
    out_field[0] = plain[1, 0] + wall_part
    for p in range(1, 4):
        out_field[p] = plain[1, p] + upper[p - 1]
    for p in range(4, cx - 3):
        out_field[p] = plain[1, p]
    lower_arrived(1)
    for p in range(3):
        out_field[cx - 3 + p] = plain[1, cx - 3 + p] + lower_in[1, p]


def per_device(
    mold_temp, capacity, melt_temp, log_pressure, target_volume, inflow, self_blocks, link_blocks,
    link_columns, wall_owner, wall_slot, transfer_coef,
):
    cx, cy, cz = mold_temp.shape
    cells, blocks = melt_temp.shape
    planes = cx + 2 * WIDTH
    vmem = pl.BlockSpec(memory_space=pltpu.VMEM)
    hbm = pl.BlockSpec(memory_space=pltpu.HBM)

    def scratch(*shape):
        return pltpu.VMEM(shape, F32)

    cav = scratch(cells, blocks)
    field, melt, state = pl.pallas_call(
        kernel,
        out_shape=(
            pltpu.VMEM(mold_temp.shape, F32),
            pltpu.VMEM(melt_temp.shape, F32),
            pltpu.VMEM(melt_temp.shape, F32),
        ),
        in_specs=[hbm] * 12,
        out_specs=(vmem, vmem, vmem),
        scratch_shapes=[
            pltpu.VMEM(self_blocks.shape, BF16),
            pltpu.VMEM(link_blocks.shape, BF16),
            scratch(3, *self_blocks.shape),
            scratch(ITERS, 4, 8, 16, 128),
            scratch(2, 4, 8, 2, 16, 128),
            scratch(2, 4, 8, 2, 16, 128),
            scratch(2, 4, 2, 16, 128),
            scratch(2, 4, 2, 16, 128),
            scratch(3, planes, cy, cz),
            scratch(3, 2, 8, 8, cz),
            scratch(3, 2, 4, 8, cz),
            scratch(3, 2, 8, cz),
            scratch(3, 2, 8, cz),
            scratch(3, 2, 8, 8, cz),
            scratch(3, 2, 4, 8, cz),
            scratch(3, 2, 2, 8, cz),
            scratch(3, 2, 2, 8, cz),
            scratch(3, 2, 2, 8, cz),
            scratch(3, 2, 2, 8, cz),
            scratch(2, planes, 24, 2 * cz),
            scratch(planes, 24, 2 * cz),
            scratch(planes, 24, 2 * cz),
            scratch(ITERS, cx, cy, cz),
            scratch(ITERS, 2, 8, cz),
            scratch(ITERS, 10, 8, cz),
            scratch(ITERS, 3, cy, cz),
            scratch(ITERS, 3, cy, cz),
            pltpu.VMEM((512, 128), BF16),
            pltpu.VMEM((128, 512), BF16),
            pltpu.VMEM((128, 256), BF16),
            cav, cav, cav, cav, cav, cav, cav, cav, cav, cav, cav,
            pltpu.VMEM((2, blocks), jnp.int32),
            pltpu.VMEM((1, blocks), jnp.int32),
            pltpu.VMEM((1, blocks), jnp.int32),
            pltpu.SemaphoreType.DMA((12,)),
            *[pltpu.SemaphoreType.DMA((ITERS, 4))] * 8,
            *[pltpu.SemaphoreType.DMA((ITERS, 3))] * 2,
            *[pltpu.SemaphoreType.DMA((ITERS,))] * 2,
            *[pltpu.SemaphoreType.DMA((2, 2, 7))] * 2,
        ],
        compiler_params=pltpu.CompilerParams(
            collective_id=0, has_side_effects=True, vmem_limit_bytes=56 * 1024 * 1024
        ),
    )(
        mold_temp, capacity, melt_temp, log_pressure, target_volume, inflow, transfer_coef,
        link_columns, wall_owner.reshape(1, blocks), wall_slot.reshape(1, blocks), self_blocks, link_blocks,
    )
    pressure = BULK_BASE * jnp.exp(-BULK_SLOPE * melt) * (jnp.exp(state) - 1.0)
    shrinkage = 1.0 - jnp.exp(EXPAND * melt) * (1.0 - TAIT_C * state)
    return field, pressure, shrinkage


def solution(mesh):
    cavity = P(None, ("wide", "mid", "narrow"))
    brick = P("wide", "mid", "narrow")
    flat = P(("wide", "mid", "narrow"))
    return jax.shard_map(
        per_device,
        mesh=mesh,
        in_specs=(
            brick, brick, cavity, cavity, cavity, cavity,
            P(None, None, ("wide", "mid", "narrow")),
            P(None, None, None, ("wide", "mid", "narrow")),
            cavity, flat, flat, cavity,
        ),
        out_specs=(brick, cavity, cavity),
        check_vma=False,
    )
```
